128 devices in a mesh: ctx: 8 (over z, core), fsdp: 16 (over y, x).
Axes of the slice: x: 4, y: 4, z: 4, core: 2. Of those that a mesh axis runs over, the one named last changes fastest.
Arguments:
- tokens: bfloat16 [16, 2, 1024, 1024], P('fsdp', None, 'ctx'), may hold values from -6 to 6
- routes: int32 [16, 2, 1024, 8], P('fsdp', None, 'ctx'), may hold values from 0 to 31, all different within a row; in each aligned block of 128 rows (0 to 127, 128 to 255, ..., all dimensions but the last counted through in order) at most 40 rows name the same one
- doc_starts: int32 [16, 2, 1024], P('fsdp', None, 'ctx'), may hold values from 0 to 2047, as said below
- attn_gain: bfloat16 [1024], P('fsdp'), may hold values from 0.099609375 to 1.8984375
- attn_q: bfloat16 [1024, 1024], P('fsdp'), may hold values from -0.1875 to 0.1875
- attn_k: bfloat16 [1024, 512], P('fsdp'), may hold values from -0.1875 to 0.1875
- attn_v: bfloat16 [1024, 512], P('fsdp'), may hold values from -0.1875 to 0.1875
- attn_out: bfloat16 [1024, 1024], P('fsdp'), may hold values from -0.75 to 0.75
- ffn_gain: bfloat16 [1024], P('fsdp'), may hold values from 0.099609375 to 1.8984375
- router: bfloat16 [1024, 32], P('fsdp'), may hold values from -0.09375 to 0.09375
- w_gate: bfloat16 [32, 1024, 512], P('ctx', 'fsdp'), may hold values from -0.1875 to 0.1875
- w_up: bfloat16 [32, 1024, 512], P('ctx', 'fsdp'), may hold values from -0.1875 to 0.1875
- w_down: bfloat16 [32, 512, 1024], P('ctx', 'fsdp'), may hold values from -1 to 1
- cotangent: bfloat16 [16, 2, 1024, 1024], P('fsdp', None, 'ctx'), may hold values from -6 to 6
Outputs:
- mixed: bfloat16 [16, 2, 1024, 1024], P('fsdp', None, 'ctx')
- d_tokens: float32 [16, 2, 1024, 1024], P('fsdp', None, 'ctx')
- d_attn_gain: float32 [1024], P('fsdp')
- d_attn_q: float32 [1024, 1024], P('fsdp')
- d_attn_k: float32 [1024, 512], P('fsdp')
- d_attn_v: float32 [1024, 512], P('fsdp')
- d_attn_out: float32 [1024, 1024], P('fsdp')
- d_ffn_gain: float32 [1024], P('fsdp')
- d_router: float32 [1024, 32], P('fsdp')
- d_w_gate: float32 [32, 1024, 512], P('ctx', 'fsdp')
- d_w_up: float32 [32, 1024, 512], P('ctx', 'fsdp')
- d_w_down: float32 [32, 512, 1024], P('ctx', 'fsdp')
The draws below stay inside these ranges and needn't reach their ends.
Inputs may be any that keep to these rules, and one draw needn't show every extreme that they name: `routes`: each row names 8 different experts; in the 128 rows of one device in one micro-batch no expert is named more than 40 times, a bound that some block reaches in some of them. doc_starts at position p is 0 for p = 0 and otherwise p or its value at p - 1; in every stream one document covers a whole micro-batch.
All inputs are finite; a program needn't handle non-finite values.
Results may differ from the reference program's by a relative error of at most 0.025.
Values may be sent and summed in bfloat16 or wider, within the bound.
No kernel may reach another device: no remote copies, remote signals or barrier semaphores. Data moves between devices by JAX's collectives and lax.ppermute only.
A program may use at most 256 MiB of HBM per device.

```python
import math
import jax
import jax.numpy as jnp
import numpy as np
from jax import lax

D = 1024
HEADS = 16
KV_HEADS = 8
HEAD_DIM = 64
FF = 512
TOP = 8
MICRO = 2
TOK_DEV = 128
MB_LEN = 1024
STREAM = 2048
STREAMS = 16
EXPERTS = 32
CAP = 40
N_CTX = 8


def draw_doc_starts(key, part):
    key = jax.random.fold_in(key, 11)
    mark_key, batch_key = jax.random.split(key)
    position = jnp.arange(STREAM, dtype=jnp.int32)[None, :]
    boundary = jax.random.randint(mark_key, (STREAMS, STREAM), 0, max(MB_LEN // 2, 2)) == 0
    whole_batch = jax.random.randint(batch_key, (STREAMS, 1), 0, MICRO)
    inside_mask = (position // MB_LEN == whole_batch) & (position % MB_LEN != 0)
    boundary = boundary & jnp.logical_not(inside_mask) | (position == 0)
    starts = lax.cummax(jnp.where(boundary, position, 0), axis=1)
    return starts.reshape(STREAMS, MICRO, MB_LEN).astype(jnp.int32)


def shard_levels(key, extent, pieces, least, top_value):
    def one(dim, parts):
        draws = jax.random.uniform(jax.random.fold_in(jax.random.fold_in(key, 6), dim), (parts,), jnp.float32, least / len(pieces), top_value / len(pieces))
        return jnp.repeat(jnp.exp(draws), extent[dim] // parts).reshape((-1,) + (1,) * (len(extent) - dim - 1))

    loudness = one(*pieces[0])
    for cut in pieces[1:]:
        loudness = loudness * one(*cut)
    return loudness


def assign_block(key, own, number, rows, amount, top, bound, skew):
    order = jax.random.permutation(key, amount)
    crowded, ordinary = portions_of(amount, rows * top, bound, skew, True), portions_of(amount, rows * top, bound, skew, False)
    places = jnp.arange(amount)

    def named(tallies, rotation):
        used = int((tallies > 0).sum())
        fixed = max(1, used // 4)
        passed = fixed + (places - fixed + rotation * (used - fixed)) % max(1, amount - fixed)
        return jnp.zeros((amount,), jnp.int32).at[order[jnp.where(places < fixed, places, passed)]].set(jnp.asarray(tallies, jnp.int32))

    tallies = jnp.where(number % 4 == 0, named(crowded, number // 4), named(ordinary, number - number // 4 - 1))
    mixed = jax.random.permutation(jax.random.fold_in(own, 3), amount)
    source_of, receiver = mixed[0:amount // 2 * 2:2], mixed[1:amount // 2 * 2:2]
    room = jnp.minimum(tallies[source_of] - 1, bound - tallies[receiver]) // 2
    room = jnp.where((source_of == order[0]) | (receiver == order[0]) | (tallies[receiver] == 0), 0, jnp.maximum(room, 0))
    passed = jax.random.randint(jax.random.fold_in(own, 4), (amount // 2,), 0, 1 << 20) % (room + 1)
    tallies = tallies.at[source_of].add(-passed).at[receiver].add(passed)
    items = jnp.searchsorted(jnp.cumsum(tallies), jnp.arange(rows * top), side="right").astype(jnp.int32)
    grid = items.reshape(top, rows).T
    grid = grid[jax.random.permutation(jax.random.fold_in(own, 1), rows)]
    rotation = jax.random.randint(jax.random.fold_in(own, 2), (rows, 1), 0, top)
    return jnp.take_along_axis(grid, (jnp.arange(top)[None, :] + rotation) % top, axis=1)


def portions_of(amount, total, reach, slope, full):
    portions = [(1 << 20) // math.isqrt(rank ** slope) + 1 for rank in range(1, amount + 1)]
    largest = reach if full else min(reach, max(-(-total // amount), total * portions[0] // sum(portions)))
    least = 1 if total - largest >= amount - 1 else 0
    holding, rest = [largest] + [least] * (amount - 1), total - largest - least * (amount - 1)
    while rest > 0:
        movable = [i for i in range(1, amount) if holding[i] < largest] or [i for i in range(1, amount) if holding[i] < reach]
        mass, remaining = sum([portions[i] for i in movable]), rest
        for i in movable:
            more = min(reach - holding[i], max(1, remaining * portions[i] // mass), rest)
            holding[i] = holding[i] + more
            rest = rest - more
    return np.array(holding)


def bell_draw(own_key, extent, width, reach, cuts=(), kind=jnp.bfloat16):
    level = shard_levels(own_key, extent, cuts, -0.22, 0.18) if cuts else 1.0
    result = jax.random.normal(own_key, extent, jnp.float32) * width * level
    return jnp.minimum(jnp.maximum(result, -reach), reach).astype(kind)


def setup_inputs(seed: int = 0) -> dict:
    arg_keys = jax.random.split(jax.random.key(seed), 15)
    tokens = bell_draw(arg_keys[0], (STREAMS, MICRO, MB_LEN, D), 1.0, 6.0, ((0, 16), (2, 8)))
    routes_keys = jax.random.split(jax.random.fold_in(arg_keys[1], 1), STREAMS * MICRO * MB_LEN // TOK_DEV)
    routes_turns = jax.random.permutation(jax.random.fold_in(arg_keys[1], 3), STREAMS * MICRO * MB_LEN // TOK_DEV)
    routes = jax.vmap(lambda own, number: assign_block(jax.random.fold_in(arg_keys[1], 2), own, number, TOK_DEV, EXPERTS, TOP, CAP, 1))(routes_keys, routes_turns).reshape((STREAMS, MICRO, MB_LEN, TOP))
    doc_starts = draw_doc_starts(jax.random.fold_in(arg_keys[14], 71), 0)
    attn_gain = jnp.clip(1.0 + 0.18 * jax.random.normal(arg_keys[3], (D,), jnp.float32), 0.099609375, 1.8984375).astype(jnp.bfloat16)
    attn_q = bell_draw(arg_keys[4], (D, HEADS * HEAD_DIM), D ** -0.5, 0.1875, ((0, 16),))
    attn_k = bell_draw(arg_keys[5], (D, KV_HEADS * HEAD_DIM), D ** -0.5, 0.1875, ((0, 16),))
    attn_v = bell_draw(arg_keys[6], (D, KV_HEADS * HEAD_DIM), D ** -0.5, 0.1875, ((0, 16),))
    attn_out = bell_draw(arg_keys[7], (HEADS * HEAD_DIM, D), (HEADS * HEAD_DIM // 16) ** -0.5, 0.75, ((0, 16),))
    ffn_gain = jnp.clip(1.0 + 0.18 * jax.random.normal(arg_keys[8], (D,), jnp.float32), 0.099609375, 1.8984375).astype(jnp.bfloat16)
    router = bell_draw(arg_keys[9], (D, EXPERTS), (4 * D) ** -0.5, 0.09375, ((0, 16),))
    w_gate = bell_draw(arg_keys[10], (EXPERTS, D, FF), D ** -0.5, 0.1875, ((0, 8), (1, 16)))
    w_up = bell_draw(arg_keys[11], (EXPERTS, D, FF), D ** -0.5, 0.1875, ((0, 8), (1, 16)))
    w_down = bell_draw(arg_keys[12], (EXPERTS, FF, D), (FF // 16) ** -0.5, 1.0, ((0, 8), (1, 16)))
    cotangent = bell_draw(arg_keys[13], (STREAMS, MICRO, MB_LEN, D), 1.0, 6.0, ((0, 16), (2, 8)))
    return dict(tokens=tokens, routes=routes, doc_starts=doc_starts, attn_gain=attn_gain, attn_q=attn_q, attn_k=attn_k, attn_v=attn_v, attn_out=attn_out, ffn_gain=ffn_gain, router=router, w_gate=w_gate, w_up=w_up, w_down=w_down, cotangent=cotangent)


@jax.custom_vjp
def low(v):
    return lax.optimization_barrier(v.astype(jnp.bfloat16)).astype(jnp.float32)

@jax.custom_vjp
def low_back(v):
    return v

def low_keep(v):
    return (low(v), None)

def low_pass(kept, grad):
    return (grad,)

def back_keep(v):
    return (v, None)

def back_low(kept, grad):
    return (low(grad),)
low.defvjp(low_keep, low_pass)
low_back.defvjp(back_keep, back_low)
HIGHEST = lax.Precision.HIGHEST

def normalize(values):
    return values * lax.rsqrt(lax.optimization_barrier(jnp.mean(values * values, -1, keepdims=True)) + 1e-06)

def angles(positions):
    half_width = HEAD_DIM // 2
    frequencies = 10000.0 ** (-2.0 * jnp.arange(half_width, dtype=jnp.float32) / HEAD_DIM)
    turned = positions.astype(jnp.float32)[:, None] * frequencies[None, :]
    return (jnp.cos(turned)[:, None, :], jnp.sin(turned)[:, None, :])

def rotate(values, cosine_rows, sine_rows):
    half_width = values.shape[-1] // 2
    front_half = values[..., :half_width]
    back_half = values[..., half_width:]
    return jnp.concatenate([front_half * cosine_rows - back_half * sine_rows, back_half * cosine_rows + front_half * sine_rows], -1)

def softmax_rows(scores):
    biggest = lax.optimization_barrier(jnp.max(scores, -1, keepdims=True))
    raised = jnp.exp(scores - biggest)
    return raised / lax.optimization_barrier(jnp.sum(raised, -1, keepdims=True))

def stream_layer(stream_in, stream_routes, stream_starts, weights):
    gain_one, weight_q, weight_k, weight_v, weight_o, gain_two, weight_r, weight_g, weight_u, weight_d = weights
    positions = jnp.arange(STREAM, dtype=jnp.int32)
    cosine_rows, sine_rows = angles(positions)
    hidden_in = low(normalize(stream_in) * gain_one)
    query_lin = low_back(jnp.dot(hidden_in, weight_q, precision=HIGHEST))
    key_lin = low_back(jnp.dot(hidden_in, weight_k, precision=HIGHEST))
    values = low(low_back(jnp.dot(hidden_in, weight_v, precision=HIGHEST))).reshape(STREAM, KV_HEADS, HEAD_DIM)
    queries = low(rotate(query_lin.reshape(STREAM, HEADS, HEAD_DIM), cosine_rows, sine_rows))
    queries = queries.reshape(STREAM, KV_HEADS, HEADS // KV_HEADS, HEAD_DIM)
    keys = low(rotate(key_lin.reshape(STREAM, KV_HEADS, HEAD_DIM), cosine_rows, sine_rows))
    block_rows = math.gcd(STREAM, 512)

    def attend(block_index):
        first_row = block_index * block_rows
        query_block = lax.dynamic_slice_in_dim(queries, first_row, block_rows, 0)
        query_pos = first_row + jnp.arange(block_rows, dtype=jnp.int32)
        query_start = lax.dynamic_slice_in_dim(stream_starts, first_row, block_rows, 0)
        scores = low_back(jnp.einsum('qgcd,jgd->gcqj', query_block, keys, precision=HIGHEST) * (1.0 / math.sqrt(HEAD_DIM)))
        visible = (positions[None, :] >= query_start[:, None]) & (positions[None, :] <= query_pos[:, None])
        scores = jnp.where(visible[None, None], scores, -jnp.inf)
        weights_low = low(softmax_rows(scores))
        return jnp.einsum('gcqj,jgd->qgcd', weights_low, values, precision=HIGHEST)
    attended = lax.map(jax.checkpoint(attend), jnp.arange(STREAM // block_rows, dtype=jnp.int32))
    attended = low_back(low(attended.reshape(STREAM, HEADS * HEAD_DIM)))
    residual = stream_in + low_back(jnp.dot(attended, weight_o, precision=HIGHEST))
    hidden_two = low(normalize(residual) * gain_two)
    logits = jnp.dot(hidden_two, weight_r, precision=HIGHEST)
    gate_rows = softmax_rows(jnp.take_along_axis(logits, stream_routes, axis=1))
    flat_routes = stream_routes.reshape(-1)
    flat_gates = gate_rows.reshape(-1)
    slot_bound = MICRO * N_CTX * CAP

    def expert(mixture, expert_item):
        expert_id, gate_weight, up_weight, down_weight = expert_item
        hit_mask = (flat_routes == expert_id).astype(jnp.int32)
        slot_places = jnp.where(hit_mask > 0, jnp.cumsum(hit_mask).astype(jnp.int32) - 1, slot_bound)
        route_ids = jnp.zeros((slot_bound,), jnp.int32).at[slot_places].set(jnp.arange(STREAM * TOP, dtype=jnp.int32), mode='drop')
        live_mask = (jnp.arange(slot_bound, dtype=jnp.int32) < jnp.sum(hit_mask).astype(jnp.int32)).astype(jnp.float32)
        token_ids = route_ids // TOP
        taken_rows = low_back(hidden_two[token_ids])
        gate_lin = low_back(jnp.dot(taken_rows, gate_weight, precision=HIGHEST))
        up_lin = low_back(jnp.dot(taken_rows, up_weight, precision=HIGHEST))
        inner_act = low(gate_lin * jax.nn.sigmoid(gate_lin) * up_lin)
        expert_out = low_back(low(jnp.dot(inner_act, down_weight, precision=HIGHEST)))
        scaled = (flat_gates[route_ids] * live_mask)[:, None] * expert_out
        return (mixture.at[token_ids].add(scaled), None)
    mixture, unused = lax.scan(jax.checkpoint(expert), jnp.zeros((STREAM, D), jnp.float32), (jnp.arange(EXPERTS, dtype=jnp.int32), weight_g, weight_u, weight_d))
    return residual + mixture

def reference(tokens, routes, doc_starts, attn_gain, attn_q, attn_k, attn_v, attn_out, ffn_gain, router, w_gate, w_up, w_down, cotangent):
    streams_in = tokens.astype(jnp.float32).reshape(STREAMS, STREAM, D)
    route_rows = routes.reshape(STREAMS, STREAM, TOP)
    start_rows = doc_starts.reshape(STREAMS, STREAM)
    weights = (attn_gain.astype(jnp.float32), attn_q.astype(jnp.float32), attn_k.astype(jnp.float32), attn_v.astype(jnp.float32), attn_out.astype(jnp.float32), ffn_gain.astype(jnp.float32), router.astype(jnp.float32), w_gate.astype(jnp.float32), w_up.astype(jnp.float32), w_down.astype(jnp.float32))

    def whole_layer(stream_values, weight_set):

        def single(stream_item):
            return stream_layer(stream_item[0], stream_item[1], stream_item[2], weight_set)
        return lax.map(jax.checkpoint(single), (stream_values, route_rows, start_rows))
    outputs, pullback = jax.vjp(whole_layer, streams_in, weights)
    grad_in, grad_weights = pullback(cotangent.astype(jnp.float32).reshape(STREAMS, STREAM, D))
    out_shape = (STREAMS, MICRO, MB_LEN, D)
    return (outputs.astype(jnp.bfloat16).reshape(out_shape), grad_in.reshape(out_shape), grad_weights[0], grad_weights[1], grad_weights[2], grad_weights[3], grad_weights[4], grad_weights[5], grad_weights[6], grad_weights[7], grad_weights[8], grad_weights[9])
```

```python
import functools
import math

import jax
import jax.numpy as jnp
from jax import lax
from jax.experimental import pallas as pl
from jax.experimental.pallas import tpu as pltpu
from jax.sharding import PartitionSpec as P

HEADS = 16
KV_HEADS = 8
HEAD_DIM = 64
MICRO = 2
EPSILON = 1e-06
HIDDEN = -1e30
BF = jnp.bfloat16
F32 = jnp.float32
HIGHEST = lax.Precision.HIGHEST
PAIR = 2 * HEAD_DIM
VMEM_LIMIT = 56 * 1024 * 1024

NN = (((1,), (0,)), ((), ()))
NT = (((1,), (1,)), ((), ()))
TN = (((0,), (0,)), ((), ()))


def mm(left, right, dims=NN, precision=None):
    return lax.dot_general(left, right, dims, preferred_element_type=F32, precision=precision)


def params():
    return pltpu.CompilerParams(vmem_limit_bytes=VMEM_LIMIT)


def cost(flops, moved):
    return pl.CostEstimate(flops=int(flops), bytes_accessed=int(moved), transcendentals=0)


def lanes(shape):
    return lax.broadcasted_iota(jnp.int32, shape, len(shape) - 1)


def turn(values, cosine, sine):
    spot = lanes(values.shape) % HEAD_DIM
    swapped = jnp.where(
        spot < HEAD_DIM // 2,
        pltpu.roll(values, PAIR - HEAD_DIM // 2, 1),
        pltpu.roll(values, HEAD_DIM // 2, 1),
    )
    return values * cosine + swapped * sine


def angle_tables(length):
    half = HEAD_DIM // 2
    frequencies = 10000.0 ** (-2.0 * jnp.arange(half, dtype=F32) / HEAD_DIM)
    turned = jnp.arange(length, dtype=jnp.int32).astype(F32)[:, None] * frequencies[None, :]
    cosine, sine = jnp.cos(turned), jnp.sin(turned)
    return (
        jnp.concatenate([cosine] * 4, -1),
        jnp.concatenate([-sine, sine, -sine, sine], -1),
    )


def project_kernel(x_ref, w_ref, gain_ref, cos_ref, sin_ref, q_ref, kv_ref, h_ref):
    rows = x_ref.shape[1]
    x = x_ref[0].astype(F32)
    scale = lax.rsqrt(jnp.mean(x * x, -1, keepdims=True) + EPSILON)
    h = (x * scale * gain_ref[...]).astype(BF)
    h_ref[0] = h
    lin = mm(h, w_ref[...])
    cosine = cos_ref[...].reshape(rows, PAIR)
    sine = sin_ref[...].reshape(rows, PAIR)
    q = turn(lin[:, :PAIR], cosine, sine).astype(BF).astype(F32)
    q_ref[...] = (q * (1.0 / math.sqrt(HEAD_DIM))).astype(BF).reshape(q_ref.shape)
    flat = lin[:, PAIR:]
    kv = jnp.where(lanes(flat.shape) < HEAD_DIM, turn(flat, cosine, sine), flat)
    kv_ref[...] = kv.astype(BF).reshape(kv_ref.shape)


def project(x_all, weight, gain, cosine, sine):
    units, rows, width = x_all.shape
    length = units * rows // MICRO
    part = rows // MICRO
    place = pl.BlockSpec((MICRO, part, PAIR), lambda u: (0, u, 0))
    table = pl.BlockSpec((MICRO, part, PAIR), lambda u: (0, u, 0))
    return pl.pallas_call(
        project_kernel,
        grid=(units,),
        in_specs=[
            pl.BlockSpec((1, rows, width), lambda u: (u, 0, 0)),
            pl.BlockSpec((width, 2 * PAIR), lambda u: (0, 0)),
            pl.BlockSpec((1, width), lambda u: (0, 0)),
            table,
            table,
        ],
        out_specs=[place, place, pl.BlockSpec((1, rows, width), lambda u: (u, 0, 0))],
        out_shape=[
            jax.ShapeDtypeStruct((MICRO, length, PAIR), BF),
            jax.ShapeDtypeStruct((MICRO, length, PAIR), BF),
            jax.ShapeDtypeStruct((units, rows, width), BF),
        ],
        compiler_params=params(),
        cost_estimate=cost(2 * units * rows * width * 2 * PAIR, 4 * units * rows * width),
        name="project",
    )(
        x_all,
        weight,
        gain,
        cosine.reshape(MICRO, length, PAIR),
        sine.reshape(MICRO, length, PAIR),
    )


def front_heads(pair):
    pair = pair.astype(F32)
    front = lanes(pair.shape) < HEAD_DIM
    return jnp.concatenate(
        [jnp.where(front, pair, 0.0), jnp.where(front, pltpu.roll(pair, HEAD_DIM, 1), 0.0)], 0
    ).astype(BF)


def back_heads(pair):
    pair = pair.astype(F32)
    back = lanes(pair.shape) >= HEAD_DIM
    return jnp.concatenate(
        [jnp.where(back, pltpu.roll(pair, HEAD_DIM, 1), 0.0), jnp.where(back, pair, 0.0)], 0
    ).astype(BF)


def attend_kernel(q_ref, kv_ref, start_ref, o_ref, lse_ref, s_ref, kvt_ref, acc_ref):
    tile = pl.program_id(0)
    rows = q_ref.shape[0]
    chunks = kv_ref.shape[0]

    @pl.when(tile == 0)
    def _():
        for chunk in range(chunks):
            kvt_ref[chunk] = kv_ref[chunk].astype(F32).T.astype(BF)

    queries = front_heads(q_ref[...])
    start = jnp.concatenate([start_ref[0], start_ref[0]], -1)
    key_row = lax.broadcasted_iota(jnp.int32, (rows, 2 * rows), 0)
    query_row = lanes((rows, 2 * rows)) % rows

    def scores(chunk):
        found = mm(kv_ref[chunk], queries, NT)
        return jnp.where(key_row >= start - chunk * rows, found, HIDDEN)

    def fold(values, how):
        return how(values.reshape(rows // 8, 8, 2 * rows), axis=0)

    def fill(chunk, top):
        found = scores(chunk)
        s_ref[chunk] = found
        return jnp.maximum(top, fold(found, jnp.max))

    own = jnp.where(key_row <= query_row, scores(tile), HIDDEN)
    s_ref[tile] = own
    top = lax.fori_loop(0, tile, fill, fold(own, jnp.max))
    top = jnp.max(top, axis=0, keepdims=True)
    acc_ref[...] = jnp.zeros_like(acc_ref)

    def weigh(chunk, total):
        raised = jnp.exp(s_ref[chunk] - top)
        acc_ref[...] += mm(kvt_ref[chunk], raised.astype(BF))
        return total + fold(raised, jnp.sum)

    total = lax.fori_loop(0, tile + 1, weigh, jnp.zeros((8, 2 * rows), F32))
    total = jnp.sum(total, axis=0, keepdims=True)
    out = acc_ref[HEAD_DIM:, :] * (1.0 / total)
    out = jnp.concatenate([out[:, :rows], out[:, rows:]], 0)
    o_ref[...] = out.T.astype(BF)
    lse_ref[0] = top + jnp.log(total)


def attend(q, kv, starts, rows=256):
    length = q.shape[0]
    tiles = length // rows
    return pl.pallas_call(
        attend_kernel,
        grid=(tiles,),
        in_specs=[
            pl.BlockSpec((rows, PAIR), lambda t: (t, 0)),
            pl.BlockSpec((tiles, rows, PAIR), lambda t: (0, 0, 0)),
            pl.BlockSpec((1, 1, rows), lambda t: (t, 0, 0)),
        ],
        out_specs=[
            pl.BlockSpec((rows, PAIR), lambda t: (t, 0)),
            pl.BlockSpec((1, 1, 2 * rows), lambda t: (t, 0, 0)),
        ],
        out_shape=[
            jax.ShapeDtypeStruct((length, PAIR), BF),
            jax.ShapeDtypeStruct((tiles, 1, 2 * rows), F32),
        ],
        scratch_shapes=[
            pltpu.VMEM((tiles, rows, 2 * rows), F32),
            pltpu.VMEM((tiles, PAIR, rows), BF),
            pltpu.VMEM((PAIR, 2 * rows), F32),
        ],
        compiler_params=params(),
        cost_estimate=cost(8 * length * length * PAIR, 8 * length * PAIR),
        name="attend",
    )(q, kv.reshape(tiles, rows, PAIR), starts.reshape(tiles, 1, rows))


def attend_back_kernel(
    q_ref, kv_ref, start_ref, lse_ref, o_ref, do_ref, cos_ref, sin_ref, dq_ref, dkv_ref,
    kvt_ref, dkv_acc, dq_acc,
):
    tile = pl.program_id(0)
    rows = q_ref.shape[0]
    chunks = kv_ref.shape[0]

    @pl.when(tile == 0)
    def _():
        dkv_acc[...] = jnp.zeros_like(dkv_acc)
        for chunk in range(chunks):
            kvt_ref[chunk] = kv_ref[chunk].astype(F32).T.astype(BF)

    grad_o = do_ref[...].reshape(rows, PAIR)
    queries = front_heads(q_ref[...])
    grads = back_heads(grad_o)
    product = grad_o.astype(F32) * o_ref[...].astype(F32)
    half = lax.broadcasted_iota(jnp.int32, (8, PAIR), 0)
    picked = (lanes((8, PAIR)) // HEAD_DIM == half).astype(F32)
    sums = mm(picked, product, NT, HIGHEST)
    delta = jnp.concatenate([sums[0:1], sums[1:2]], -1)
    start = jnp.concatenate([start_ref[0], start_ref[0]], -1)
    lse = lse_ref[0]
    key_row = lax.broadcasted_iota(jnp.int32, (rows, 2 * rows), 0)
    query_row = lanes((rows, 2 * rows)) % rows
    dq_acc[...] = jnp.zeros_like(dq_acc)

    def step(chunk, causal):
        keys = kv_ref[chunk]
        seen = key_row >= start - chunk * rows
        if causal:
            seen = seen & (key_row <= query_row)
        found = jnp.where(seen, mm(keys, queries, NT), HIDDEN)
        prob = jnp.exp(found - lse)
        grad_s = (prob * (mm(keys, grads, NT) - delta)).astype(BF)
        dkv_acc[chunk] += mm(grad_s, queries) + mm(prob.astype(BF), grads)
        dq_acc[...] += mm(kvt_ref[chunk], grad_s)

    def earlier(chunk, carry):
        step(chunk, False)
        return carry

    lax.fori_loop(0, tile, earlier, 0)
    step(tile, True)
    dq = dq_acc[:HEAD_DIM, :] * (1.0 / math.sqrt(HEAD_DIM))
    dq = jnp.concatenate([dq[:, :rows], dq[:, rows:]], 0).T
    mine = pl.ds(pl.multiple_of(tile * rows, rows), rows)
    dq_ref[...] = turn(dq, cos_ref[mine, :], -sin_ref[mine, :]).astype(BF)

    @pl.when(tile == chunks - 1)
    def _():
        for chunk in range(chunks):
            flat = dkv_acc[chunk]
            spot = pl.ds(chunk * rows, rows)
            turned = turn(flat, cos_ref[spot, :], -sin_ref[spot, :])
            dkv_ref[spot, :] = jnp.where(lanes(flat.shape) < HEAD_DIM, turned, flat).astype(BF)


def attend_back(q, kv, starts, lse, o, grad_o, cosine, sine, rows=256):
    length = q.shape[0]
    tiles = length // rows
    units, _, part, _ = grad_o.shape
    span = rows // part
    half = tiles // MICRO
    whole = pl.BlockSpec((length, PAIR), lambda t: (0, 0))
    return pl.pallas_call(
        attend_back_kernel,
        grid=(tiles,),
        in_specs=[
            pl.BlockSpec((rows, PAIR), lambda t: (t, 0)),
            pl.BlockSpec((tiles, rows, PAIR), lambda t: (0, 0, 0)),
            pl.BlockSpec((1, 1, rows), lambda t: (t, 0, 0)),
            pl.BlockSpec((1, 1, 2 * rows), lambda t: (t, 0, 0)),
            pl.BlockSpec((rows, PAIR), lambda t: (t, 0)),
            pl.BlockSpec((span, 1, part, PAIR), lambda t: (t % half, t // half, 0, 0)),
            whole,
            whole,
        ],
        out_specs=[pl.BlockSpec((rows, PAIR), lambda t: (t, 0)), whole],
        out_shape=[
            jax.ShapeDtypeStruct((length, PAIR), BF),
            jax.ShapeDtypeStruct((length, PAIR), BF),
        ],
        scratch_shapes=[
            pltpu.VMEM((tiles, PAIR, rows), BF),
            pltpu.VMEM((tiles, rows, PAIR), F32),
            pltpu.VMEM((PAIR, 2 * rows), F32),
        ],
        compiler_params=params(),
        cost_estimate=cost(20 * length * length * PAIR, 16 * length * PAIR),
        name="attend_back",
    )(q, kv.reshape(tiles, rows, PAIR), starts.reshape(tiles, 1, rows), lse, o, grad_o, cosine, sine)


def one_hot(rank_rows, local, capacity):
    slots = lax.broadcasted_iota(jnp.int32, (capacity, rank_rows.shape[1]), 0).astype(F32)
    return jnp.concatenate([(rank_rows[e : e + 1] == slots).astype(F32) for e in range(local)], 0)


def route_kernel(
    local, capacity,
    own_ref, o_ref, x_ref, g_ref, wo_ref, gain_ref, router_ref, routes_ref,
    xs_ref, gs_ref, slot_gate_ref, rank_ref, x1_ref, h2_ref, gates_ref,
):
    unit = pl.program_id(0)
    rows = x_ref.shape[1]
    experts = router_ref.shape[0]
    groups = o_ref.shape[0]
    heads = jnp.concatenate([o_ref[i].reshape(rows, PAIR) for i in range(groups)], 1)
    x1 = x_ref[0].astype(F32) + mm(heads, wo_ref[...])
    scale = lax.rsqrt(jnp.mean(x1 * x1, -1, keepdims=True) + EPSILON)
    h2 = (x1 * scale * gain_ref[...]).astype(BF)
    logits = mm(router_ref[...], h2, NT)
    ids = lax.broadcasted_iota(jnp.int32, (experts, rows), 0)
    chosen = jnp.zeros((experts, rows), F32)
    for k in range(routes_ref.shape[1]):
        chosen = chosen + (ids == routes_ref[0, k : k + 1, :]).astype(F32)
    masked = jnp.where(chosen > 0, logits, HIDDEN)
    raised = jnp.where(chosen > 0, jnp.exp(masked - jnp.max(masked, 0, keepdims=True)), 0.0)
    gates = raised / jnp.sum(raised, 0, keepdims=True)
    before = lax.broadcasted_iota(jnp.int32, (rows, rows), 0) < lanes((rows, rows))
    rank = mm(chosen.astype(BF), before.astype(F32).astype(BF))
    rank = jnp.where(chosen > 0, rank, -1.0)[:8]
    rank_ref[0] = rank
    hot = one_hot(rank, local, capacity)
    low = hot.astype(BF)
    xs_ref[...] = mm(low, h2).astype(BF).reshape(xs_ref.shape)
    gs_ref[...] = mm(low, g_ref[0]).astype(BF).reshape(gs_ref.shape)
    spread = jnp.concatenate(
        [jnp.broadcast_to(gates[e : e + 1], (capacity, rows)) for e in range(local)], 0
    )
    slot_gate = jnp.sum(hot * spread, -1, keepdims=True)
    slot_gate_ref[...] = jnp.broadcast_to(slot_gate, (local * capacity, PAIR)).reshape(
        slot_gate_ref.shape
    )

    @pl.when(unit == own_ref[0])
    def _():
        x1_ref[...] = x1
        h2_ref[...] = h2
        gates_ref[...] = gates


def route(own, o_all, x_all, g_all, w_out, gain, router_t, routes_t, local, capacity):
    units, rows, width = x_all.shape
    groups = o_all.shape[0]
    part = rows // MICRO
    experts = router_t.shape[0]
    slots = pl.BlockSpec((1, local, capacity, width), lambda u, s: (u, 0, 0, 0))
    block = pl.BlockSpec((1, rows, width), lambda u, s: (u, 0, 0))

    def fixed(*shape):
        return pl.BlockSpec(shape, lambda u, s: (0,) * len(shape))

    return pl.pallas_call(
        functools.partial(route_kernel, local, capacity),
        grid_spec=pltpu.PrefetchScalarGridSpec(
            num_scalar_prefetch=1,
            grid=(units,),
            in_specs=[
                pl.BlockSpec((groups, MICRO, part, PAIR), lambda u, s: (0, 0, u, 0)),
                block,
                block,
                fixed(groups * PAIR, width),
                fixed(1, width),
                fixed(experts, width),
                pl.BlockSpec((1, routes_t.shape[1], rows), lambda u, s: (u, 0, 0)),
            ],
            out_specs=[
                slots,
                slots,
                pl.BlockSpec((1, local, capacity, PAIR), lambda u, s: (u, 0, 0, 0)),
                pl.BlockSpec((1, 8, rows), lambda u, s: (u, 0, 0)),
                fixed(rows, width),
                fixed(rows, width),
                fixed(experts, rows),
            ],
        ),
        out_shape=[
            jax.ShapeDtypeStruct((units, local, capacity, width), BF),
            jax.ShapeDtypeStruct((units, local, capacity, width), BF),
            jax.ShapeDtypeStruct((units, local, capacity, PAIR), F32),
            jax.ShapeDtypeStruct((units, 8, rows), F32),
            jax.ShapeDtypeStruct((rows, width), F32),
            jax.ShapeDtypeStruct((rows, width), BF),
            jax.ShapeDtypeStruct((experts, rows), F32),
        ],
        compiler_params=params(),
        cost_estimate=cost(
            2 * units * rows * width * (width + 2 * local * capacity), 14 * units * rows * width
        ),
        name="route",
    )(own, o_all, x_all, g_all, w_out, gain, router_t, routes_t)


def expert_kernel(
    local, experts,
    own_ref, xs_ref, gs_ref, gate_ref, w_ref,
    ys_ref, dx_ref, dg_ref, dw_ref,
):
    expert = pl.program_id(0)
    units, _, capacity, width = xs_ref.shape
    total = units * capacity
    shards, _, _, block, hidden = w_ref.shape
    half = block // 2
    depth = shards * block
    xs = xs_ref[...].reshape(total, width)
    gs = gs_ref[...].reshape(total, width)
    gate = gate_ref[...].reshape(total, PAIR)[:, :1]
    w_gate = w_ref[:, 0, 0].reshape(depth, hidden)
    w_up = w_ref[:, 0, 1].reshape(depth, hidden)
    w_down = jnp.concatenate(
        [w_ref[:, 0, 2, :half].reshape(hidden, hidden), w_ref[:, 0, 2, half:].reshape(hidden, hidden)], 1
    )
    a = mm(xs, w_gate)
    b = mm(xs, w_up)
    sigmoid = jax.nn.sigmoid(a)
    silu = a * sigmoid
    hid = (silu * b).astype(BF)
    y = mm(hid, w_down).astype(BF).astype(F32)
    ys_ref[...] = (gate * y).astype(BF).reshape(ys_ref.shape)
    back = mm(gs, w_down, NT)
    hid_full = hid.astype(F32)
    d_gate = jnp.sum(back * hid_full, -1, keepdims=True)
    d_hid = gate * back
    da = (d_hid * b * sigmoid * (1.0 + a * (1.0 - sigmoid))).astype(BF)
    db = (d_hid * silu).astype(BF)
    dx = mm(da, w_gate, NT) + mm(db, w_up, NT)
    dx_ref[...] = dx.astype(BF).reshape(dx_ref.shape)
    high = d_gate.astype(BF).astype(F32)
    rest = d_gate - high
    shape = (units, capacity, PAIR)
    source = lax.broadcasted_iota(jnp.int32, shape, 0)
    place = (local * (own_ref[0] - source) + expert + experts) % experts
    spot = lanes(shape)
    high = jnp.broadcast_to(high, (total, PAIR)).reshape(shape)
    rest = jnp.broadcast_to(rest, (total, PAIR)).reshape(shape)
    spread = jnp.where(spot == place, high, jnp.where(spot == place + experts, rest, 0.0))
    dg_ref[...] = spread.astype(BF).reshape(dg_ref.shape)
    d_gate_w = mm(xs, da, TN).astype(BF)
    dw_ref[:, 0, 0] = d_gate_w.reshape(shards, block, hidden)
    d_up_w = mm(xs, db, TN).astype(BF)
    dw_ref[:, 0, 1] = d_up_w.reshape(shards, block, hidden)
    scaled = (hid_full * gate).astype(BF)
    d_down_w = mm(scaled, gs, TN).astype(BF)
    dw_ref[:, 0, 2, :half] = d_down_w[:, :hidden].reshape(shards, half, hidden)
    dw_ref[:, 0, 2, half:] = d_down_w[:, hidden:].reshape(shards, half, hidden)


def run_experts(own, xs, gs, gate, weights, experts):
    units, local, capacity, width = xs.shape
    shards, _, kinds, block, hidden = weights.shape
    rows = pl.BlockSpec((units, 1, capacity, width), lambda e, s: (0, e, 0, 0))
    narrow = pl.BlockSpec((units, 1, capacity, PAIR), lambda e, s: (0, e, 0, 0))
    wide = pl.BlockSpec((shards, 1, kinds, block, hidden), lambda e, s: (0, e, 0, 0, 0))
    return pl.pallas_call(
        functools.partial(expert_kernel, local, experts),
        grid_spec=pltpu.PrefetchScalarGridSpec(
            num_scalar_prefetch=1,
            grid=(local,),
            in_specs=[rows, rows, narrow, wide],
            out_specs=[rows, rows, narrow, wide],
        ),
        out_shape=[
            jax.ShapeDtypeStruct(xs.shape, BF),
            jax.ShapeDtypeStruct(xs.shape, BF),
            jax.ShapeDtypeStruct((units, local, capacity, PAIR), BF),
            jax.ShapeDtypeStruct(weights.shape, BF),
        ],
        compiler_params=params(),
        cost_estimate=cost(
            18 * units * local * capacity * width * hidden, 4 * weights.size + 8 * xs.size
        ),
        name="run_experts",
    )(own, xs, gs, gate, weights)


def combine_kernel(local, capacity, rank_ref, ys_ref, dx_ref, dg_ref, mix_ref, grad_ref):
    slots = local * capacity
    width = ys_ref.shape[-1]
    hot = one_hot(rank_ref[0], local, capacity).astype(BF)
    mix_ref[0] = mm(hot, ys_ref[0].reshape(slots, width), TN).astype(BF)
    grad_ref[0, :, :width] = mm(hot, dx_ref[0].reshape(slots, width), TN).astype(BF)
    grad_ref[0, :, width:] = mm(hot, dg_ref[0].reshape(slots, PAIR), TN).astype(BF)


def combine(rank, ys, dx, dg):
    units, local, capacity, width = ys.shape
    rows = rank.shape[-1]
    slots = pl.BlockSpec((1, local, capacity, width), lambda u: (u, 0, 0, 0))
    return pl.pallas_call(
        functools.partial(combine_kernel, local, capacity),
        grid=(units,),
        in_specs=[
            pl.BlockSpec((1, 8, rows), lambda u: (u, 0, 0)),
            slots,
            slots,
            pl.BlockSpec((1, local, capacity, PAIR), lambda u: (u, 0, 0, 0)),
        ],
        out_specs=[
            pl.BlockSpec((1, rows, width), lambda u: (u, 0, 0)),
            pl.BlockSpec((1, rows, width + PAIR), lambda u: (u, 0, 0)),
        ],
        out_shape=[
            jax.ShapeDtypeStruct((units, rows, width), BF),
            jax.ShapeDtypeStruct((units, rows, width + PAIR), BF),
        ],
        compiler_params=params(),
        cost_estimate=cost(4 * units * rows * local * capacity * width, 16 * units * rows * width),
        name="combine",
    )(rank, ys, dx, dg)


def own_kernel(
    own_ref, grad_ref, mix_ref, x1_ref, h2_ref, gates_ref, g_ref, router_ref, gain_ref, wo_ref, o_ref,
    mixed_ref, dx1_ref, do_ref, dwo_ref, dr_ref, dgain_ref,
):
    rows, width = x1_ref.shape
    experts = router_ref.shape[0]
    groups = o_ref.shape[0]
    x1 = x1_ref[...]
    mixed_ref[...] = (x1 + mix_ref[...].astype(F32)).astype(BF)
    flat = grad_ref[:, width:].astype(F32).T
    d_gate = flat[:experts] + flat[experts : 2 * experts]
    gates = gates_ref[...]
    d_logit = gates * (d_gate - jnp.sum(gates * d_gate, 0, keepdims=True))
    router = router_ref[...].astype(F32)
    dh2 = grad_ref[:, :width].astype(F32) + mm(d_logit, router, TN, HIGHEST)
    dr_ref[...] = mm(d_logit, h2_ref[...].astype(F32), NN, HIGHEST)
    scale = lax.rsqrt(jnp.mean(x1 * x1, -1, keepdims=True) + EPSILON)
    normed = x1 * scale
    dgain_ref[...] = jnp.sum(dh2 * normed, 0, keepdims=True)
    dn = dh2 * gain_ref[...]
    dx1 = g_ref[...].astype(F32) + scale * (dn - normed * jnp.mean(dn * normed, -1, keepdims=True))
    dx1_ref[...] = dx1
    dz = dx1.astype(BF)
    grad_o = mm(dz, wo_ref[...], NT).astype(BF)
    heads = jnp.concatenate([o_ref[i].reshape(rows, PAIR) for i in range(groups)], 1)
    dwo = mm(heads, dz, TN).astype(BF)
    for i in range(groups):
        do_ref[i] = grad_o[:, i * PAIR : (i + 1) * PAIR]
        dwo_ref[i] = dwo[:, i * PAIR : (i + 1) * PAIR]


def own_tokens(own, grad, mix, x1, h2, gates, g, router_t, gain, w_out, o_all):
    rows, width = x1.shape
    groups = o_all.shape[0]
    part = rows // MICRO
    experts = router_t.shape[0]

    def fixed(*shape):
        return pl.BlockSpec(shape, lambda i, s: (0,) * len(shape))

    return pl.pallas_call(
        own_kernel,
        grid_spec=pltpu.PrefetchScalarGridSpec(
            num_scalar_prefetch=1,
            grid=(1,),
            in_specs=[
                fixed(*grad.shape),
                fixed(rows, width),
                fixed(rows, width),
                fixed(rows, width),
                fixed(experts, rows),
                fixed(rows, width),
                fixed(experts, width),
                fixed(1, width),
                fixed(groups * PAIR, width),
                pl.BlockSpec((groups, MICRO, part, PAIR), lambda i, s: (0, 0, s[0], 0)),
            ],
            out_specs=[
                fixed(rows, width),
                fixed(rows, width),
                fixed(groups, rows, PAIR),
                fixed(groups, groups * PAIR, PAIR),
                fixed(experts, width),
                fixed(1, width),
            ],
        ),
        out_shape=[
            jax.ShapeDtypeStruct((rows, width), BF),
            jax.ShapeDtypeStruct((rows, width), F32),
            jax.ShapeDtypeStruct((groups, rows, PAIR), BF),
            jax.ShapeDtypeStruct((groups, groups * PAIR, PAIR), BF),
            jax.ShapeDtypeStruct((experts, width), F32),
            jax.ShapeDtypeStruct((1, width), F32),
        ],
        compiler_params=params(),
        cost_estimate=cost(4 * rows * width * width, 20 * rows * width),
        name="own_tokens",
    )(own, grad, mix, x1, h2, gates, g, router_t, gain, w_out, o_all)


def project_back_kernel(x_ref, h_ref, dq_ref, dkv_ref, w_ref, dw_ref, dh_ref, dgain_ref):
    unit = pl.program_id(0)
    rows = x_ref.shape[1]

    @pl.when(unit == 0)
    def _():
        dw_ref[...] = jnp.zeros_like(dw_ref)
        dgain_ref[...] = jnp.zeros_like(dgain_ref)

    grads = jnp.concatenate(
        [dq_ref[...].reshape(rows, PAIR), dkv_ref[...].reshape(rows, PAIR)], 1
    )
    dw_ref[...] += mm(grads, h_ref[0], TN)
    dh = mm(grads, w_ref[...], NT)
    dh_ref[0] = dh.astype(BF)
    x = x_ref[0].astype(F32)
    scale = lax.rsqrt(jnp.mean(x * x, -1, keepdims=True) + EPSILON)
    dgain_ref[...] += jnp.sum(dh * (x * scale), 0, keepdims=True)


def project_back(x_all, h_all, dq, dkv, weight):
    units, rows, width = x_all.shape
    part = rows // MICRO
    block = pl.BlockSpec((1, rows, width), lambda u: (u, 0, 0))
    place = pl.BlockSpec((MICRO, part, PAIR), lambda u: (0, u, 0))
    return pl.pallas_call(
        project_back_kernel,
        grid=(units,),
        in_specs=[block, block, place, place, pl.BlockSpec((width, 2 * PAIR), lambda u: (0, 0))],
        out_specs=[
            pl.BlockSpec((2 * PAIR, width), lambda u: (0, 0)),
            block,
            pl.BlockSpec((1, width), lambda u: (0, 0)),
        ],
        out_shape=[
            jax.ShapeDtypeStruct((2 * PAIR, width), F32),
            jax.ShapeDtypeStruct((units, rows, width), BF),
            jax.ShapeDtypeStruct((1, width), F32),
        ],
        compiler_params=params(),
        cost_estimate=cost(8 * units * rows * width * PAIR, 6 * units * rows * width),
        name="project_back",
    )(x_all, h_all, dq.reshape(MICRO, -1, PAIR), dkv.reshape(MICRO, -1, PAIR), weight)


def per_device(
    tokens,
    routes,
    doc_starts,
    attn_gain,
    attn_q,
    attn_k,
    attn_v,
    attn_out,
    ffn_gain,
    router,
    w_gate,
    w_up,
    w_down,
    cotangent,
):
    part = tokens.shape[2]
    width = tokens.shape[3]
    top = routes.shape[3]
    experts = router.shape[1]
    local, shard, hidden = w_gate.shape
    units = lax.axis_size("ctx")
    shards = lax.axis_size("fsdp")
    rank = lax.axis_index("ctx")
    rows = MICRO * part
    length = units * rows
    capacity = MICRO * (5 * part * top // (4 * experts))
    own = rank.astype(jnp.int32).reshape(1)

    def gather_ctx(block):
        return lax.all_gather(block, "ctx", axis=0, tiled=False)

    piece = shard * PAIR // PAIR
    columns = jnp.concatenate(
        [
            lax.dynamic_slice_in_dim(attn_q, rank * PAIR, PAIR, 1),
            lax.dynamic_slice_in_dim(attn_k, rank * HEAD_DIM, HEAD_DIM, 1),
            lax.dynamic_slice_in_dim(attn_v, rank * HEAD_DIM, HEAD_DIM, 1),
            lax.dynamic_slice_in_dim(attn_out, rank * PAIR, PAIR, 1),
        ],
        1,
    )
    small = jnp.concatenate([attn_gain, ffn_gain, router.reshape(-1)])
    wide = columns.shape[1]
    extra = -(-small.shape[0] // (8 * wide)) * 8
    small = jnp.pad(small, (0, extra * wide - small.shape[0])).reshape(extra, wide)
    dense = lax.all_gather(jnp.concatenate([columns, small], 0), "fsdp", axis=0, tiled=False)
    columns = dense[:, :piece].reshape(shards * shard, wide)
    w_qkv = columns[:, : 2 * PAIR]
    w_out_part = columns[:, 2 * PAIR :]
    small = dense[:, piece:].reshape(shards, -1)
    gain_one = small[:, :shard].reshape(1, width).astype(F32)
    gain_two = small[:, shard : 2 * shard].reshape(1, width).astype(F32)
    router_all = small[:, 2 * shard : 2 * shard + shard * experts].reshape(width, experts)
    router_t = jnp.roll(router_all.T, -local * rank, 0)

    expert_pack = jnp.stack(
        [w_gate, w_up, jnp.concatenate([w_down[..., :hidden], w_down[..., hidden:]], 1)], 1
    )
    weights = lax.all_gather(expert_pack, "fsdp", axis=0, tiled=False)

    x_own = tokens[0].reshape(rows, width)
    g_own = cotangent[0].reshape(rows, width)
    x_all = gather_ctx(x_own)
    g_all = gather_ctx(g_own)
    w_out = gather_ctx(w_out_part).transpose(1, 0, 2).reshape(units * PAIR, width)
    index = jnp.concatenate([routes[0].reshape(rows, top).T, doc_starts[0].reshape(1, rows)], 0)
    index = gather_ctx(index)
    routes_t = (index[:, :top] - local * rank) % experts
    starts = index[:, top].reshape(units, MICRO, part).transpose(1, 0, 2).reshape(1, length)

    cosine, sine = angle_tables(length)
    q, kv, h_all = project(x_all, w_qkv, gain_one, cosine, sine)
    q = q.reshape(length, PAIR)
    kv = kv.reshape(length, PAIR)
    o, lse = attend(q, kv, starts)
    o_all = gather_ctx(o).reshape(units, MICRO, length // MICRO, PAIR)
    xs, gs, slot_gate, ranks, x1, h2, gates = route(
        own, o_all, x_all, g_all, w_out, gain_two, router_t, routes_t, local, capacity
    )
    ys, dx, dg, dw = run_experts(own, xs, gs, slot_gate, weights, experts)
    mix, grad = combine(ranks, ys, dx, dg)
    grad = lax.psum_scatter(grad, "ctx", scatter_dimension=0, tiled=True)[0]
    mix = lax.psum_scatter(mix, "ctx", scatter_dimension=0, tiled=True)[0]
    mixed, dx1, grad_o, dwo, d_router, d_gain_two = own_tokens(
        own, grad, mix, x1, h2, gates, g_own, router_t, gain_two, w_out, o_all
    )
    grad_o = lax.all_to_all(grad_o, "ctx", split_axis=0, concat_axis=0, tiled=True)
    grad_o = grad_o.reshape(units, MICRO, part, PAIR)
    dwo = lax.psum_scatter(dwo, "ctx", scatter_dimension=0, tiled=True)[0]
    dq, dkv = attend_back(q, kv, starts, lse, o, grad_o, cosine, sine)
    dw_qkv, dh, d_gain_one = project_back(x_all, h_all, dq, dkv, w_qkv)
    dh = lax.psum_scatter(dh, "ctx", scatter_dimension=0, tiled=True)[0].astype(F32)

    x = x_own.astype(F32)
    scale = lax.rsqrt(jnp.mean(x * x, -1, keepdims=True) + EPSILON)
    normed = x * scale
    dn = dh * gain_one
    d_tokens = dx1 + scale * (dn - normed * jnp.mean(dn * normed, -1, keepdims=True))

    pack = jnp.concatenate(
        [
            dw_qkv.T.astype(BF),
            dwo.astype(BF),
            jnp.roll(d_router, local * rank, 0).T.astype(BF),
            d_gain_one.T.astype(BF),
            d_gain_two.T.astype(BF),
        ],
        1,
    )
    used = pack.shape[1]
    pack = jnp.pad(pack, ((0, 0), (0, -used % PAIR))).reshape(shards, shard, -1)
    pack = lax.all_to_all(pack, "fsdp", split_axis=0, concat_axis=0, tiled=True)
    pack = jnp.sum(pack.astype(F32), 0).astype(BF)
    pack = gather_ctx(pack).astype(F32)

    def wide_columns(first, count):
        return pack[:, :, first : first + count].transpose(1, 0, 2).reshape(shard, units * count)

    def summed(first, count):
        return jnp.sum(pack[:, :, first : first + count], 0)

    dw = lax.psum_scatter(dw, "fsdp", scatter_dimension=0, tiled=True)[0].astype(F32)
    d_down = dw[:, 2]
    d_down = jnp.concatenate([d_down[:, : shard // 2], d_down[:, shard // 2 :]], -1)
    first_small = 3 * PAIR
    return (
        mixed.reshape(1, MICRO, part, width),
        d_tokens.reshape(1, MICRO, part, width),
        summed(first_small + experts, 1).reshape(shard),
        wide_columns(0, PAIR),
        wide_columns(PAIR, HEAD_DIM),
        wide_columns(PAIR + HEAD_DIM, HEAD_DIM),
        wide_columns(2 * PAIR, PAIR),
        summed(first_small + experts + 1, 1).reshape(shard),
        summed(first_small, experts),
        dw[:, 0],
        dw[:, 1],
        d_down,
    )


def solution(mesh):
    return jax.shard_map(
        per_device,
        mesh=mesh,
        in_specs=(
            P("fsdp", None, "ctx", None),
            P("fsdp", None, "ctx", None),
            P("fsdp", None, "ctx"),
            P("fsdp"),
            P("fsdp", None),
            P("fsdp", None),
            P("fsdp", None),
            P("fsdp", None),
            P("fsdp"),
            P("fsdp", None),
            P("ctx", "fsdp", None),
            P("ctx", "fsdp", None),
            P("ctx", "fsdp", None),
            P("fsdp", None, "ctx", None),
        ),
        out_specs=(
            P("fsdp", None, "ctx", None),
            P("fsdp", None, "ctx", None),
            P("fsdp"),
            P("fsdp", None),
            P("fsdp", None),
            P("fsdp", None),
            P("fsdp", None),
            P("fsdp"),
            P("fsdp", None),
            P("ctx", "fsdp", None),
            P("ctx", "fsdp", None),
            P("ctx", "fsdp", None),
        ),
        check_vma=False,
    )
```

```python
import functools
import math

import jax
import jax.numpy as jnp
import numpy as np
from jax import lax
from jax.experimental import pallas as pl
from jax.experimental.pallas import tpu as pltpu
from jax.sharding import PartitionSpec as P

HEADS = 16
KV_HEADS = 8
HEAD_DIM = 64
MICRO = 2
EPSILON = 1e-06
HIDDEN = -1e30
BF = jnp.bfloat16
F32 = jnp.float32
HIGHEST = lax.Precision.HIGHEST
PAIR = 2 * HEAD_DIM
MEBI = 1024 * 1024

NN = (((1,), (0,)), ((), ()))
NT = (((1,), (1,)), ((), ()))
TN = (((0,), (0,)), ((), ()))


def mm(left, right, dims=NN, precision=None):
    return lax.dot_general(left, right, dims, preferred_element_type=F32, precision=precision)


def params(mebibytes):
    return pltpu.CompilerParams(vmem_limit_bytes=mebibytes * MEBI)


def cost(flops, moved):
    return pl.CostEstimate(flops=int(flops), bytes_accessed=int(moved), transcendentals=0)


def busy(microseconds):
    return pl.CostEstimate(flops=int(1.1e9 * microseconds), bytes_accessed=1, transcendentals=0)


LIGHT = pl.CostEstimate(flops=1, bytes_accessed=1, transcendentals=0)


def together(*values):
    return lax.optimization_barrier(values)


def lanes(shape):
    return lax.broadcasted_iota(jnp.int32, shape, len(shape) - 1)


def turn(values, cosine, sine):
    spot = lanes(values.shape) % HEAD_DIM
    swapped = jnp.where(
        spot < HEAD_DIM // 2,
        pltpu.roll(values, PAIR - HEAD_DIM // 2, 1),
        pltpu.roll(values, HEAD_DIM // 2, 1),
    )
    return values * cosine + swapped * sine


def angle_tables(first, count, step):
    half = HEAD_DIM // 2
    frequencies = 10000.0 ** (-2.0 * np.arange(half) / HEAD_DIM)
    turned = (first + step * np.arange(count))[:, None] * frequencies[None, :]
    return (
        jnp.asarray(np.concatenate([np.cos(turned)] * 4, -1), F32),
        jnp.asarray(np.concatenate([np.sin(turned)] * 4, -1), F32),
    )


def block_angles(tables, block):
    cos_a, sin_a, cos_b, sin_b = tables
    cos_a, sin_a = cos_a[pl.ds(block, 1), :], sin_a[pl.ds(block, 1), :]
    cos_b, sin_b = cos_b[...], sin_b[...]
    sine = sin_a * cos_b + cos_a * sin_b
    back = lanes(sine.shape) % HEAD_DIM >= HEAD_DIM // 2
    return cos_a * cos_b - sin_a * sin_b, jnp.where(back, sine, -sine)


VMEM = pl.BlockSpec(memory_space=pltpu.VMEM)
SMEM = pl.BlockSpec(memory_space=pltpu.SMEM)
ANY = pl.BlockSpec(memory_space=pl.ANY)


def prepare_kernel(
    rank_ref, x_ref, routes_ref, starts_ref, q_ref, k_ref, v_ref, o_ref, gain_one_ref, gain_two_ref,
    router_ref, gate_ref, up_ref, down_ref,
    tall_ref, dense_ref, pack_ref,
):
    rank = rank_ref[0]
    local, shard, hidden = gate_ref.shape
    half = shard // 2
    for i in range(local):
        first = 3 * shard * i
        pack_ref[first : first + shard, :] = gate_ref[i]
        pack_ref[first + shard : first + 2 * shard, :] = up_ref[i]
        first = first + 2 * shard
        pack_ref[first : first + half, :] = down_ref[i, :, :hidden]
        pack_ref[first + half : first + shard, :] = down_ref[i, :, hidden:]
    rows = x_ref.shape[0]
    tall_ref[:rows, :] = x_ref[...]
    routes = routes_ref[...].astype(F32)
    starts = starts_ref[...]
    high = (starts // HEAD_DIM).astype(F32)
    low = (starts % HEAD_DIM).astype(F32)
    none = jnp.zeros_like(high)
    index = [routes[i : i + 1] for i in range(routes.shape[0])] + [high, low, none, none]
    across = x_ref.shape[1] // rows
    index = [
        jnp.concatenate(index[i : i + across], 1) for i in range(0, len(index), across)
    ]
    spare = tall_ref.shape[0] - rows
    index.append(jnp.zeros((spare - len(index), x_ref.shape[1]), F32))
    tall_ref[rows:, :] = jnp.concatenate(index, 0).astype(BF)

    mine = pl.ds(pl.multiple_of(rank * PAIR, PAIR), PAIR)
    dense_ref[:shard, :PAIR] = q_ref[:, mine]
    dense_ref[:shard, 2 * PAIR :] = o_ref[:, mine]
    pair = pl.ds(pl.multiple_of(rank // 2 * PAIR, PAIR), PAIR)
    keys = k_ref[:, pair].astype(F32)
    values = v_ref[:, pair].astype(F32)
    odd = rank % 2 == 1
    keys = jnp.where(odd, pltpu.roll(keys, HEAD_DIM, 1), keys)
    values = jnp.where(odd, values, pltpu.roll(values, HEAD_DIM, 1))
    front = lanes(keys.shape) < HEAD_DIM
    dense_ref[:shard, PAIR : 2 * PAIR] = jnp.where(front, keys, values).astype(BF)
    router = router_ref[...].astype(F32)
    gains = jnp.concatenate(
        [gain_one_ref[...].astype(F32), gain_two_ref[...].astype(F32), jnp.zeros((6, shard), F32)], 0
    )
    groups = [router[i : i + 8] for i in range(0, router.shape[0], 8)]
    empty = jnp.zeros_like(gains)
    dense_ref[shard:, :] = jnp.concatenate([*groups, gains, empty], 1).astype(BF)


def prepare(rank, x, routes_t, starts, attn, gains, router_t, experts):
    rows, width = x.shape
    local, shard, hidden = experts[0].shape
    return pl.pallas_call(
        prepare_kernel,
        in_specs=[SMEM] + [VMEM] * 13,
        out_specs=[VMEM] * 3,
        out_shape=[
            jax.ShapeDtypeStruct((rows + 16, width), BF),
            jax.ShapeDtypeStruct((shard + 8, 3 * PAIR), BF),
            jax.ShapeDtypeStruct((local * 3 * shard, hidden), BF),
        ],
        compiler_params=params(56),
        cost_estimate=busy(3),
        name="prepare",
    )(rank, x, routes_t, starts, *attn, *gains, router_t, *experts)


def load_blocks(blocks, target, sems, rows):
    found, used = [], 0
    for i, parts in enumerate(blocks):
        copies, first = [], 0
        for part in parts:
            count = min(part.shape[0], rows - first)
            copies.append(
                pltpu.make_async_copy(
                    part.at[pl.ds(0, count)], target.at[i, pl.ds(first, count)], sems.at[used]
                )
            )
            first, used = first + count, used + 1
        for copy in copies:
            copy.start()
        found.append(copies)
    return found


def project_kernel(counts, top, order_ref, *refs):
    x_refs, refs = split_refs(refs, counts)
    (
        dense_ref, cos_a_ref, sin_a_ref, cos_b_ref, sin_b_ref,
        q_ref, kv_ref, routes_ref, starts_ref, w_ref, gain_one_ref, gain_two_ref, router_ref,
        held_ref, sems,
    ) = refs
    tables = (cos_a_ref, sin_a_ref, cos_b_ref, sin_b_ref)
    tall, width = held_ref.shape[1:]
    units = len(counts)
    part = q_ref.shape[1] // units
    rows = MICRO * part
    shards = dense_ref.shape[0]
    shard = width // shards
    loads = load_blocks(x_refs, held_ref, sems, tall)
    w_ref[...] = dense_ref[:, :shard, : 2 * PAIR].reshape(width, 2 * PAIR)
    for i in range(0, shards, 2):
        small = [dense_ref[i + j, shard:, :].astype(F32) for j in range(2)]
        spot = pl.ds(i * shard, PAIR)
        front = lanes((8, PAIR)) < HEAD_DIM
        for group in range(5):
            lane = group // 2 * PAIR
            pair = [piece[:, lane : lane + PAIR] for piece in small]
            if group % 2 == 0:
                both = jnp.where(front, pair[0], pltpu.roll(pair[1], HEAD_DIM, 1))
            else:
                both = jnp.where(front, pltpu.roll(pair[0], HEAD_DIM, 1), pair[1])
            if group < 4:
                router_ref[group * 8 : group * 8 + 8, spot] = both
            else:
                gain_one_ref[:, spot] = both[0:1]
                gain_two_ref[:, spot] = both[1:2]
    gain = gain_one_ref[...]
    for unit in range(units):
        for copy in loads[unit]:
            copy.wait()
        x = held_ref[unit, :rows, :].astype(F32)
        scale = lax.rsqrt(jnp.mean(x * x, -1, keepdims=True) + EPSILON)
        lin = mm((x * scale * gain).astype(BF), w_ref[...])
        place = order_ref[unit]
        for m in range(MICRO):
            cosine, sine = block_angles(tables, m * units + place)
            here = lin[m * part : (m + 1) * part]
            spot = pl.ds(pl.multiple_of(place * part, part), part)
            q = turn(here[:, :PAIR], cosine, sine).astype(BF).astype(F32)
            q_ref[m, spot, :] = (q * (1.0 / math.sqrt(HEAD_DIM))).astype(BF)
            kv = here[:, PAIR:]
            kv = jnp.where(lanes(kv.shape) < HEAD_DIM, turn(kv, cosine, sine), kv)
            kv_ref[m, spot, :] = kv.astype(BF)
        index = held_ref[unit, rows:, :].astype(F32)
        across = width // rows

        def number(i, index=index, across=across):
            first = (i % across) * rows
            return index[i // across : i // across + 1, first : first + rows]

        routes_ref[unit] = jnp.concatenate([number(k) for k in range(top)], 0)
        starts = number(top) * HEAD_DIM + number(top + 1)
        starts_ref[unit] = jnp.broadcast_to(starts, starts_ref.shape[1:])


def project(order, x_blocks, top, dense, tables, experts):
    units = len(x_blocks)
    tall, width = x_blocks[0][0].shape
    part = tables[2].shape[0]
    parts = flat(x_blocks)
    index = jax.ShapeDtypeStruct((units, 8, MICRO * part), F32)
    return pl.pallas_call(
        functools.partial(project_kernel, counts_of(x_blocks), top),
        in_specs=[SMEM] + [ANY] * len(parts) + [VMEM] * 5,
        out_specs=[VMEM] * 8,
        out_shape=[
            jax.ShapeDtypeStruct((MICRO, units * part, PAIR), BF),
            jax.ShapeDtypeStruct((MICRO, units * part, PAIR), BF),
            index,
            index,
            jax.ShapeDtypeStruct((width, 2 * PAIR), BF),
            jax.ShapeDtypeStruct((1, width), F32),
            jax.ShapeDtypeStruct((1, width), F32),
            jax.ShapeDtypeStruct((experts, width), F32),
        ],
        scratch_shapes=[
            pltpu.VMEM((units, tall, width), BF),
            pltpu.SemaphoreType.DMA((len(parts),)),
        ],
        compiler_params=params(48),
        cost_estimate=busy(8),
        name="project",
    )(order, *parts, dense, *tables)


def front_heads(pair):
    pair = pair.astype(F32)
    front = lanes(pair.shape) < HEAD_DIM
    return jnp.concatenate(
        [jnp.where(front, pair, 0.0), jnp.where(front, pltpu.roll(pair, HEAD_DIM, 1), 0.0)], 0
    ).astype(BF)


def back_heads(pair):
    pair = pair.astype(F32)
    back = lanes(pair.shape) >= HEAD_DIM
    return jnp.concatenate(
        [jnp.where(back, pltpu.roll(pair, HEAD_DIM, 1), 0.0), jnp.where(back, pair, 0.0)], 0
    ).astype(BF)


def tile_starts(find_ref, start_ref, tile, rows):
    units, _, both = start_ref.shape
    part = both // MICRO
    span = rows // part
    half = units // span
    spot = pl.ds(pl.multiple_of(lax.div(tile, half) * part, part), part)
    pieces = [start_ref[find_ref[lax.rem(tile, half) * span + i], 0:1, spot] for i in range(span)]
    return jnp.concatenate(pieces + pieces, -1)


def attend_kernel(find_ref, q_ref, kv_ref, start_ref, o_ref, lse_ref, s_ref, kvt_ref, p_ref):
    tile = pl.program_id(0)
    rows = q_ref.shape[0]
    tiles = kv_ref.shape[0]

    @pl.when(tile == 0)
    def _():
        for chunk in range(tiles):
            kvt_ref[:, chunk * rows : (chunk + 1) * rows] = kv_ref[chunk].astype(F32).T.astype(BF)

    queries = front_heads(q_ref[...])
    start = tile_starts(find_ref, start_ref, tile, rows).astype(jnp.int32)
    key_row = lax.broadcasted_iota(jnp.int32, (rows, 2 * rows), 0)
    query_row = lanes((rows, 2 * rows)) % rows

    def fold(values, how):
        return how(values.reshape(rows // 8, 8, 2 * rows), axis=0)

    def one_tile(last):
        top = None
        for chunk in range(last + 1):
            seen = key_row >= start - chunk * rows
            if chunk == last:
                seen = seen & (key_row <= query_row)
            found = jnp.where(seen, mm(kv_ref[chunk], queries, NT), HIDDEN)
            s_ref[chunk] = found
            here = fold(found, jnp.max)
            top = here if top is None else jnp.maximum(top, here)
        top = jnp.max(top, axis=0, keepdims=True)
        total = jnp.zeros((8, 2 * rows), F32)
        for chunk in range(last + 1):
            raised = jnp.exp(s_ref[chunk] - top)
            p_ref[chunk * rows : (chunk + 1) * rows, :] = raised.astype(BF)
            total = total + fold(raised, jnp.sum)
        total = jnp.sum(total, axis=0, keepdims=True)
        depth = (last + 1) * rows
        out = mm(kvt_ref[:, :depth], p_ref[:depth, :])[HEAD_DIM:, :] * (1.0 / total)
        out = jnp.concatenate([out[:, :rows], out[:, rows:]], 0)
        o_ref[...] = out.T.astype(BF)
        lse_ref[0] = top + jnp.log(total)

    for last in range(tiles):
        pl.when(tile == last)(functools.partial(one_tile, last))


def attend(find, q, kv, starts, rows=256):
    length = q.shape[0]
    tiles = length // rows
    return pl.pallas_call(
        attend_kernel,
        grid_spec=pltpu.PrefetchScalarGridSpec(
            num_scalar_prefetch=1,
            grid=(tiles,),
            in_specs=[
                pl.BlockSpec((rows, PAIR), lambda t, s: (t, 0)),
                pl.BlockSpec((tiles, rows, PAIR), lambda t, s: (0, 0, 0)),
                pl.BlockSpec(starts.shape, lambda t, s: (0, 0, 0)),
            ],
            out_specs=[
                pl.BlockSpec((rows, PAIR), lambda t, s: (t, 0)),
                pl.BlockSpec((1, 1, 2 * rows), lambda t, s: (t, 0, 0)),
            ],
            scratch_shapes=[
                pltpu.VMEM((tiles, rows, 2 * rows), F32),
                pltpu.VMEM((PAIR, length), BF),
                pltpu.VMEM((length, 2 * rows), BF),
            ],
        ),
        out_shape=[
            jax.ShapeDtypeStruct((length, PAIR), BF),
            jax.ShapeDtypeStruct((tiles, 1, 2 * rows), F32),
        ],
        compiler_params=params(14),
        cost_estimate=busy(20),
        name="attend",
    )(find, q, kv.reshape(tiles, rows, PAIR), starts)


def attend_back_kernel(
    find_ref, q_ref, kv_ref, start_ref, lse_ref, o_ref, do_ref, cos_a_ref, sin_a_ref, cos_b_ref, sin_b_ref,
    dq_ref, dkv_ref, kvt_ref, dkv_acc, ds_ref, dqt_ref,
):
    tile = pl.program_id(0)
    rows = q_ref.shape[0]
    chunks = kv_ref.shape[0]

    @pl.when(tile == 0)
    def _():
        dkv_acc[...] = jnp.zeros_like(dkv_acc)
        for chunk in range(chunks):
            kvt_ref[:, chunk * rows : (chunk + 1) * rows] = kv_ref[chunk].astype(F32).T.astype(BF)

    grad_o = do_ref[...].reshape(rows, PAIR)
    queries = front_heads(q_ref[...])
    grads = back_heads(grad_o)
    product = grad_o.astype(F32) * o_ref[...].astype(F32)
    half = lax.broadcasted_iota(jnp.int32, (8, PAIR), 0)
    picked = (lanes((8, PAIR)) // HEAD_DIM == half).astype(F32)
    sums = mm(picked, product, NT, HIGHEST)
    delta = jnp.concatenate([sums[0:1], sums[1:2]], -1)
    start = tile_starts(find_ref, start_ref, tile, rows).astype(jnp.int32)
    lse = lse_ref[0]
    key_row = lax.broadcasted_iota(jnp.int32, (rows, 2 * rows), 0)
    query_row = lanes((rows, 2 * rows)) % rows

    def one_tile(last):
        for chunk in range(last + 1):
            keys = kv_ref[chunk]
            seen = key_row >= start - chunk * rows
            if chunk == last:
                seen = seen & (key_row <= query_row)
            found = jnp.where(seen, mm(keys, queries, NT), HIDDEN)
            prob = jnp.exp(found - lse)
            grad_s = (prob * (mm(keys, grads, NT) - delta)).astype(BF)
            ds_ref[chunk * rows : (chunk + 1) * rows, :] = grad_s
            dkv_acc[chunk] += mm(grad_s, queries) + mm(prob.astype(BF), grads)
        depth = (last + 1) * rows
        dqt_ref[...] = mm(kvt_ref[:, :depth], ds_ref[:depth, :])[:HEAD_DIM]

    for last in range(chunks):
        pl.when(tile == last)(functools.partial(one_tile, last))

    dq = dqt_ref[...] * (1.0 / math.sqrt(HEAD_DIM))
    dq = jnp.concatenate([dq[:, :rows], dq[:, rows:]], 0).T
    tables = (cos_a_ref, sin_a_ref, cos_b_ref, sin_b_ref)
    part = cos_b_ref.shape[0]

    def turn_back(values, first):
        pieces = []
        for i in range(rows // part):
            cosine, sine = block_angles(tables, first + i)
            pieces.append(turn(values[i * part : (i + 1) * part], cosine, -sine))
        return jnp.concatenate(pieces, 0)

    dq_ref[...] = turn_back(dq, tile * (rows // part)).astype(BF)

    @pl.when(tile == chunks - 1)
    def _():
        for chunk in range(chunks):
            flat = dkv_acc[chunk]
            spot = pl.ds(chunk * rows, rows)
            turned = turn_back(flat, chunk * (rows // part))
            dkv_ref[spot, :] = jnp.where(lanes(flat.shape) < HEAD_DIM, turned, flat).astype(BF)


def attend_back(find, q, kv, starts, lse, o, grad_o, tables, rows=256):
    length = q.shape[0]
    tiles = length // rows
    units, _, part, _ = grad_o.shape
    span = rows // part
    half = tiles // MICRO
    whole = pl.BlockSpec((length, PAIR), lambda t, s: (0, 0))
    return pl.pallas_call(
        attend_back_kernel,
        grid_spec=pltpu.PrefetchScalarGridSpec(
            num_scalar_prefetch=1,
            grid=(tiles,),
            in_specs=[
                pl.BlockSpec((rows, PAIR), lambda t, s: (t, 0)),
                pl.BlockSpec((tiles, rows, PAIR), lambda t, s: (0, 0, 0)),
                pl.BlockSpec(starts.shape, lambda t, s: (0, 0, 0)),
                pl.BlockSpec((1, 1, 2 * rows), lambda t, s: (t, 0, 0)),
                pl.BlockSpec((rows, PAIR), lambda t, s: (t, 0)),
                pl.BlockSpec((span, 1, part, PAIR), lambda t, s: (t % half, t // half, 0, 0)),
            ]
            + [pl.BlockSpec(table.shape, lambda t, s: (0, 0)) for table in tables],
            out_specs=[pl.BlockSpec((rows, PAIR), lambda t, s: (t, 0)), whole],
            scratch_shapes=[
                pltpu.VMEM((PAIR, length), BF),
                pltpu.VMEM((tiles, rows, PAIR), F32),
                pltpu.VMEM((length, 2 * rows), BF),
                pltpu.VMEM((HEAD_DIM, 2 * rows), F32),
            ],
        ),
        out_shape=[
            jax.ShapeDtypeStruct((length, PAIR), BF),
            jax.ShapeDtypeStruct((length, PAIR), BF),
        ],
        compiler_params=params(56),
        cost_estimate=busy(26),
        name="attend_back",
    )(find, q, kv.reshape(tiles, rows, PAIR), starts, lse, o, grad_o, *tables)


def one_hot(rank_rows, local, capacity):
    slots = lax.broadcasted_iota(jnp.int32, (capacity, rank_rows.shape[1]), 0).astype(F32)
    return jnp.concatenate([(rank_rows[e : e + 1] == slots).astype(F32) for e in range(local)], 0)


def gather_lanes(order_ref, blocks, out_ref):
    for i, refs in enumerate(blocks):
        spot = pl.multiple_of(order_ref[i] * PAIR, PAIR)
        first = 0
        for ref in refs:
            part = ref[...].reshape(-1, PAIR)
            last = first + part.shape[0]
            out_ref[first:last, pl.ds(spot, PAIR)] = part
            first = last


def chosen_rows(order_ref, routes, local, experts):
    rows = routes.shape[1]
    routes = routes.astype(jnp.int32) - local * order_ref[0]
    routes = jnp.where(routes < 0, routes + experts, routes)
    ids = lax.broadcasted_iota(jnp.int32, (experts, rows), 0)
    chosen = jnp.zeros((experts, rows), F32)
    for k in range(routes.shape[0]):
        chosen = chosen + (ids == routes[k : k + 1, :]).astype(F32)
    return chosen


def pick_kernel(local, capacity, experts, counts, order_ref, *refs):
    g_refs, refs = split_refs(refs, counts)
    routes_ref, rank_ref, gs_ref, wo_ref, held_ref, out_ref, load_sems, store_sems = refs
    units, tall, width = held_ref.shape
    rows = tall - PAIR
    loads = load_blocks(g_refs, held_ref, load_sems, tall)
    before = lax.broadcasted_iota(jnp.int32, (rows, rows), 0) < lanes((rows, rows))
    before = before.astype(F32).astype(BF)
    stores = []
    for unit in range(units):
        chosen = chosen_rows(order_ref, routes_ref[unit], local, experts)[:8]
        rank = jnp.where(chosen > 0, mm(chosen.astype(BF), before), -1.0)
        rank_ref[unit] = rank
        hot = one_hot(rank, local, capacity).astype(BF)
        for copy in loads[unit]:
            copy.wait()
        out_ref[unit] = mm(hot, held_ref[unit, :rows, :]).astype(BF)
        stores.append(pltpu.make_async_copy(out_ref.at[unit], gs_ref.at[unit], store_sems.at[unit]))
        stores[-1].start()
        spot = pl.ds(pl.multiple_of(order_ref[unit] * PAIR, PAIR), PAIR)
        for i in range(width // PAIR):
            here = slice(i * PAIR, (i + 1) * PAIR)
            wo_ref[here, spot] = held_ref[unit, rows:, here]
    for copy in stores:
        copy.wait()


def pick(order, g_blocks, routes, local, capacity, experts):
    units = len(g_blocks)
    tall, width = g_blocks[0][0].shape
    rows = routes.shape[-1]
    parts = flat(g_blocks)
    return pl.pallas_call(
        functools.partial(pick_kernel, local, capacity, experts, counts_of(g_blocks)),
        in_specs=[SMEM] + [ANY] * len(parts) + [VMEM],
        out_specs=[VMEM, ANY, VMEM],
        out_shape=[
            jax.ShapeDtypeStruct((units, 8, rows), F32),
            jax.ShapeDtypeStruct((units, local * capacity, width), BF),
            jax.ShapeDtypeStruct((units * PAIR, width), BF),
        ],
        scratch_shapes=[
            pltpu.VMEM((units, tall, width), BF),
            pltpu.VMEM((units, local * capacity, width), BF),
            pltpu.SemaphoreType.DMA((len(parts),)),
            pltpu.SemaphoreType.DMA((units,)),
        ],
        compiler_params=params(56),
        cost_estimate=busy(1),
        name="pick",
    )(order, *parts, routes)


def lane_copies(order_ref, blocks, target, sems):
    copies = []
    for i, parts in enumerate(blocks):
        spot = pl.ds(pl.multiple_of(order_ref[i] * PAIR, PAIR), PAIR)
        first = 0
        for part in parts:
            count = part.shape[0]
            place = target.at[(pl.ds(first, count),) + (slice(None),) * (len(part.shape) - 2) + (spot,)]
            copies.append(pltpu.make_async_copy(part, place, sems.at[len(copies)]))
            first = first + count
    return copies


def route_kernel(local, capacity, o_counts, x_counts, order_ref, *refs):
    o_refs, refs = split_refs(refs, o_counts)
    x_refs, refs = split_refs(refs, x_counts)
    (
        wo_ref, gain_ref, router_ref, routes_ref, rank_ref,
        xs_ref, rows_ref, x1_ref, h2_ref, gates_ref, heads_own_ref,
        heads_ref, held_ref, out_ref, o_sems, x_sems, store_sems,
    ) = refs
    units, rows, _ = held_ref.shape
    part = rows // MICRO
    experts = router_ref.shape[0]
    o_loads = lane_copies(order_ref, o_refs, heads_ref, o_sems)
    for copy in o_loads:
        copy.start()
    x_loads = load_blocks(x_refs, held_ref, x_sems, rows)
    for copy in o_loads:
        copy.wait()
    for copies in x_loads:
        for copy in copies:
            copy.wait()
    router = router_ref[...].astype(BF)
    for unit in range(units):
        spot = pl.ds(pl.multiple_of(order_ref[unit] * part, part), part)
        heads = jnp.concatenate([heads_ref[m, spot, :] for m in range(MICRO)], 0)
        x1 = held_ref[unit].astype(F32) + mm(heads, wo_ref[...])
        scale = lax.rsqrt(jnp.mean(x1 * x1, -1, keepdims=True) + EPSILON)
        h2 = (x1 * scale * gain_ref[...]).astype(BF)
        held_ref[unit] = h2
        if unit == 0:
            x1_ref[...] = x1
            h2_ref[...] = h2
            heads_own_ref[...] = heads
    stores = []
    for unit in range(units):
        h2 = held_ref[unit]
        hot = one_hot(rank_ref[unit], local, capacity).astype(BF)
        out_ref[unit] = mm(hot, h2).astype(BF)
        stores.append(pltpu.make_async_copy(out_ref.at[unit], xs_ref.at[unit], store_sems.at[unit]))
        stores[-1].start()
        logits = mm(router, h2, NT)
        chosen = chosen_rows(order_ref, routes_ref[unit], local, experts)
        masked = jnp.where(chosen > 0, logits, HIDDEN)
        raised = jnp.exp(masked - jnp.max(masked, 0, keepdims=True))
        raised = jnp.where(chosen > 0, raised, 0.0)
        gates = raised / jnp.sum(raised, 0, keepdims=True)
        rows_ref[unit] = gates[:8]
        if unit == 0:
            gates_ref[...] = gates
    for copy in stores:
        copy.wait()


def route(order, o_blocks, x_blocks, w_out, gain, router_t, routes, ranks, local, capacity):
    units, _, rows = ranks.shape
    experts, width = router_t.shape
    pieces = [flat(o_blocks), flat(x_blocks)]

    def sems(number):
        return pltpu.SemaphoreType.DMA((number,))

    return pl.pallas_call(
        functools.partial(
            route_kernel, local, capacity, counts_of(o_blocks), counts_of(x_blocks)
        ),
        in_specs=[SMEM] + [ANY] * (len(pieces[0]) + len(pieces[1])) + [VMEM] * 5,
        out_specs=[ANY] + [VMEM] * 5,
        out_shape=[
            jax.ShapeDtypeStruct((units, local * capacity, width), BF),
            jax.ShapeDtypeStruct((units, 8, rows), F32),
            jax.ShapeDtypeStruct((rows, width), F32),
            jax.ShapeDtypeStruct((rows, width), BF),
            jax.ShapeDtypeStruct((experts, rows), F32),
            jax.ShapeDtypeStruct((rows, width), BF),
        ],
        scratch_shapes=[
            pltpu.VMEM((MICRO, units * rows // MICRO, width), BF),
            pltpu.VMEM((units, rows, width), BF),
            pltpu.VMEM((units, local * capacity, width), BF),
            sems(len(pieces[0])),
            sems(len(pieces[1])),
            sems(units),
        ],
        compiler_params=params(56),
        cost_estimate=busy(12),
        name="route",
    )(order, *pieces[0], *pieces[1], w_out, gain, router_t, routes, ranks)


def expert_kernel(
    local, experts,
    order_ref, xs_ref, gs_ref, rank_ref, rows_ref, w_ref,
    ys_ref, dx_ref, dg_ref, da_ref, db_ref, hid_ref,
):
    expert = pl.program_id(0)
    units, _, capacity, width = xs_ref.shape
    total = units * capacity
    shards, _, _, block, hidden = w_ref.shape
    half = block // 2
    depth = shards * block
    xs = xs_ref[...].reshape(total, width)
    gs = gs_ref[...].reshape(total, width)
    mine = pl.ds(expert, 1)
    tokens = rank_ref.shape[2]
    slots = lax.broadcasted_iota(jnp.int32, (capacity, tokens), 0).astype(F32)
    gate = jnp.concatenate(
        [
            jnp.sum(jnp.where(rank_ref[u, mine, :] == slots, rows_ref[u, mine, :], 0.0), 1, keepdims=True)
            for u in range(units)
        ],
        0,
    )
    w_gate = w_ref[:, 0, 0].reshape(depth, hidden)
    w_up = w_ref[:, 0, 1].reshape(depth, hidden)
    w_down = jnp.concatenate(
        [w_ref[:, 0, 2, :half].reshape(hidden, hidden), w_ref[:, 0, 2, half:].reshape(hidden, hidden)], 1
    )
    a = mm(xs, w_gate)
    b = mm(xs, w_up)
    sigmoid = jax.nn.sigmoid(a)
    silu = a * sigmoid
    hid = (silu * b).astype(BF)
    y = mm(hid, w_down).astype(BF).astype(F32)
    ys_ref[...] = (gate * y).astype(BF).reshape(ys_ref.shape)
    back = mm(gs, w_down, NT)
    hid_full = hid.astype(F32)
    d_gate = jnp.sum(back * hid_full, -1, keepdims=True)
    d_hid = gate * back
    da = (d_hid * b * sigmoid * (1.0 + a * (1.0 - sigmoid))).astype(BF)
    db = (d_hid * silu).astype(BF)
    dx = mm(da, w_gate, NT) + mm(db, w_up, NT)
    dx_ref[...] = dx.astype(BF).reshape(dx_ref.shape)
    high = d_gate.astype(BF).astype(F32)
    rest = d_gate - high
    shape = (units, capacity, PAIR)
    spot = lanes(shape)
    source = lax.broadcasted_iota(jnp.int32, shape, 0)
    place = jnp.zeros(shape, jnp.int32)
    for unit in range(units):
        ahead = local * (order_ref[0] - order_ref[unit]) + expert + experts
        place = jnp.where(source == unit, lax.rem(ahead, experts), place)
    high = jnp.broadcast_to(high, (total, PAIR)).reshape(shape)
    rest = jnp.broadcast_to(rest, (total, PAIR)).reshape(shape)
    spread = jnp.where(spot == place, high, jnp.where(spot == place + experts, rest, 0.0))
    dg_ref[...] = spread.astype(BF).reshape(dg_ref.shape)
    da_ref[0] = da
    db_ref[0] = db
    hid_ref[0] = (hid_full * gate).astype(BF)


def run_experts(order, xs, gs, ranks, gate_rows, weights, experts):
    units, local, capacity, width = xs.shape
    index = pl.BlockSpec(ranks.shape, lambda e, s: (0, 0, 0))
    shards, _, kinds, block, hidden = weights.shape
    total = units * capacity
    rows = pl.BlockSpec((units, 1, capacity, width), lambda e, s: (0, e, 0, 0))
    narrow = pl.BlockSpec((units, 1, capacity, PAIR), lambda e, s: (0, e, 0, 0))
    wide = pl.BlockSpec((shards, 1, kinds, block, hidden), lambda e, s: (0, e, 0, 0, 0))
    inner = pl.BlockSpec((1, total, hidden), lambda e, s: (e, 0, 0))
    return pl.pallas_call(
        functools.partial(expert_kernel, local, experts),
        grid_spec=pltpu.PrefetchScalarGridSpec(
            num_scalar_prefetch=1,
            grid=(local,),
            in_specs=[rows, rows, index, index, wide],
            out_specs=[rows, rows, narrow, inner, inner, inner],
        ),
        out_shape=[
            jax.ShapeDtypeStruct(xs.shape, BF),
            jax.ShapeDtypeStruct(xs.shape, BF),
            jax.ShapeDtypeStruct((units, local, capacity, PAIR), BF),
            jax.ShapeDtypeStruct((local, total, hidden), BF),
            jax.ShapeDtypeStruct((local, total, hidden), BF),
            jax.ShapeDtypeStruct((local, total, hidden), BF),
        ],
        compiler_params=params(56),
        cost_estimate=busy(24),
        name="run_experts",
    )(order, xs, gs, ranks, gate_rows, weights)


def expert_weights_kernel(xs_ref, gs_ref, da_ref, db_ref, hid_ref, dw_ref):
    units, _, capacity, width = xs_ref.shape
    total = units * capacity
    shards, _, _, block, hidden = dw_ref.shape
    half = block // 2
    xs = xs_ref[...].reshape(total, width)
    gs = gs_ref[...].reshape(total, width)
    dw_ref[:, 0, 0] = mm(xs, da_ref[0], TN).astype(BF).reshape(shards, block, hidden)
    dw_ref[:, 0, 1] = mm(xs, db_ref[0], TN).astype(BF).reshape(shards, block, hidden)
    d_down_w = mm(hid_ref[0], gs, TN).astype(BF)
    dw_ref[:, 0, 2, :half] = d_down_w[:, :hidden].reshape(shards, half, hidden)
    dw_ref[:, 0, 2, half:] = d_down_w[:, hidden:].reshape(shards, half, hidden)


def expert_weights(xs, gs, da, db, hid, shape):
    units, local, capacity, width = xs.shape
    _, total, hidden = da.shape
    shards, _, kinds, block, _ = shape
    rows = pl.BlockSpec((units, 1, capacity, width), lambda e: (0, e, 0, 0))
    inner = pl.BlockSpec((1, total, hidden), lambda e: (e, 0, 0))
    return pl.pallas_call(
        expert_weights_kernel,
        grid=(local,),
        in_specs=[rows, rows, inner, inner, inner],
        out_specs=pl.BlockSpec((shards, 1, kinds, block, hidden), lambda e: (0, e, 0, 0, 0)),
        out_shape=jax.ShapeDtypeStruct(shape, BF),
        compiler_params=params(48),
        cost_estimate=busy(1),
        name="expert_weights",
    )(xs, gs, da, db, hid)


def combine_kernel(local, capacity, rank_ref, ys_ref, out_ref):
    hot = one_hot(rank_ref[0], local, capacity).astype(BF)
    slots = local * capacity
    out_ref[0] = mm(hot, ys_ref[0].reshape(slots, ys_ref.shape[-1]), TN).astype(BF)


def combine_narrow_kernel(local, capacity, rank_ref, ys_ref, dg_ref, out_ref):
    hot = one_hot(rank_ref[0], local, capacity).astype(BF)
    slots = local * capacity
    width = ys_ref.shape[-1]
    out_ref[0, :, :width] = mm(hot, ys_ref[0].reshape(slots, width), TN).astype(BF)
    out_ref[0, :, width:] = mm(hot, dg_ref[0].reshape(slots, PAIR), TN).astype(BF)


def combine(core, rank, ys, *dg):
    units, local, capacity, width = ys.shape
    rows = rank.shape[-1]
    count = units // 2
    out_width = width + PAIR * len(dg)

    def slots(last):
        return pl.BlockSpec((1, local, capacity, last), lambda u: (2 * u + core, 0, 0, 0))

    return pl.pallas_call(
        functools.partial(combine_narrow_kernel if dg else combine_kernel, local, capacity),
        grid=(count,),
        in_specs=[pl.BlockSpec((1, 8, rows), lambda u: (2 * u + core, 0, 0)), slots(width)]
        + [slots(PAIR)] * len(dg),
        out_specs=pl.BlockSpec((1, rows, out_width), lambda u: (u, 0, 0)),
        out_shape=jax.ShapeDtypeStruct((count, rows, out_width), BF),
        compiler_params=params(16),
        cost_estimate=busy(1),
        name="combine",
    )(rank, ys, *dg)


def own_kernel(count, *refs):
    grad_refs = refs[:count]
    (
        x1_ref, gates_ref, g_ref, router_ref, gain_ref, wo_ref,
        dx1_ref, do_ref, logit_ref, dgain_ref,
    ) = refs[count:]
    width = x1_ref.shape[1]
    experts = router_ref.shape[0]
    groups = do_ref.shape[0]
    grad = sum(r[...].astype(F32) for r in grad_refs)
    x1 = x1_ref[...]
    flat = grad[:, width:].T
    d_gate = flat[:experts] + flat[experts : 2 * experts]
    gates = gates_ref[...]
    d_logit = gates * (d_gate - jnp.sum(gates * d_gate, 0, keepdims=True))
    logit_ref[...] = d_logit
    high = d_logit.astype(BF)
    low = (d_logit - high.astype(F32)).astype(BF)
    router = router_ref[...]
    dh2 = grad[:, :width] + mm(
        jnp.concatenate([high, low], 0), jnp.concatenate([router, router], 0), TN
    )
    scale = lax.rsqrt(jnp.mean(x1 * x1, -1, keepdims=True) + EPSILON)
    normed = x1 * scale
    dgain_ref[...] = jnp.sum(dh2 * normed, 0, keepdims=True)
    dn = dh2 * gain_ref[...]
    dx1 = g_ref[...].astype(F32) + scale * (dn - normed * jnp.mean(dn * normed, -1, keepdims=True))
    dx1_ref[...] = dx1
    grad_o = mm(dx1.astype(BF), wo_ref[...], NT).astype(BF)
    for i in range(groups):
        do_ref[i] = grad_o[:, i * PAIR : (i + 1) * PAIR]


def own_tokens(grads, x1, gates, g, router_t, gain, w_out):
    rows, width = x1.shape
    groups = w_out.shape[0] // PAIR
    return pl.pallas_call(
        functools.partial(own_kernel, len(grads)),
        out_shape=[
            jax.ShapeDtypeStruct((rows, width), F32),
            jax.ShapeDtypeStruct((groups, rows, PAIR), BF),
            jax.ShapeDtypeStruct(gates.shape, F32),
            jax.ShapeDtypeStruct((1, width), F32),
        ],
        compiler_params=params(56),
        cost_estimate=busy(6),
        name="own_tokens",
    )(*grads, x1, gates, g, router_t, gain, w_out)


def own_weights_kernel(order_ref, dx1_ref, heads_ref, logit_ref, h2_ref, own_ref, other_ref, dr_ref, dwo_ref):
    groups = 2 * own_ref.shape[0]
    dwo_ref[...] = mm(heads_ref[...], dx1_ref[...].astype(BF), TN).astype(BF)
    for i in range(groups):
        spot = pl.multiple_of(order_ref[i] * PAIR, PAIR)
        target = other_ref if i % 2 else own_ref
        target[i // 2] = dwo_ref[:, pl.ds(spot, PAIR)]
    d_logit = logit_ref[...]
    high = d_logit.astype(BF)
    low = (d_logit - high.astype(F32)).astype(BF)
    both = mm(jnp.concatenate([high, low], 0), h2_ref[...])
    experts = d_logit.shape[0]
    dr_ref[...] = both[:experts] + both[experts:]


def own_weights(order, dx1, heads, logit, h2):
    rows, width = dx1.shape
    groups = order.shape[0]
    half = jax.ShapeDtypeStruct((groups // 2, groups * PAIR, PAIR), BF)
    return pl.pallas_call(
        own_weights_kernel,
        in_specs=[pl.BlockSpec(memory_space=pltpu.SMEM)]
        + [pl.BlockSpec(memory_space=pltpu.VMEM)] * 4,
        out_shape=[half, half, jax.ShapeDtypeStruct((logit.shape[0], width), F32)],
        scratch_shapes=[pltpu.VMEM((groups * PAIR, width), BF)],
        compiler_params=params(20),
        cost_estimate=busy(4),
        name="own_weights",
    )(order, dx1, heads, logit, h2)


def project_back_kernel(counts, units, order_ref, *refs):
    x_refs, refs = split_refs(refs, counts)
    gain_ref, dq_ref, dkv_ref, w_ref, dw_in_ref, dgain_in_ref = refs[:6]
    dw_ref, dh_ref, dgain_ref, held_ref, out_ref, load_sems, store_sems = refs[6:]
    rows = held_ref.shape[1]
    part = rows // MICRO
    loads = load_blocks(x_refs, held_ref, load_sems, rows)
    dw = dw_in_ref[...]
    dgain = dgain_in_ref[...]
    stores = []
    for i, unit in enumerate(units):
        spot = pl.ds(pl.multiple_of(order_ref[unit] * part, part), part)
        grads = jnp.concatenate(
            [
                jnp.concatenate([ref[m, spot, :] for m in range(MICRO)], 0)
                for ref in (dq_ref, dkv_ref)
            ],
            1,
        )
        dh = mm(grads, w_ref[...], NT)
        out_ref[i] = dh.astype(BF)
        stores.append(pltpu.make_async_copy(out_ref.at[i], dh_ref.at[i], store_sems.at[i]))
        stores[-1].start()
        for copy in loads[i]:
            copy.wait()
        x = held_ref[i].astype(F32)
        scale = lax.rsqrt(jnp.mean(x * x, -1, keepdims=True) + EPSILON)
        normed = x * scale
        dw = dw + mm(grads, (normed * gain_ref[...]).astype(BF), TN)
        dgain = dgain + jnp.sum(dh * normed, 0, keepdims=True)
    dw_ref[...] = dw
    dgain_ref[...] = dgain
    for copy in stores:
        copy.wait()


def project_back(core, order, x_blocks, rows, gain, dq, dkv, weight, dw, dgain):
    units = list(range(core, len(x_blocks), 2))
    blocks = [x_blocks[unit] for unit in units]
    parts = flat(blocks)
    width = weight.shape[0]
    count = len(units)
    return pl.pallas_call(
        functools.partial(project_back_kernel, counts_of(blocks), units),
        in_specs=[SMEM] + [ANY] * len(parts) + [VMEM] * 6,
        out_specs=[VMEM, ANY, VMEM],
        out_shape=[
            jax.ShapeDtypeStruct((2 * PAIR, width), F32),
            jax.ShapeDtypeStruct((count, rows, width), BF),
            jax.ShapeDtypeStruct((1, width), F32),
        ],
        scratch_shapes=[
            pltpu.VMEM((count, rows, width), BF),
            pltpu.VMEM((count, rows, width), BF),
            pltpu.SemaphoreType.DMA((len(parts),)),
            pltpu.SemaphoreType.DMA((count,)),
        ],
        compiler_params=params(16),
        cost_estimate=busy(4),
        name="project_back",
    )(
        order,
        *parts,
        gain,
        dq.reshape(MICRO, -1, PAIR),
        dkv.reshape(MICRO, -1, PAIR),
        weight,
        dw,
        dgain,
    )


def pack_kernel(local, order_ref, dw_ref, *refs):
    terms = refs[: len(refs) - 4]
    dr_ref, gain_one_ref, gain_two_ref, out_ref = refs[len(refs) - 4 :]
    experts, width = dr_ref.shape
    out_ref[:, : 2 * PAIR] = dw_ref[...].T.astype(BF)
    out_ref[:, 2 * PAIR : 3 * PAIR] = sum(r[...].astype(F32) for r in terms).astype(BF)
    router = pltpu.roll(dr_ref[...], local * order_ref[0], 0)
    rest = jnp.zeros((PAIR - experts - 16, width), F32)
    gains = [jnp.broadcast_to(r[...], (8, width)) for r in (gain_one_ref, gain_two_ref)]
    out_ref[:, 3 * PAIR :] = jnp.concatenate([router, *gains, rest], 0).T.astype(BF)


def pack_dense(order, local, dw, terms, d_router, gain_one, gain_two):
    width = dw.shape[1]
    vmem = pl.BlockSpec(memory_space=pltpu.VMEM)
    return pl.pallas_call(
        functools.partial(pack_kernel, local),
        in_specs=[pl.BlockSpec(memory_space=pltpu.SMEM)] + [vmem] * (len(terms) + 4),
        out_specs=vmem,
        out_shape=jax.ShapeDtypeStruct((width, 4 * PAIR), BF),
        compiler_params=params(14),
        cost_estimate=cost(1, 4 * width * 4 * PAIR),
        name="pack_dense",
    )(order, dw, *terms, d_router, gain_one, gain_two)


def add_up_kernel(pieces_ref, out_ref):
    total = pieces_ref[0].astype(F32)
    for i in range(1, pieces_ref.shape[0]):
        total = total + pieces_ref[i].astype(F32)
    out_ref[...] = total.astype(BF)


def add_up(pieces):
    return pl.pallas_call(
        add_up_kernel,
        out_shape=jax.ShapeDtypeStruct(pieces.shape[1:], BF),
        compiler_params=params(8),
        cost_estimate=cost(1, 2 * pieces.size),
        name="add_up",
    )(pieces)


def unpack_kernel(experts, pack_ref, q_ref, k_ref, v_ref, o_ref, router_ref, gain_one_ref, gain_two_ref):
    units = pack_ref.shape[0]
    total = jnp.zeros(pack_ref.shape[1:2] + (PAIR,), F32)
    for i in range(units):
        piece = pack_ref[i].astype(F32)
        q_ref[:, i * PAIR : (i + 1) * PAIR] = piece[:, :PAIR]
        o_ref[:, i * PAIR : (i + 1) * PAIR] = piece[:, 2 * PAIR : 3 * PAIR]
        total = total + piece[:, 3 * PAIR :]
    front = lanes(total.shape) < HEAD_DIM
    for i in range(0, units, 2):
        first = pack_ref[i, :, PAIR : 2 * PAIR].astype(F32)
        second = pack_ref[i + 1, :, PAIR : 2 * PAIR].astype(F32)
        spot = pl.ds(i * HEAD_DIM, PAIR)
        k_ref[:, spot] = jnp.where(front, first, pltpu.roll(second, HEAD_DIM, 1))
        v_ref[:, spot] = jnp.where(front, pltpu.roll(first, HEAD_DIM, 1), second)
    flat = total.T
    router_ref[...] = flat[:experts]
    gain_one_ref[...] = flat[experts : experts + 1]
    gain_two_ref[...] = flat[experts + 8 : experts + 9]


def unpack_dense(pack, experts):
    units, shard, _ = pack.shape
    return pl.pallas_call(
        functools.partial(unpack_kernel, experts),
        out_shape=[
            jax.ShapeDtypeStruct((shard, units * PAIR), F32),
            jax.ShapeDtypeStruct((shard, units * HEAD_DIM), F32),
            jax.ShapeDtypeStruct((shard, units * HEAD_DIM), F32),
            jax.ShapeDtypeStruct((shard, units * PAIR), F32),
            jax.ShapeDtypeStruct((experts, shard), F32),
            jax.ShapeDtypeStruct((1, shard), F32),
            jax.ShapeDtypeStruct((1, shard), F32),
        ],
        compiler_params=params(8),
        cost_estimate=cost(1, 4 * pack.size),
        name="unpack_dense",
    )(pack)


def open_kernel(local, pack_ref, gate_ref, up_ref, down_ref):
    shard, hidden = gate_ref.shape[1:]
    half = shard // 2
    for i in range(local):
        first = i * 3 * shard
        gate_ref[i] = pack_ref[first : first + shard, :].astype(F32)
        up_ref[i] = pack_ref[first + shard : first + 2 * shard, :].astype(F32)
        first = first + 2 * shard
        down_ref[i, :, :hidden] = pack_ref[first : first + half, :].astype(F32)
        down_ref[i, :, hidden:] = pack_ref[first + half : first + shard, :].astype(F32)


def open_experts(pack, local):
    hidden = pack.shape[1]
    shard = pack.shape[0] // (3 * local)
    return pl.pallas_call(
        functools.partial(open_kernel, local),
        out_shape=[
            jax.ShapeDtypeStruct((local, shard, hidden), F32),
            jax.ShapeDtypeStruct((local, shard, hidden), F32),
            jax.ShapeDtypeStruct((local, shard // 2, 2 * hidden), F32),
        ],
        compiler_params=params(12),
        cost_estimate=cost(1, 6 * pack.size),
        name="open_experts",
    )(pack)


def finish_kernel(x_ref, dx1_ref, gain_ref, *refs):
    out_ref = refs[-1]
    dh = sum(r[...].astype(F32) for r in refs[:-1])
    x = x_ref[...].astype(F32)
    scale = lax.rsqrt(jnp.mean(x * x, -1, keepdims=True) + EPSILON)
    normed = x * scale
    dn = dh * gain_ref[...]
    out_ref[...] = dx1_ref[...] + scale * (dn - normed * jnp.mean(dn * normed, -1, keepdims=True))


def finish(x, dx1, gain, terms):
    return pl.pallas_call(
        finish_kernel,
        out_shape=jax.ShapeDtypeStruct(dx1.shape, F32),
        compiler_params=params(16),
        cost_estimate=cost(1, 8 * dx1.size),
        name="finish",
    )(x, dx1, gain, *terms)


def swap_cores(block):
    units = lax.axis_size("ctx")
    return lax.ppermute(block, "ctx", [(i, i ^ 1) for i in range(units)])


def send_along(block, ahead):
    units = lax.axis_size("ctx")
    return lax.ppermute(block, "ctx", [(i, (i + 2 * ahead) % units) for i in range(units)])


def split_refs(refs, counts):
    found, first = [], 0
    for count in counts:
        found.append(refs[first : first + count])
        first = first + count
    return found, refs[first:]


def counts_of(blocks):
    return [len(parts) for parts in blocks]


def gather_near(block):
    return send_along(block, -1), send_along(block, 1)


def gather_far(near, cut):
    ahead, behind = near
    return send_along(behind[:cut], 1), send_along(ahead[cut:], -1)


def gather_chips(block):
    chips = lax.axis_size("ctx") // 2
    return [block] + [send_along(block, chips - ahead) for ahead in range(1, chips)]


def relative(block, near, far):
    return [(block,), near[:1], far, near[1:]]


def gather_cores(blocks):
    return [piece for parts in blocks for piece in (parts, tuple(swap_cores(part) for part in parts))]


def flat(blocks):
    return [part for parts in blocks for part in parts]


def scatter_cores(own, other):
    came = swap_cores(other)
    return [(a.astype(F32) + b.astype(F32)).astype(BF) for a, b in zip(own, came)]


def scatter_chips(sums):
    return [sums[0]] + [send_along(sums[i], i) for i in range(1, len(sums))]


def scatter_far(far, cut):
    return send_along(far[:cut], 1), send_along(far[cut:], -1)


def pass_on(sums, passed):
    front, back = passed
    cut = front.shape[0]
    ahead = sums[1].astype(F32).at[:cut].add(front.astype(F32)).astype(BF)
    behind = sums[3].astype(F32).at[cut:].add(back.astype(F32)).astype(BF)
    return [sums[0], ahead, behind]


def scatter_near(sums):
    own, ahead, behind = sums
    return [own, send_along(ahead, 1), send_along(behind, -1)]


def scatter_ctx(own, other):
    return scatter_chips(scatter_cores(own, other))


def per_device(
    tokens,
    routes,
    doc_starts,
    attn_gain,
    attn_q,
    attn_k,
    attn_v,
    attn_out,
    ffn_gain,
    router,
    w_gate,
    w_up,
    w_down,
    cotangent,
):
    part = tokens.shape[2]
    width = tokens.shape[3]
    top = routes.shape[3]
    experts = router.shape[1]
    local, shard, hidden = w_gate.shape
    units = lax.axis_size("ctx")
    shards = lax.axis_size("fsdp")
    rank = lax.axis_index("ctx").astype(jnp.int32)
    rows = MICRO * part
    length = units * rows
    capacity = MICRO * (5 * part * top // (4 * experts))
    places = jnp.arange(units, dtype=jnp.int32)
    order = (2 * (rank // 2 + places // 2) + ((rank ^ places) & 1)) % units
    find = (2 * (places // 2 - rank // 2) + ((rank ^ places) & 1)) % units

    x_own = tokens[0].reshape(rows, width)
    g_own = cotangent[0].reshape(rows, width)
    x_tall, dense, expert_pack = prepare(
        rank.reshape(1),
        x_own,
        routes[0].reshape(rows, top).T,
        doc_starts[0].reshape(1, rows),
        (attn_q, attn_k, attn_v, attn_out),
        (attn_gain.reshape(1, shard), ffn_gain.reshape(1, shard)),
        router.T,
        (w_gate, w_up, w_down),
    )
    weights = lax.all_gather(expert_pack, "fsdp", axis=0, tiled=True)
    weights = weights.reshape(shards, local, 3, shard, hidden)
    x_near = gather_chips(x_tall)
    dense = lax.all_gather(dense, "fsdp", axis=0, tiled=True)
    dense, x_near = together(dense, x_near)
    dense = dense.reshape(shards, -1, 3 * PAIR)
    x_blocks = gather_cores([(block,) for block in x_near])
    wo_part = dense[:, :shard, 2 * PAIR :].reshape(units, PAIR, PAIR)
    wo_part = wo_part.transpose(1, 0, 2).reshape(PAIR, width)
    g_wo = jnp.concatenate([g_own, wo_part], 0)
    g_wo, x_blocks = together(g_wo, x_blocks)
    g_near = gather_near(g_wo)

    tables = angle_tables(0, length // part, part) + angle_tables(0, part, 1)
    q, kv, route_rows, starts, w_qkv, gain_one, gain_two, router_t = project(
        order, x_blocks, top, dense, tables, experts
    )
    q = q.reshape(length, PAIR)
    kv = kv.reshape(length, PAIR)
    o, lse = attend(find, q, kv, starts)
    o = o.reshape(MICRO, length // MICRO, PAIR)
    o, g_near, g_wo = together(o, g_near, g_wo)
    o_chips = gather_chips(o)
    g_far = gather_far(g_near, (rows + PAIR) // 2)
    g_blocks = gather_cores(relative(g_wo, g_near, g_far))
    ranks, gs, w_out = pick(order, g_blocks, route_rows, local, capacity, experts)
    o_chips[2], ranks = together(o_chips[2], ranks)
    o_blocks = gather_cores([(block,) for block in o_chips])
    o = o.reshape(length, PAIR)
    router_t = jnp.roll(router_t, -local * rank, 0)
    xs, gate_rows, x1, h2, gates, heads = route(
        order, o_blocks, x_blocks, w_out, gain_two, router_t, route_rows, ranks, local, capacity
    )
    xs = xs.reshape(units, local, capacity, width)
    gs = gs.reshape(units, local, capacity, width)
    router_t = router_t.astype(BF)
    ys, dx, dg, da, db, hid = run_experts(order, xs, gs, ranks, gate_rows, weights, experts)
    grad_sums = scatter_cores(combine(0, ranks, dx, dg), combine(1, ranks, dx, dg))
    grad_sums, ys, da = together(grad_sums, ys, da)
    dw = expert_weights(xs, gs, da, db, hid, weights.shape)
    dw = dw.reshape(shards * local * 3 * shard, hidden)
    mix_sums = scatter_cores(combine(0, ranks, ys), combine(1, ranks, ys))
    grads, mix_sums, dw = together(scatter_chips(grad_sums), mix_sums, dw)
    dw = lax.psum_scatter(dw, "fsdp", scatter_dimension=0, tiled=True)
    mix_passed = scatter_far(mix_sums[2], part)
    dx1, grad_o, d_logit, d_gain_two = own_tokens(
        grads, x1, gates, g_own, router_t, gain_two, w_out
    )
    grad_o = lax.all_to_all(grad_o, "ctx", split_axis=0, concat_axis=0, tiled=True)
    grad_o = grad_o.reshape(units, MICRO, part, PAIR)
    dwo_own, dwo_other, d_router = own_weights(order, dx1, heads, d_logit, h2)
    dwo_sums = scatter_cores(dwo_own, dwo_other)
    mix_sums = pass_on(mix_sums, mix_passed)
    grad_o, dwo_sums, mix_sums = together(grad_o, dwo_sums, mix_sums)
    mixes = scatter_near(mix_sums)
    dwo_terms = scatter_chips(dwo_sums)
    dq, dkv = attend_back(find, q, kv, starts, lse, o, grad_o, tables)
    dq, dkv, mixes, dwo_terms = together(dq, dkv, mixes, dwo_terms)
    dw_qkv = jnp.zeros((2 * PAIR, width), F32)
    d_gain_one = jnp.zeros((1, width), F32)
    dw_qkv, dh_other, d_gain_one = project_back(
        1, order, x_blocks, rows, gain_one, dq, dkv, w_qkv, dw_qkv, d_gain_one
    )
    dw_qkv, dh_own, d_gain_one = project_back(
        0, order, x_blocks, rows, gain_one, dq, dkv, w_qkv, dw_qkv, d_gain_one
    )
    dh_terms = scatter_ctx(dh_own, dh_other)
    pack = pack_dense(order, local, dw_qkv, dwo_terms, d_router, d_gain_one, d_gain_two)
    pack = pack.reshape(shards, shard, -1)
    pack = lax.all_to_all(pack, "fsdp", split_axis=0, concat_axis=0, tiled=True)
    d_gate, d_up, d_down = open_experts(dw, local)
    mixed = (x1 + sum(term.astype(F32) for term in mixes)).astype(BF)
    pack, mixed, d_gate, d_up, d_down = together(pack, mixed, d_gate, d_up, d_down)
    pack = lax.all_gather(add_up(pack), "ctx", axis=0, tiled=False)
    pack, dh_terms = together(pack, dh_terms)
    d_tokens = finish(x_own, dx1, gain_one, dh_terms)
    d_q, d_k, d_v, d_out, d_router, d_gain_one, d_gain_two = unpack_dense(pack, experts)
    return (
        mixed.reshape(1, MICRO, part, width),
        d_tokens.reshape(1, MICRO, part, width),
        d_gain_one.reshape(shard),
        d_q,
        d_k,
        d_v,
        d_out,
        d_gain_two.reshape(shard),
        d_router.T,
        d_gate,
        d_up,
        d_down,
    )


def solution(mesh):
    return jax.shard_map(
        per_device,
        mesh=mesh,
        in_specs=(
            P("fsdp", None, "ctx", None),
            P("fsdp", None, "ctx", None),
            P("fsdp", None, "ctx"),
            P("fsdp"),
            P("fsdp", None),
            P("fsdp", None),
            P("fsdp", None),
            P("fsdp", None),
            P("fsdp"),
            P("fsdp", None),
            P("ctx", "fsdp", None),
            P("ctx", "fsdp", None),
            P("ctx", "fsdp", None),
            P("fsdp", None, "ctx", None),
        ),
        out_specs=(
            P("fsdp", None, "ctx", None),
            P("fsdp", None, "ctx", None),
            P("fsdp"),
            P("fsdp", None),
            P("fsdp", None),
            P("fsdp", None),
            P("fsdp", None),
            P("fsdp"),
            P("fsdp", None),
            P("ctx", "fsdp", None),
            P("ctx", "fsdp", None),
            P("ctx", "fsdp", None),
        ),
        check_vma=False,
    )
```

```python
import functools
import math

import jax
import jax.numpy as jnp
import numpy as np
from jax import lax
from jax.experimental import pallas as pl
from jax.experimental.pallas import tpu as pltpu
from jax.sharding import PartitionSpec as P

HEADS = 16
KV_HEADS = 8
HEAD_DIM = 64
MICRO = 2
EPSILON = 1e-06
HIDDEN = -1e30
BF = jnp.bfloat16
F32 = jnp.float32
HIGHEST = lax.Precision.HIGHEST
PAIR = 2 * HEAD_DIM
MEBI = 1024 * 1024

NN = (((1,), (0,)), ((), ()))
NT = (((1,), (1,)), ((), ()))
TN = (((0,), (0,)), ((), ()))


def mm(left, right, dims=NN, precision=None):
    return lax.dot_general(left, right, dims, preferred_element_type=F32, precision=precision)


def params(mebibytes):
    return pltpu.CompilerParams(vmem_limit_bytes=mebibytes * MEBI)


def cost(flops, moved):
    return pl.CostEstimate(flops=int(flops), bytes_accessed=int(moved), transcendentals=0)


def busy(microseconds):
    return pl.CostEstimate(flops=int(1.1e9 * microseconds), bytes_accessed=1, transcendentals=0)


LIGHT = pl.CostEstimate(flops=1, bytes_accessed=1, transcendentals=0)


def together(*values):
    return lax.optimization_barrier(values)


def lanes(shape):
    return lax.broadcasted_iota(jnp.int32, shape, len(shape) - 1)


def turn(values, cosine, sine):
    spot = lanes(values.shape) % HEAD_DIM
    swapped = jnp.where(
        spot < HEAD_DIM // 2,
        pltpu.roll(values, PAIR - HEAD_DIM // 2, 1),
        pltpu.roll(values, HEAD_DIM // 2, 1),
    )
    return values * cosine + swapped * sine


def angle_tables(first, count, step):
    half = HEAD_DIM // 2
    frequencies = 10000.0 ** (-2.0 * np.arange(half) / HEAD_DIM)
    turned = (first + step * np.arange(count))[:, None] * frequencies[None, :]
    return (
        jnp.asarray(np.concatenate([np.cos(turned)] * 4, -1), F32),
        jnp.asarray(np.concatenate([np.sin(turned)] * 4, -1), F32),
    )


def block_angles(tables, block):
    cos_a, sin_a, cos_b, sin_b = tables
    cos_a, sin_a = cos_a[pl.ds(block, 1), :], sin_a[pl.ds(block, 1), :]
    cos_b, sin_b = cos_b[...], sin_b[...]
    sine = sin_a * cos_b + cos_a * sin_b
    back = lanes(sine.shape) % HEAD_DIM >= HEAD_DIM // 2
    return cos_a * cos_b - sin_a * sin_b, jnp.where(back, sine, -sine)


VMEM = pl.BlockSpec(memory_space=pltpu.VMEM)
SMEM = pl.BlockSpec(memory_space=pltpu.SMEM)
ANY = pl.BlockSpec(memory_space=pl.ANY)


def prepare_kernel(
    rank_ref, x_ref, routes_ref, starts_ref, q_ref, k_ref, v_ref, o_ref, gain_one_ref, gain_two_ref,
    router_ref, gate_ref, up_ref, down_ref,
    tall_ref, dense_ref, pack_ref,
):
    rank = rank_ref[0]
    local, shard, hidden = gate_ref.shape
    half = shard // 2
    for i in range(local):
        first = 3 * shard * i
        pack_ref[first : first + shard, :] = gate_ref[i]
        pack_ref[first + shard : first + 2 * shard, :] = up_ref[i]
        first = first + 2 * shard
        pack_ref[first : first + half, :] = down_ref[i, :, :hidden]
        pack_ref[first + half : first + shard, :] = down_ref[i, :, hidden:]
    rows = x_ref.shape[0]
    tall_ref[:rows, :] = x_ref[...]
    routes = routes_ref[...].astype(F32)
    starts = starts_ref[...]
    high = (starts // HEAD_DIM).astype(F32)
    low = (starts % HEAD_DIM).astype(F32)
    none = jnp.zeros_like(high)
    index = [routes[i : i + 1] for i in range(routes.shape[0])] + [high, low, none, none]
    across = x_ref.shape[1] // rows
    index = [
        jnp.concatenate(index[i : i + across], 1) for i in range(0, len(index), across)
    ]
    spare = tall_ref.shape[0] - rows
    index.append(jnp.zeros((spare - len(index), x_ref.shape[1]), F32))
    tall_ref[rows:, :] = jnp.concatenate(index, 0).astype(BF)

    mine = pl.ds(pl.multiple_of(rank * PAIR, PAIR), PAIR)
    dense_ref[:shard, :PAIR] = q_ref[:, mine]
    dense_ref[:shard, 2 * PAIR :] = o_ref[:, mine]
    pair = pl.ds(pl.multiple_of(rank // 2 * PAIR, PAIR), PAIR)
    keys = k_ref[:, pair].astype(F32)
    values = v_ref[:, pair].astype(F32)
    odd = rank % 2 == 1
    keys = jnp.where(odd, pltpu.roll(keys, HEAD_DIM, 1), keys)
    values = jnp.where(odd, values, pltpu.roll(values, HEAD_DIM, 1))
    front = lanes(keys.shape) < HEAD_DIM
    dense_ref[:shard, PAIR : 2 * PAIR] = jnp.where(front, keys, values).astype(BF)
    router = router_ref[...].astype(F32)
    gains = jnp.concatenate(
        [gain_one_ref[...].astype(F32), gain_two_ref[...].astype(F32), jnp.zeros((6, shard), F32)], 0
    )
    groups = [router[i : i + 8] for i in range(0, router.shape[0], 8)]
    empty = jnp.zeros_like(gains)
    dense_ref[shard:, :] = jnp.concatenate([*groups, gains, empty], 1).astype(BF)


def prepare(rank, x, routes_t, starts, attn, gains, router_t, experts):
    rows, width = x.shape
    local, shard, hidden = experts[0].shape
    return pl.pallas_call(
        prepare_kernel,
        in_specs=[SMEM] + [VMEM] * 13,
        out_specs=[VMEM] * 3,
        out_shape=[
            jax.ShapeDtypeStruct((rows + 16, width), BF),
            jax.ShapeDtypeStruct((shard + 8, 3 * PAIR), BF),
            jax.ShapeDtypeStruct((local * 3 * shard, hidden), BF),
        ],
        compiler_params=params(56),
        cost_estimate=busy(3),
        name="prepare",
    )(rank, x, routes_t, starts, *attn, *gains, router_t, *experts)


def load_blocks(blocks, target, sems, rows):
    found, used = [], 0
    for i, parts in enumerate(blocks):
        copies, first = [], 0
        for part in parts:
            count = min(part.shape[0], rows - first)
            copies.append(
                pltpu.make_async_copy(
                    part.at[pl.ds(0, count)], target.at[i, pl.ds(first, count)], sems.at[used]
                )
            )
            first, used = first + count, used + 1
        for copy in copies:
            copy.start()
        found.append(copies)
    return found


def project_kernel(counts, top, order_ref, *refs):
    x_refs, refs = split_refs(refs, counts)
    (
        dense_ref, cos_a_ref, sin_a_ref, cos_b_ref, sin_b_ref,
        q_ref, kv_ref, routes_ref, starts_ref, w_ref, gain_one_ref, gain_two_ref, router_ref,
        held_ref, sems,
    ) = refs
    tables = (cos_a_ref, sin_a_ref, cos_b_ref, sin_b_ref)
    tall, width = held_ref.shape[1:]
    units = len(counts)
    part = q_ref.shape[1] // units
    rows = MICRO * part
    shards = dense_ref.shape[0]
    shard = width // shards
    loads = load_blocks(x_refs, held_ref, sems, tall)
    w_ref[...] = dense_ref[:, :shard, : 2 * PAIR].reshape(width, 2 * PAIR)
    for i in range(0, shards, 2):
        small = [dense_ref[i + j, shard:, :].astype(F32) for j in range(2)]
        spot = pl.ds(i * shard, PAIR)
        front = lanes((8, PAIR)) < HEAD_DIM
        for group in range(5):
            lane = group // 2 * PAIR
            pair = [piece[:, lane : lane + PAIR] for piece in small]
            if group % 2 == 0:
                both = jnp.where(front, pair[0], pltpu.roll(pair[1], HEAD_DIM, 1))
            else:
                both = jnp.where(front, pltpu.roll(pair[0], HEAD_DIM, 1), pair[1])
            if group < 4:
                router_ref[group * 8 : group * 8 + 8, spot] = both
            else:
                gain_one_ref[:, spot] = both[0:1]
                gain_two_ref[:, spot] = both[1:2]
    gain = gain_one_ref[...]
    for unit in range(units):
        for copy in loads[unit]:
            copy.wait()
        x = held_ref[unit, :rows, :].astype(F32)
        scale = lax.rsqrt(jnp.mean(x * x, -1, keepdims=True) + EPSILON)
        lin = mm((x * scale * gain).astype(BF), w_ref[...])
        place = order_ref[unit]
        for m in range(MICRO):
            cosine, sine = block_angles(tables, m * units + place)
            here = lin[m * part : (m + 1) * part]
            spot = pl.ds(pl.multiple_of(place * part, part), part)
            q = turn(here[:, :PAIR], cosine, sine).astype(BF).astype(F32)
            q_ref[m, spot, :] = (q * (1.0 / math.sqrt(HEAD_DIM))).astype(BF)
            kv = here[:, PAIR:]
            kv = jnp.where(lanes(kv.shape) < HEAD_DIM, turn(kv, cosine, sine), kv)
            kv_ref[m, spot, :] = kv.astype(BF)
        index = held_ref[unit, rows:, :].astype(F32)
        across = width // rows

        def number(i, index=index, across=across):
            first = (i % across) * rows
            return index[i // across : i // across + 1, first : first + rows]

        routes_ref[unit] = jnp.concatenate([number(k) for k in range(top)], 0)
        starts = number(top) * HEAD_DIM + number(top + 1)
        starts_ref[unit] = jnp.broadcast_to(starts, starts_ref.shape[1:])


def project(order, x_blocks, top, dense, tables, experts):
    units = len(x_blocks)
    tall, width = x_blocks[0][0].shape
    part = tables[2].shape[0]
    parts = flat(x_blocks)
    index = jax.ShapeDtypeStruct((units, 8, MICRO * part), F32)
    return pl.pallas_call(
        functools.partial(project_kernel, counts_of(x_blocks), top),
        in_specs=[SMEM] + [ANY] * len(parts) + [VMEM] * 5,
        out_specs=[VMEM] * 8,
        out_shape=[
            jax.ShapeDtypeStruct((MICRO, units * part, PAIR), BF),
            jax.ShapeDtypeStruct((MICRO, units * part, PAIR), BF),
            index,
            index,
            jax.ShapeDtypeStruct((width, 2 * PAIR), BF),
            jax.ShapeDtypeStruct((1, width), F32),
            jax.ShapeDtypeStruct((1, width), F32),
            jax.ShapeDtypeStruct((experts, width), F32),
        ],
        scratch_shapes=[
            pltpu.VMEM((units, tall, width), BF),
            pltpu.SemaphoreType.DMA((len(parts),)),
        ],
        compiler_params=params(48),
        cost_estimate=busy(8),
        name="project",
    )(order, *parts, dense, *tables)


def front_heads(pair):
    pair = pair.astype(F32)
    front = lanes(pair.shape) < HEAD_DIM
    return jnp.concatenate(
        [jnp.where(front, pair, 0.0), jnp.where(front, pltpu.roll(pair, HEAD_DIM, 1), 0.0)], 0
    ).astype(BF)


def back_heads(pair):
    pair = pair.astype(F32)
    back = lanes(pair.shape) >= HEAD_DIM
    return jnp.concatenate(
        [jnp.where(back, pltpu.roll(pair, HEAD_DIM, 1), 0.0), jnp.where(back, pair, 0.0)], 0
    ).astype(BF)


def tile_starts(find_ref, start_ref, tile, rows):
    units, _, both = start_ref.shape
    part = both // MICRO
    span = rows // part
    half = units // span
    spot = pl.ds(pl.multiple_of(lax.div(tile, half) * part, part), part)
    pieces = [start_ref[find_ref[lax.rem(tile, half) * span + i], 0:1, spot] for i in range(span)]
    return jnp.concatenate(pieces + pieces, -1)


def attend_kernel(find_ref, q_ref, kv_ref, start_ref, o_ref, lse_ref, s_ref, kvt_ref, p_ref):
    tile = pl.program_id(0)
    rows = q_ref.shape[0]
    tiles = kv_ref.shape[0]

    @pl.when(tile == 0)
    def _():
        for chunk in range(tiles):
            kvt_ref[:, chunk * rows : (chunk + 1) * rows] = kv_ref[chunk].astype(F32).T.astype(BF)

    queries = front_heads(q_ref[...])
    start = tile_starts(find_ref, start_ref, tile, rows).astype(jnp.int32)
    key_row = lax.broadcasted_iota(jnp.int32, (rows, 2 * rows), 0)
    query_row = lanes((rows, 2 * rows)) % rows

    def fold(values, how):
        return how(values.reshape(rows // 8, 8, 2 * rows), axis=0)

    def one_tile(last):
        top = None
        for chunk in range(last + 1):
            seen = key_row >= start - chunk * rows
            if chunk == last:
                seen = seen & (key_row <= query_row)
            found = jnp.where(seen, mm(kv_ref[chunk], queries, NT), HIDDEN)
            s_ref[chunk] = found
            here = fold(found, jnp.max)
            top = here if top is None else jnp.maximum(top, here)
        top = jnp.max(top, axis=0, keepdims=True)
        total = jnp.zeros((8, 2 * rows), F32)
        for chunk in range(last + 1):
            raised = jnp.exp(s_ref[chunk] - top)
            p_ref[chunk * rows : (chunk + 1) * rows, :] = raised.astype(BF)
            total = total + fold(raised, jnp.sum)
        total = jnp.sum(total, axis=0, keepdims=True)
        depth = (last + 1) * rows
        out = mm(kvt_ref[:, :depth], p_ref[:depth, :])[HEAD_DIM:, :] * (1.0 / total)
        out = jnp.concatenate([out[:, :rows], out[:, rows:]], 0)
        o_ref[...] = out.T.astype(BF)
        lse_ref[0] = top + jnp.log(total)

    for last in range(tiles):
        pl.when(tile == last)(functools.partial(one_tile, last))


def attend(find, q, kv, starts, rows=256):
    length = q.shape[0]
    tiles = length // rows
    return pl.pallas_call(
        attend_kernel,
        grid_spec=pltpu.PrefetchScalarGridSpec(
            num_scalar_prefetch=1,
            grid=(tiles,),
            in_specs=[
                pl.BlockSpec((rows, PAIR), lambda t, s: (t, 0)),
                pl.BlockSpec((tiles, rows, PAIR), lambda t, s: (0, 0, 0)),
                pl.BlockSpec(starts.shape, lambda t, s: (0, 0, 0)),
            ],
            out_specs=[
                pl.BlockSpec((rows, PAIR), lambda t, s: (t, 0)),
                pl.BlockSpec((1, 1, 2 * rows), lambda t, s: (t, 0, 0)),
            ],
            scratch_shapes=[
                pltpu.VMEM((tiles, rows, 2 * rows), F32),
                pltpu.VMEM((PAIR, length), BF),
                pltpu.VMEM((length, 2 * rows), BF),
            ],
        ),
        out_shape=[
            jax.ShapeDtypeStruct((length, PAIR), BF),
            jax.ShapeDtypeStruct((tiles, 1, 2 * rows), F32),
        ],
        compiler_params=params(14),
        cost_estimate=busy(20),
        name="attend",
    )(find, q, kv.reshape(tiles, rows, PAIR), starts)


def attend_back_kernel(
    find_ref, q_ref, kv_ref, start_ref, lse_ref, o_ref, do_ref, cos_a_ref, sin_a_ref, cos_b_ref, sin_b_ref,
    dq_ref, dkv_ref, kvt_ref, dkv_acc, ds_ref, dqt_ref,
):
    tile = pl.program_id(0)
    rows = q_ref.shape[0]
    chunks = kv_ref.shape[0]

    @pl.when(tile == 0)
    def _():
        dkv_acc[...] = jnp.zeros_like(dkv_acc)
        for chunk in range(chunks):
            kvt_ref[:, chunk * rows : (chunk + 1) * rows] = kv_ref[chunk].astype(F32).T.astype(BF)

    grad_o = do_ref[...].reshape(rows, PAIR)
    queries = front_heads(q_ref[...])
    grads = back_heads(grad_o)
    product = grad_o.astype(F32) * o_ref[...].astype(F32)
    half = lax.broadcasted_iota(jnp.int32, (8, PAIR), 0)
    picked = (lanes((8, PAIR)) // HEAD_DIM == half).astype(F32)
    sums = mm(picked, product, NT, HIGHEST)
    delta = jnp.concatenate([sums[0:1], sums[1:2]], -1)
    start = tile_starts(find_ref, start_ref, tile, rows).astype(jnp.int32)
    lse = lse_ref[0]
    key_row = lax.broadcasted_iota(jnp.int32, (rows, 2 * rows), 0)
    query_row = lanes((rows, 2 * rows)) % rows

    def one_tile(last):
        for chunk in range(last + 1):
            keys = kv_ref[chunk]
            seen = key_row >= start - chunk * rows
            if chunk == last:
                seen = seen & (key_row <= query_row)
            found = jnp.where(seen, mm(keys, queries, NT), HIDDEN)
            prob = jnp.exp(found - lse)
            grad_s = (prob * (mm(keys, grads, NT) - delta)).astype(BF)
            ds_ref[chunk * rows : (chunk + 1) * rows, :] = grad_s
            dkv_acc[chunk] += mm(grad_s, queries) + mm(prob.astype(BF), grads)
        depth = (last + 1) * rows
        dqt_ref[...] = mm(kvt_ref[:, :depth], ds_ref[:depth, :])[:HEAD_DIM]

    for last in range(chunks):
        pl.when(tile == last)(functools.partial(one_tile, last))

    dq = dqt_ref[...] * (1.0 / math.sqrt(HEAD_DIM))
    dq = jnp.concatenate([dq[:, :rows], dq[:, rows:]], 0).T
    tables = (cos_a_ref, sin_a_ref, cos_b_ref, sin_b_ref)
    part = cos_b_ref.shape[0]

    def turn_back(values, first):
        pieces = []
        for i in range(rows // part):
            cosine, sine = block_angles(tables, first + i)
            pieces.append(turn(values[i * part : (i + 1) * part], cosine, -sine))
        return jnp.concatenate(pieces, 0)

    dq_ref[...] = turn_back(dq, tile * (rows // part)).astype(BF)

    @pl.when(tile == chunks - 1)
    def _():
        for chunk in range(chunks):
            flat = dkv_acc[chunk]
            spot = pl.ds(chunk * rows, rows)
            turned = turn_back(flat, chunk * (rows // part))
            dkv_ref[spot, :] = jnp.where(lanes(flat.shape) < HEAD_DIM, turned, flat).astype(BF)


def attend_back(find, q, kv, starts, lse, o, grad_o, tables, rows=256):
    length = q.shape[0]
    tiles = length // rows
    units, _, part, _ = grad_o.shape
    span = rows // part
    half = tiles // MICRO
    whole = pl.BlockSpec((length, PAIR), lambda t, s: (0, 0))
    return pl.pallas_call(
        attend_back_kernel,
        grid_spec=pltpu.PrefetchScalarGridSpec(
            num_scalar_prefetch=1,
            grid=(tiles,),
            in_specs=[
                pl.BlockSpec((rows, PAIR), lambda t, s: (t, 0)),
                pl.BlockSpec((tiles, rows, PAIR), lambda t, s: (0, 0, 0)),
                pl.BlockSpec(starts.shape, lambda t, s: (0, 0, 0)),
                pl.BlockSpec((1, 1, 2 * rows), lambda t, s: (t, 0, 0)),
                pl.BlockSpec((rows, PAIR), lambda t, s: (t, 0)),
                pl.BlockSpec((span, 1, part, PAIR), lambda t, s: (t % half, t // half, 0, 0)),
            ]
            + [pl.BlockSpec(table.shape, lambda t, s: (0, 0)) for table in tables],
            out_specs=[pl.BlockSpec((rows, PAIR), lambda t, s: (t, 0)), whole],
            scratch_shapes=[
                pltpu.VMEM((PAIR, length), BF),
                pltpu.VMEM((tiles, rows, PAIR), F32),
                pltpu.VMEM((length, 2 * rows), BF),
                pltpu.VMEM((HEAD_DIM, 2 * rows), F32),
            ],
        ),
        out_shape=[
            jax.ShapeDtypeStruct((length, PAIR), BF),
            jax.ShapeDtypeStruct((length, PAIR), BF),
        ],
        compiler_params=params(56),
        cost_estimate=busy(26),
        name="attend_back",
    )(find, q, kv.reshape(tiles, rows, PAIR), starts, lse, o, grad_o, *tables)


def one_hot(rank_rows, local, capacity):
    slots = lax.broadcasted_iota(jnp.int32, (capacity, rank_rows.shape[1]), 0).astype(F32)
    return jnp.concatenate([(rank_rows[e : e + 1] == slots).astype(F32) for e in range(local)], 0)


def gather_lanes(order_ref, blocks, out_ref):
    for i, refs in enumerate(blocks):
        spot = pl.multiple_of(order_ref[i] * PAIR, PAIR)
        first = 0
        for ref in refs:
            part = ref[...].reshape(-1, PAIR)
            last = first + part.shape[0]
            out_ref[first:last, pl.ds(spot, PAIR)] = part
            first = last


def chosen_rows(order_ref, routes, local, experts):
    rows = routes.shape[1]
    routes = routes.astype(jnp.int32) - local * order_ref[0]
    routes = jnp.where(routes < 0, routes + experts, routes)
    ids = lax.broadcasted_iota(jnp.int32, (experts, rows), 0)
    chosen = jnp.zeros((experts, rows), F32)
    for k in range(routes.shape[0]):
        chosen = chosen + (ids == routes[k : k + 1, :]).astype(F32)
    return chosen


def pick_kernel(local, capacity, experts, counts, order_ref, *refs):
    g_refs, refs = split_refs(refs, counts)
    routes_ref, rank_ref, gs_ref, wo_ref, held_ref, out_ref, load_sems, store_sems = refs
    units, tall, width = held_ref.shape
    rows = tall - PAIR
    loads = load_blocks(g_refs, held_ref, load_sems, tall)
    before = lax.broadcasted_iota(jnp.int32, (rows, rows), 0) < lanes((rows, rows))
    before = before.astype(F32).astype(BF)
    stores = []
    for unit in range(units):
        chosen = chosen_rows(order_ref, routes_ref[unit], local, experts)[:8]
        rank = jnp.where(chosen > 0, mm(chosen.astype(BF), before), -1.0)
        rank_ref[unit] = rank
        hot = one_hot(rank, local, capacity).astype(BF)
        for copy in loads[unit]:
            copy.wait()
        out_ref[unit] = mm(hot, held_ref[unit, :rows, :]).astype(BF)
        stores.append(pltpu.make_async_copy(out_ref.at[unit], gs_ref.at[unit], store_sems.at[unit]))
        stores[-1].start()
        spot = pl.ds(pl.multiple_of(order_ref[unit] * PAIR, PAIR), PAIR)
        for i in range(width // PAIR):
            here = slice(i * PAIR, (i + 1) * PAIR)
            wo_ref[here, spot] = held_ref[unit, rows:, here]
    for copy in stores:
        copy.wait()


def pick(order, g_blocks, routes, local, capacity, experts):
    units = len(g_blocks)
    tall, width = g_blocks[0][0].shape
    rows = routes.shape[-1]
    parts = flat(g_blocks)
    return pl.pallas_call(
        functools.partial(pick_kernel, local, capacity, experts, counts_of(g_blocks)),
        in_specs=[SMEM] + [ANY] * len(parts) + [VMEM],
        out_specs=[VMEM, ANY, VMEM],
        out_shape=[
            jax.ShapeDtypeStruct((units, 8, rows), F32),
            jax.ShapeDtypeStruct((units, local * capacity, width), BF),
            jax.ShapeDtypeStruct((units * PAIR, width), BF),
        ],
        scratch_shapes=[
            pltpu.VMEM((units, tall, width), BF),
            pltpu.VMEM((units, local * capacity, width), BF),
            pltpu.SemaphoreType.DMA((len(parts),)),
            pltpu.SemaphoreType.DMA((units,)),
        ],
        compiler_params=params(56),
        cost_estimate=busy(1),
        name="pick",
    )(order, *parts, routes)


def lane_copies(order_ref, blocks, target, sems):
    copies = []
    for i, parts in enumerate(blocks):
        spot = pl.ds(pl.multiple_of(order_ref[i] * PAIR, PAIR), PAIR)
        first = 0
        for part in parts:
            count = part.shape[0]
            place = target.at[(pl.ds(first, count),) + (slice(None),) * (len(part.shape) - 2) + (spot,)]
            copies.append(pltpu.make_async_copy(part, place, sems.at[len(copies)]))
            first = first + count
    return copies


def route_kernel(local, capacity, o_counts, x_counts, order_ref, *refs):
    o_refs, refs = split_refs(refs, o_counts)
    x_refs, refs = split_refs(refs, x_counts)
    (
        wo_ref, gain_ref, router_ref, routes_ref, rank_ref,
        xs_ref, rows_ref, x1_ref, h2_ref, gates_ref, heads_own_ref,
        heads_ref, held_ref, out_ref, o_sems, x_sems, store_sems,
    ) = refs
    units, rows, _ = held_ref.shape
    part = rows // MICRO
    experts = router_ref.shape[0]
    o_loads = lane_copies(order_ref, o_refs, heads_ref, o_sems)
    for copy in o_loads:
        copy.start()
    x_loads = load_blocks(x_refs, held_ref, x_sems, rows)
    for copy in o_loads:
        copy.wait()
    for copies in x_loads:
        for copy in copies:
            copy.wait()
    router = router_ref[...].astype(BF)
    for unit in range(units):
        spot = pl.ds(pl.multiple_of(order_ref[unit] * part, part), part)
        heads = jnp.concatenate([heads_ref[m, spot, :] for m in range(MICRO)], 0)
        x1 = held_ref[unit].astype(F32) + mm(heads, wo_ref[...])
        scale = lax.rsqrt(jnp.mean(x1 * x1, -1, keepdims=True) + EPSILON)
        h2 = (x1 * scale * gain_ref[...]).astype(BF)
        held_ref[unit] = h2
        if unit == 0:
            x1_ref[...] = x1
            h2_ref[...] = h2
            heads_own_ref[...] = heads
    stores = []
    for unit in range(units):
        h2 = held_ref[unit]
        hot = one_hot(rank_ref[unit], local, capacity).astype(BF)
        out_ref[unit] = mm(hot, h2).astype(BF)
        stores.append(pltpu.make_async_copy(out_ref.at[unit], xs_ref.at[unit], store_sems.at[unit]))
        stores[-1].start()
        logits = mm(router, h2, NT)
        chosen = chosen_rows(order_ref, routes_ref[unit], local, experts)
        masked = jnp.where(chosen > 0, logits, HIDDEN)
        raised = jnp.exp(masked - jnp.max(masked, 0, keepdims=True))
        raised = jnp.where(chosen > 0, raised, 0.0)
        gates = raised / jnp.sum(raised, 0, keepdims=True)
        rows_ref[unit] = gates[:8]
        if unit == 0:
            gates_ref[...] = gates
    for copy in stores:
        copy.wait()


def route(order, o_blocks, x_blocks, w_out, gain, router_t, routes, ranks, local, capacity):
    units, _, rows = ranks.shape
    experts, width = router_t.shape
    pieces = [flat(o_blocks), flat(x_blocks)]

    def sems(number):
        return pltpu.SemaphoreType.DMA((number,))

    return pl.pallas_call(
        functools.partial(
            route_kernel, local, capacity, counts_of(o_blocks), counts_of(x_blocks)
        ),
        in_specs=[SMEM] + [ANY] * (len(pieces[0]) + len(pieces[1])) + [VMEM] * 5,
        out_specs=[ANY] + [VMEM] * 5,
        out_shape=[
            jax.ShapeDtypeStruct((units, local * capacity, width), BF),
            jax.ShapeDtypeStruct((units, 8, rows), F32),
            jax.ShapeDtypeStruct((rows, width), F32),
            jax.ShapeDtypeStruct((rows, width), BF),
            jax.ShapeDtypeStruct((experts, rows), F32),
            jax.ShapeDtypeStruct((rows, width), BF),
        ],
        scratch_shapes=[
            pltpu.VMEM((MICRO, units * rows // MICRO, width), BF),
            pltpu.VMEM((units, rows, width), BF),
            pltpu.VMEM((units, local * capacity, width), BF),
            sems(len(pieces[0])),
            sems(len(pieces[1])),
            sems(units),
        ],
        compiler_params=params(56),
        cost_estimate=busy(12),
        name="route",
    )(order, *pieces[0], *pieces[1], w_out, gain, router_t, routes, ranks)


def expert_kernel(
    local, experts,
    order_ref, xs_ref, gs_ref, rank_ref, rows_ref, w_ref,
    ys_ref, dx_ref, dg_ref, dw_ref,
):
    expert = pl.program_id(0)
    units, _, capacity, width = xs_ref.shape
    total = units * capacity
    shards, _, _, block, hidden = w_ref.shape
    half = block // 2
    depth = shards * block
    xs = xs_ref[...].reshape(total, width)
    gs = gs_ref[...].reshape(total, width)
    mine = pl.ds(expert, 1)
    tokens = rank_ref.shape[2]
    slots = lax.broadcasted_iota(jnp.int32, (capacity, tokens), 0).astype(F32)
    gate = jnp.concatenate(
        [
            jnp.sum(jnp.where(rank_ref[u, mine, :] == slots, rows_ref[u, mine, :], 0.0), 1, keepdims=True)
            for u in range(units)
        ],
        0,
    )
    w_gate = w_ref[:, 0, 0].reshape(depth, hidden)
    w_up = w_ref[:, 0, 1].reshape(depth, hidden)
    w_down = jnp.concatenate(
        [w_ref[:, 0, 2, :half].reshape(hidden, hidden), w_ref[:, 0, 2, half:].reshape(hidden, hidden)], 1
    )
    a = mm(xs, w_gate)
    b = mm(xs, w_up)
    sigmoid = jax.nn.sigmoid(a)
    silu = a * sigmoid
    hid = (silu * b).astype(BF)
    y = mm(hid, w_down).astype(BF).astype(F32)
    ys_ref[...] = (gate * y).astype(BF).reshape(ys_ref.shape)
    back = mm(gs, w_down, NT)
    hid_full = hid.astype(F32)
    d_gate = jnp.sum(back * hid_full, -1, keepdims=True)
    d_hid = gate * back
    da = (d_hid * b * sigmoid * (1.0 + a * (1.0 - sigmoid))).astype(BF)
    db = (d_hid * silu).astype(BF)
    dx = mm(da, w_gate, NT) + mm(db, w_up, NT)
    dx_ref[...] = dx.astype(BF).reshape(dx_ref.shape)
    high = d_gate.astype(BF).astype(F32)
    rest = d_gate - high
    shape = (units, capacity, PAIR)
    spot = lanes(shape)
    source = lax.broadcasted_iota(jnp.int32, shape, 0)
    place = jnp.zeros(shape, jnp.int32)
    for unit in range(units):
        ahead = local * (order_ref[0] - order_ref[unit]) + expert + experts
        place = jnp.where(source == unit, lax.rem(ahead, experts), place)
    high = jnp.broadcast_to(high, (total, PAIR)).reshape(shape)
    rest = jnp.broadcast_to(rest, (total, PAIR)).reshape(shape)
    spread = jnp.where(spot == place, high, jnp.where(spot == place + experts, rest, 0.0))
    dg_ref[...] = spread.astype(BF).reshape(dg_ref.shape)
    d_gate_w = mm(xs, da, TN).astype(BF)
    dw_ref[:, 0, 0] = d_gate_w.reshape(shards, block, hidden)
    d_up_w = mm(xs, db, TN).astype(BF)
    dw_ref[:, 0, 1] = d_up_w.reshape(shards, block, hidden)
    scaled = (hid_full * gate).astype(BF)
    d_down_w = mm(scaled, gs, TN).astype(BF)
    dw_ref[:, 0, 2, :half] = d_down_w[:, :hidden].reshape(shards, half, hidden)
    dw_ref[:, 0, 2, half:] = d_down_w[:, hidden:].reshape(shards, half, hidden)


def run_experts(order, xs, gs, ranks, gate_rows, weights, experts):
    units, local, capacity, width = xs.shape
    index = pl.BlockSpec(ranks.shape, lambda e, s: (0, 0, 0))
    shards, _, kinds, block, hidden = weights.shape
    rows = pl.BlockSpec((units, 1, capacity, width), lambda e, s: (0, e, 0, 0))
    narrow = pl.BlockSpec((units, 1, capacity, PAIR), lambda e, s: (0, e, 0, 0))
    wide = pl.BlockSpec((shards, 1, kinds, block, hidden), lambda e, s: (0, e, 0, 0, 0))
    return pl.pallas_call(
        functools.partial(expert_kernel, local, experts),
        grid_spec=pltpu.PrefetchScalarGridSpec(
            num_scalar_prefetch=1,
            grid=(local,),
            in_specs=[rows, rows, index, index, wide],
            out_specs=[rows, rows, narrow, wide],
        ),
        out_shape=[
            jax.ShapeDtypeStruct(xs.shape, BF),
            jax.ShapeDtypeStruct(xs.shape, BF),
            jax.ShapeDtypeStruct((units, local, capacity, PAIR), BF),
            jax.ShapeDtypeStruct(weights.shape, BF),
        ],
        compiler_params=params(56),
        cost_estimate=busy(34),
        name="run_experts",
    )(order, xs, gs, ranks, gate_rows, weights)


def combine_kernel(local, capacity, rank_ref, ys_ref, out_ref):
    hot = one_hot(rank_ref[0], local, capacity).astype(BF)
    slots = local * capacity
    out_ref[0] = mm(hot, ys_ref[0].reshape(slots, ys_ref.shape[-1]), TN).astype(BF)


def combine_narrow_kernel(local, capacity, rank_ref, ys_ref, dg_ref, out_ref):
    hot = one_hot(rank_ref[0], local, capacity).astype(BF)
    slots = local * capacity
    width = ys_ref.shape[-1]
    out_ref[0, :, :width] = mm(hot, ys_ref[0].reshape(slots, width), TN).astype(BF)
    out_ref[0, :, width:] = mm(hot, dg_ref[0].reshape(slots, PAIR), TN).astype(BF)


def combine(core, rank, ys, *dg):
    units, local, capacity, width = ys.shape
    rows = rank.shape[-1]
    count = units // 2
    out_width = width + PAIR * len(dg)

    def slots(last):
        return pl.BlockSpec((1, local, capacity, last), lambda u: (2 * u + core, 0, 0, 0))

    return pl.pallas_call(
        functools.partial(combine_narrow_kernel if dg else combine_kernel, local, capacity),
        grid=(count,),
        in_specs=[pl.BlockSpec((1, 8, rows), lambda u: (2 * u + core, 0, 0)), slots(width)]
        + [slots(PAIR)] * len(dg),
        out_specs=pl.BlockSpec((1, rows, out_width), lambda u: (u, 0, 0)),
        out_shape=jax.ShapeDtypeStruct((count, rows, out_width), BF),
        compiler_params=params(16),
        cost_estimate=busy(1),
        name="combine",
    )(rank, ys, *dg)


def own_kernel(count, *refs):
    grad_refs = refs[:count]
    (
        x1_ref, gates_ref, g_ref, router_ref, gain_ref, wo_ref,
        dx1_ref, do_ref, logit_ref, dgain_ref,
    ) = refs[count:]
    width = x1_ref.shape[1]
    experts = router_ref.shape[0]
    groups = do_ref.shape[0]
    grad = sum(r[...].astype(F32) for r in grad_refs)
    x1 = x1_ref[...]
    flat = grad[:, width:].T
    d_gate = flat[:experts] + flat[experts : 2 * experts]
    gates = gates_ref[...]
    d_logit = gates * (d_gate - jnp.sum(gates * d_gate, 0, keepdims=True))
    logit_ref[...] = d_logit
    high = d_logit.astype(BF)
    low = (d_logit - high.astype(F32)).astype(BF)
    router = router_ref[...]
    dh2 = grad[:, :width] + mm(
        jnp.concatenate([high, low], 0), jnp.concatenate([router, router], 0), TN
    )
    scale = lax.rsqrt(jnp.mean(x1 * x1, -1, keepdims=True) + EPSILON)
    normed = x1 * scale
    dgain_ref[...] = jnp.sum(dh2 * normed, 0, keepdims=True)
    dn = dh2 * gain_ref[...]
    dx1 = g_ref[...].astype(F32) + scale * (dn - normed * jnp.mean(dn * normed, -1, keepdims=True))
    dx1_ref[...] = dx1
    grad_o = mm(dx1.astype(BF), wo_ref[...], NT).astype(BF)
    for i in range(groups):
        do_ref[i] = grad_o[:, i * PAIR : (i + 1) * PAIR]


def own_tokens(grads, x1, gates, g, router_t, gain, w_out):
    rows, width = x1.shape
    groups = w_out.shape[0] // PAIR
    return pl.pallas_call(
        functools.partial(own_kernel, len(grads)),
        out_shape=[
            jax.ShapeDtypeStruct((rows, width), F32),
            jax.ShapeDtypeStruct((groups, rows, PAIR), BF),
            jax.ShapeDtypeStruct(gates.shape, F32),
            jax.ShapeDtypeStruct((1, width), F32),
        ],
        compiler_params=params(56),
        cost_estimate=busy(6),
        name="own_tokens",
    )(*grads, x1, gates, g, router_t, gain, w_out)


def own_weights_kernel(order_ref, dx1_ref, heads_ref, logit_ref, h2_ref, own_ref, other_ref, dr_ref, dwo_ref):
    groups = 2 * own_ref.shape[0]
    dwo_ref[...] = mm(heads_ref[...], dx1_ref[...].astype(BF), TN).astype(BF)
    for i in range(groups):
        spot = pl.multiple_of(order_ref[i] * PAIR, PAIR)
        target = other_ref if i % 2 else own_ref
        target[i // 2] = dwo_ref[:, pl.ds(spot, PAIR)]
    d_logit = logit_ref[...]
    high = d_logit.astype(BF)
    low = (d_logit - high.astype(F32)).astype(BF)
    both = mm(jnp.concatenate([high, low], 0), h2_ref[...])
    experts = d_logit.shape[0]
    dr_ref[...] = both[:experts] + both[experts:]


def own_weights(order, dx1, heads, logit, h2):
    rows, width = dx1.shape
    groups = order.shape[0]
    half = jax.ShapeDtypeStruct((groups // 2, groups * PAIR, PAIR), BF)
    return pl.pallas_call(
        own_weights_kernel,
        in_specs=[pl.BlockSpec(memory_space=pltpu.SMEM)]
        + [pl.BlockSpec(memory_space=pltpu.VMEM)] * 4,
        out_shape=[half, half, jax.ShapeDtypeStruct((logit.shape[0], width), F32)],
        scratch_shapes=[pltpu.VMEM((groups * PAIR, width), BF)],
        compiler_params=params(20),
        cost_estimate=busy(4),
        name="own_weights",
    )(order, dx1, heads, logit, h2)


def project_back_kernel(counts, units, order_ref, *refs):
    x_refs, refs = split_refs(refs, counts)
    gain_ref, dq_ref, dkv_ref, w_ref, dw_in_ref, dgain_in_ref = refs[:6]
    dw_ref, dh_ref, dgain_ref, held_ref, out_ref, load_sems, store_sems = refs[6:]
    rows = held_ref.shape[1]
    part = rows // MICRO
    loads = load_blocks(x_refs, held_ref, load_sems, rows)
    dw = dw_in_ref[...]
    dgain = dgain_in_ref[...]
    stores = []
    for i, unit in enumerate(units):
        spot = pl.ds(pl.multiple_of(order_ref[unit] * part, part), part)
        grads = jnp.concatenate(
            [
                jnp.concatenate([ref[m, spot, :] for m in range(MICRO)], 0)
                for ref in (dq_ref, dkv_ref)
            ],
            1,
        )
        dh = mm(grads, w_ref[...], NT)
        out_ref[i] = dh.astype(BF)
        stores.append(pltpu.make_async_copy(out_ref.at[i], dh_ref.at[i], store_sems.at[i]))
        stores[-1].start()
        for copy in loads[i]:
            copy.wait()
        x = held_ref[i].astype(F32)
        scale = lax.rsqrt(jnp.mean(x * x, -1, keepdims=True) + EPSILON)
        normed = x * scale
        dw = dw + mm(grads, (normed * gain_ref[...]).astype(BF), TN)
        dgain = dgain + jnp.sum(dh * normed, 0, keepdims=True)
    dw_ref[...] = dw
    dgain_ref[...] = dgain
    for copy in stores:
        copy.wait()


def project_back(core, order, x_blocks, rows, gain, dq, dkv, weight, dw, dgain):
    units = list(range(core, len(x_blocks), 2))
    blocks = [x_blocks[unit] for unit in units]
    parts = flat(blocks)
    width = weight.shape[0]
    count = len(units)
    return pl.pallas_call(
        functools.partial(project_back_kernel, counts_of(blocks), units),
        in_specs=[SMEM] + [ANY] * len(parts) + [VMEM] * 6,
        out_specs=[VMEM, ANY, VMEM],
        out_shape=[
            jax.ShapeDtypeStruct((2 * PAIR, width), F32),
            jax.ShapeDtypeStruct((count, rows, width), BF),
            jax.ShapeDtypeStruct((1, width), F32),
        ],
        scratch_shapes=[
            pltpu.VMEM((count, rows, width), BF),
            pltpu.VMEM((count, rows, width), BF),
            pltpu.SemaphoreType.DMA((len(parts),)),
            pltpu.SemaphoreType.DMA((count,)),
        ],
        compiler_params=params(16),
        cost_estimate=busy(4),
        name="project_back",
    )(
        order,
        *parts,
        gain,
        dq.reshape(MICRO, -1, PAIR),
        dkv.reshape(MICRO, -1, PAIR),
        weight,
        dw,
        dgain,
    )


def pack_kernel(local, order_ref, dw_ref, *refs):
    terms = refs[: len(refs) - 4]
    dr_ref, gain_one_ref, gain_two_ref, out_ref = refs[len(refs) - 4 :]
    experts, width = dr_ref.shape
    out_ref[:, : 2 * PAIR] = dw_ref[...].T.astype(BF)
    out_ref[:, 2 * PAIR : 3 * PAIR] = sum(r[...].astype(F32) for r in terms).astype(BF)
    router = pltpu.roll(dr_ref[...], local * order_ref[0], 0)
    rest = jnp.zeros((PAIR - experts - 16, width), F32)
    gains = [jnp.broadcast_to(r[...], (8, width)) for r in (gain_one_ref, gain_two_ref)]
    out_ref[:, 3 * PAIR :] = jnp.concatenate([router, *gains, rest], 0).T.astype(BF)


def pack_dense(order, local, dw, terms, d_router, gain_one, gain_two):
    width = dw.shape[1]
    vmem = pl.BlockSpec(memory_space=pltpu.VMEM)
    return pl.pallas_call(
        functools.partial(pack_kernel, local),
        in_specs=[pl.BlockSpec(memory_space=pltpu.SMEM)] + [vmem] * (len(terms) + 4),
        out_specs=vmem,
        out_shape=jax.ShapeDtypeStruct((width, 4 * PAIR), BF),
        compiler_params=params(14),
        cost_estimate=cost(1, 4 * width * 4 * PAIR),
        name="pack_dense",
    )(order, dw, *terms, d_router, gain_one, gain_two)


def add_up_kernel(pieces_ref, out_ref):
    total = pieces_ref[0].astype(F32)
    for i in range(1, pieces_ref.shape[0]):
        total = total + pieces_ref[i].astype(F32)
    out_ref[...] = total.astype(BF)


def add_up(pieces):
    return pl.pallas_call(
        add_up_kernel,
        out_shape=jax.ShapeDtypeStruct(pieces.shape[1:], BF),
        compiler_params=params(8),
        cost_estimate=cost(1, 2 * pieces.size),
        name="add_up",
    )(pieces)


def unpack_kernel(experts, pack_ref, q_ref, k_ref, v_ref, o_ref, router_ref, gain_one_ref, gain_two_ref):
    units = pack_ref.shape[0]
    total = jnp.zeros(pack_ref.shape[1:2] + (PAIR,), F32)
    for i in range(units):
        piece = pack_ref[i].astype(F32)
        q_ref[:, i * PAIR : (i + 1) * PAIR] = piece[:, :PAIR]
        o_ref[:, i * PAIR : (i + 1) * PAIR] = piece[:, 2 * PAIR : 3 * PAIR]
        total = total + piece[:, 3 * PAIR :]
    front = lanes(total.shape) < HEAD_DIM
    for i in range(0, units, 2):
        first = pack_ref[i, :, PAIR : 2 * PAIR].astype(F32)
        second = pack_ref[i + 1, :, PAIR : 2 * PAIR].astype(F32)
        spot = pl.ds(i * HEAD_DIM, PAIR)
        k_ref[:, spot] = jnp.where(front, first, pltpu.roll(second, HEAD_DIM, 1))
        v_ref[:, spot] = jnp.where(front, pltpu.roll(first, HEAD_DIM, 1), second)
    flat = total.T
    router_ref[...] = flat[:experts]
    gain_one_ref[...] = flat[experts : experts + 1]
    gain_two_ref[...] = flat[experts + 8 : experts + 9]


def unpack_dense(pack, experts):
    units, shard, _ = pack.shape
    return pl.pallas_call(
        functools.partial(unpack_kernel, experts),
        out_shape=[
            jax.ShapeDtypeStruct((shard, units * PAIR), F32),
            jax.ShapeDtypeStruct((shard, units * HEAD_DIM), F32),
            jax.ShapeDtypeStruct((shard, units * HEAD_DIM), F32),
            jax.ShapeDtypeStruct((shard, units * PAIR), F32),
            jax.ShapeDtypeStruct((experts, shard), F32),
            jax.ShapeDtypeStruct((1, shard), F32),
            jax.ShapeDtypeStruct((1, shard), F32),
        ],
        compiler_params=params(8),
        cost_estimate=cost(1, 4 * pack.size),
        name="unpack_dense",
    )(pack)


def open_kernel(local, pack_ref, gate_ref, up_ref, down_ref):
    shard, hidden = gate_ref.shape[1:]
    half = shard // 2
    for i in range(local):
        first = i * 3 * shard
        gate_ref[i] = pack_ref[first : first + shard, :].astype(F32)
        up_ref[i] = pack_ref[first + shard : first + 2 * shard, :].astype(F32)
        first = first + 2 * shard
        down_ref[i, :, :hidden] = pack_ref[first : first + half, :].astype(F32)
        down_ref[i, :, hidden:] = pack_ref[first + half : first + shard, :].astype(F32)


def open_experts(pack, local):
    hidden = pack.shape[1]
    shard = pack.shape[0] // (3 * local)
    return pl.pallas_call(
        functools.partial(open_kernel, local),
        out_shape=[
            jax.ShapeDtypeStruct((local, shard, hidden), F32),
            jax.ShapeDtypeStruct((local, shard, hidden), F32),
            jax.ShapeDtypeStruct((local, shard // 2, 2 * hidden), F32),
        ],
        compiler_params=params(12),
        cost_estimate=cost(1, 6 * pack.size),
        name="open_experts",
    )(pack)


def finish_kernel(x_ref, dx1_ref, gain_ref, *refs):
    out_ref = refs[-1]
    dh = sum(r[...].astype(F32) for r in refs[:-1])
    x = x_ref[...].astype(F32)
    scale = lax.rsqrt(jnp.mean(x * x, -1, keepdims=True) + EPSILON)
    normed = x * scale
    dn = dh * gain_ref[...]
    out_ref[...] = dx1_ref[...] + scale * (dn - normed * jnp.mean(dn * normed, -1, keepdims=True))


def finish(x, dx1, gain, terms):
    return pl.pallas_call(
        finish_kernel,
        out_shape=jax.ShapeDtypeStruct(dx1.shape, F32),
        compiler_params=params(16),
        cost_estimate=cost(1, 8 * dx1.size),
        name="finish",
    )(x, dx1, gain, *terms)


def swap_cores(block):
    units = lax.axis_size("ctx")
    return lax.ppermute(block, "ctx", [(i, i ^ 1) for i in range(units)])


def send_along(block, ahead):
    units = lax.axis_size("ctx")
    return lax.ppermute(block, "ctx", [(i, (i + 2 * ahead) % units) for i in range(units)])


def split_refs(refs, counts):
    found, first = [], 0
    for count in counts:
        found.append(refs[first : first + count])
        first = first + count
    return found, refs[first:]


def counts_of(blocks):
    return [len(parts) for parts in blocks]


def gather_near(block):
    return send_along(block, -1), send_along(block, 1)


def gather_far(near, cut):
    ahead, behind = near
    return send_along(behind[:cut], 1), send_along(ahead[cut:], -1)


def gather_chips(block):
    chips = lax.axis_size("ctx") // 2
    return [block] + [send_along(block, chips - ahead) for ahead in range(1, chips)]


def relative(block, near, far):
    return [(block,), near[:1], far, near[1:]]


def gather_cores(blocks):
    return [piece for parts in blocks for piece in (parts, tuple(swap_cores(part) for part in parts))]


def flat(blocks):
    return [part for parts in blocks for part in parts]


def scatter_cores(own, other):
    came = swap_cores(other)
    return [(a.astype(F32) + b.astype(F32)).astype(BF) for a, b in zip(own, came)]


def scatter_chips(sums):
    return [sums[0]] + [send_along(sums[i], i) for i in range(1, len(sums))]


def scatter_far(far, cut):
    return send_along(far[:cut], 1), send_along(far[cut:], -1)


def pass_on_kernel(ahead_ref, behind_ref, front_ref, back_ref, to_ahead_ref, to_behind_ref):
    cut = front_ref.shape[0]
    front = ahead_ref[:cut, :].astype(F32) + front_ref[...].astype(F32)
    to_ahead_ref[:cut, :] = front.astype(BF)
    to_ahead_ref[cut:, :] = ahead_ref[cut:, :]
    back = behind_ref[cut:, :].astype(F32) + back_ref[...].astype(F32)
    to_behind_ref[:cut, :] = behind_ref[:cut, :]
    to_behind_ref[cut:, :] = back.astype(BF)


def pass_on(sums, passed):
    shape = jax.ShapeDtypeStruct(sums[1].shape, BF)
    ahead, behind = pl.pallas_call(
        pass_on_kernel,
        out_shape=[shape, shape],
        compiler_params=params(10),
        cost_estimate=busy(1),
        name="pass_on",
    )(sums[1], sums[3], *passed)
    return [sums[0], ahead, behind]


def scatter_near(sums):
    own, ahead, behind = sums
    return [own, send_along(ahead, 1), send_along(behind, -1)]


def scatter_ctx(own, other):
    return scatter_chips(scatter_cores(own, other))


def per_device(
    tokens,
    routes,
    doc_starts,
    attn_gain,
    attn_q,
    attn_k,
    attn_v,
    attn_out,
    ffn_gain,
    router,
    w_gate,
    w_up,
    w_down,
    cotangent,
):
    part = tokens.shape[2]
    width = tokens.shape[3]
    top = routes.shape[3]
    experts = router.shape[1]
    local, shard, hidden = w_gate.shape
    units = lax.axis_size("ctx")
    shards = lax.axis_size("fsdp")
    rank = lax.axis_index("ctx").astype(jnp.int32)
    rows = MICRO * part
    length = units * rows
    capacity = MICRO * (5 * part * top // (4 * experts))
    places = jnp.arange(units, dtype=jnp.int32)
    order = (2 * (rank // 2 + places // 2) + ((rank ^ places) & 1)) % units
    find = (2 * (places // 2 - rank // 2) + ((rank ^ places) & 1)) % units

    x_own = tokens[0].reshape(rows, width)
    g_own = cotangent[0].reshape(rows, width)
    x_tall, dense, expert_pack = prepare(
        rank.reshape(1),
        x_own,
        routes[0].reshape(rows, top).T,
        doc_starts[0].reshape(1, rows),
        (attn_q, attn_k, attn_v, attn_out),
        (attn_gain.reshape(1, shard), ffn_gain.reshape(1, shard)),
        router.T,
        (w_gate, w_up, w_down),
    )
    weights = lax.all_gather(expert_pack, "fsdp", axis=0, tiled=True)
    weights = weights.reshape(shards, local, 3, shard, hidden)
    x_near = gather_chips(x_tall)
    dense = lax.all_gather(dense, "fsdp", axis=0, tiled=True)
    dense, x_near = together(dense, x_near)
    dense = dense.reshape(shards, -1, 3 * PAIR)
    x_blocks = gather_cores([(block,) for block in x_near])
    wo_part = dense[:, :shard, 2 * PAIR :].reshape(units, PAIR, PAIR)
    wo_part = wo_part.transpose(1, 0, 2).reshape(PAIR, width)
    g_wo = jnp.concatenate([g_own, wo_part], 0)
    g_wo, x_blocks = together(g_wo, x_blocks)
    g_near = gather_near(g_wo)

    tables = angle_tables(0, length // part, part) + angle_tables(0, part, 1)
    q, kv, route_rows, starts, w_qkv, gain_one, gain_two, router_t = project(
        order, x_blocks, top, dense, tables, experts
    )
    q = q.reshape(length, PAIR)
    kv = kv.reshape(length, PAIR)
    o, lse = attend(find, q, kv, starts)
    o = o.reshape(MICRO, length // MICRO, PAIR)
    o, g_near, g_wo = together(o, g_near, g_wo)
    o_chips = gather_chips(o)
    g_far = gather_far(g_near, (rows + PAIR) // 2)
    g_blocks = gather_cores(relative(g_wo, g_near, g_far))
    ranks, gs, w_out = pick(order, g_blocks, route_rows, local, capacity, experts)
    o_chips[2], ranks = together(o_chips[2], ranks)
    o_blocks = gather_cores([(block,) for block in o_chips])
    o = o.reshape(length, PAIR)
    router_t = jnp.roll(router_t, -local * rank, 0)
    xs, gate_rows, x1, h2, gates, heads = route(
        order, o_blocks, x_blocks, w_out, gain_two, router_t, route_rows, ranks, local, capacity
    )
    xs = xs.reshape(units, local, capacity, width)
    gs = gs.reshape(units, local, capacity, width)
    router_t = router_t.astype(BF)
    ys, dx, dg, dw = run_experts(order, xs, gs, ranks, gate_rows, weights, experts)
    dw = dw.reshape(shards * local * 3 * shard, hidden)
    dw = lax.psum_scatter(dw, "fsdp", scatter_dimension=0, tiled=True)
    grad_own, grad_other = combine(0, ranks, dx, dg), combine(1, ranks, dx, dg)
    grad_own, ys = together(grad_own, ys)
    grad_sums = scatter_cores(grad_own, grad_other)
    mix_sums = scatter_cores(combine(0, ranks, ys), combine(1, ranks, ys))
    grad_sums = pass_on(grad_sums, scatter_far(grad_sums[2], part))
    grads, mix_sums = together(scatter_near(grad_sums), mix_sums)
    mix_passed = scatter_far(mix_sums[2], part)
    dx1, grad_o, d_logit, d_gain_two = own_tokens(
        grads, x1, gates, g_own, router_t, gain_two, w_out
    )
    grad_o = lax.all_to_all(grad_o, "ctx", split_axis=0, concat_axis=0, tiled=True)
    grad_o = grad_o.reshape(units, MICRO, part, PAIR)
    dwo_own, dwo_other, d_router = own_weights(order, dx1, heads, d_logit, h2)
    dwo_sums = scatter_cores(dwo_own, dwo_other)
    mix_sums = pass_on(mix_sums, mix_passed)
    grad_o, dwo_sums, mix_sums = together(grad_o, dwo_sums, mix_sums)
    mixes = scatter_near(mix_sums)
    dwo_terms = scatter_chips(dwo_sums)
    dq, dkv = attend_back(find, q, kv, starts, lse, o, grad_o, tables)
    dq, dkv, mixes, dwo_terms = together(dq, dkv, mixes, dwo_terms)
    dw_qkv = jnp.zeros((2 * PAIR, width), F32)
    d_gain_one = jnp.zeros((1, width), F32)
    dw_qkv, dh_other, d_gain_one = project_back(
        1, order, x_blocks, rows, gain_one, dq, dkv, w_qkv, dw_qkv, d_gain_one
    )
    dw_qkv, dh_own, d_gain_one = project_back(
        0, order, x_blocks, rows, gain_one, dq, dkv, w_qkv, dw_qkv, d_gain_one
    )
    dh_sums = scatter_cores(dh_own, dh_other)
    dh_sums, d_gain_one = together(dh_sums, d_gain_one)
    dh_terms = scatter_near(pass_on(dh_sums, scatter_far(dh_sums[2], part)))
    pack = pack_dense(order, local, dw_qkv, dwo_terms, d_router, d_gain_one, d_gain_two)
    pack = pack.reshape(shards, shard, -1)
    pack = lax.all_to_all(pack, "fsdp", split_axis=0, concat_axis=0, tiled=True)
    d_gate, d_up, d_down = open_experts(dw, local)
    mixed = (x1 + sum(term.astype(F32) for term in mixes)).astype(BF)
    pack, mixed, d_gate, d_up, d_down = together(pack, mixed, d_gate, d_up, d_down)
    pack = lax.all_gather(add_up(pack), "ctx", axis=0, tiled=False)
    pack, dh_terms = together(pack, dh_terms)
    d_tokens = finish(x_own, dx1, gain_one, dh_terms)
    d_q, d_k, d_v, d_out, d_router, d_gain_one, d_gain_two = unpack_dense(pack, experts)
    return (
        mixed.reshape(1, MICRO, part, width),
        d_tokens.reshape(1, MICRO, part, width),
        d_gain_one.reshape(shard),
        d_q,
        d_k,
        d_v,
        d_out,
        d_gain_two.reshape(shard),
        d_router.T,
        d_gate,
        d_up,
        d_down,
    )


def solution(mesh):
    return jax.shard_map(
        per_device,
        mesh=mesh,
        in_specs=(
            P("fsdp", None, "ctx", None),
            P("fsdp", None, "ctx", None),
            P("fsdp", None, "ctx"),
            P("fsdp"),
            P("fsdp", None),
            P("fsdp", None),
            P("fsdp", None),
            P("fsdp", None),
            P("fsdp"),
            P("fsdp", None),
            P("ctx", "fsdp", None),
            P("ctx", "fsdp", None),
            P("ctx", "fsdp", None),
            P("fsdp", None, "ctx", None),
        ),
        out_specs=(
            P("fsdp", None, "ctx", None),
            P("fsdp", None, "ctx", None),
            P("fsdp"),
            P("fsdp", None),
            P("fsdp", None),
            P("fsdp", None),
            P("fsdp", None),
            P("fsdp"),
            P("fsdp", None),
            P("ctx", "fsdp", None),
            P("ctx", "fsdp", None),
            P("ctx", "fsdp", None),
        ),
        check_vma=False,
    )
```

```python
import functools
import math

import jax
import jax.numpy as jnp
import numpy as np
from jax import lax
from jax.experimental import pallas as pl
from jax.experimental.pallas import tpu as pltpu
from jax.sharding import PartitionSpec as P

HEADS = 16
KV_HEADS = 8
HEAD_DIM = 64
MICRO = 2
EPSILON = 1e-06
HIDDEN = -1e30
BF = jnp.bfloat16
F32 = jnp.float32
HIGHEST = lax.Precision.HIGHEST
PAIR = 2 * HEAD_DIM
MEBI = 1024 * 1024

NN = (((1,), (0,)), ((), ()))
NT = (((1,), (1,)), ((), ()))
TN = (((0,), (0,)), ((), ()))


def mm(left, right, dims=NN, precision=None):
    return lax.dot_general(left, right, dims, preferred_element_type=F32, precision=precision)


def params(mebibytes):
    return pltpu.CompilerParams(vmem_limit_bytes=mebibytes * MEBI)


def cost(flops, moved):
    return pl.CostEstimate(flops=int(flops), bytes_accessed=int(moved), transcendentals=0)


def busy(microseconds):
    return pl.CostEstimate(flops=int(1.1e9 * microseconds), bytes_accessed=1, transcendentals=0)


LIGHT = pl.CostEstimate(flops=1, bytes_accessed=1, transcendentals=0)


def together(*values):
    return lax.optimization_barrier(values)


def lanes(shape):
    return lax.broadcasted_iota(jnp.int32, shape, len(shape) - 1)


def turn(values, cosine, sine):
    spot = lanes(values.shape) % HEAD_DIM
    swapped = jnp.where(
        spot < HEAD_DIM // 2,
        pltpu.roll(values, PAIR - HEAD_DIM // 2, 1),
        pltpu.roll(values, HEAD_DIM // 2, 1),
    )
    return values * cosine + swapped * sine


def angle_tables(first, count, step):
    half = HEAD_DIM // 2
    frequencies = 10000.0 ** (-2.0 * np.arange(half) / HEAD_DIM)
    turned = (first + step * np.arange(count))[:, None] * frequencies[None, :]
    return (
        jnp.asarray(np.concatenate([np.cos(turned)] * 4, -1), F32),
        jnp.asarray(np.concatenate([np.sin(turned)] * 4, -1), F32),
    )


def block_angles(tables, block):
    cos_a, sin_a, cos_b, sin_b = tables
    cos_a, sin_a = cos_a[pl.ds(block, 1), :], sin_a[pl.ds(block, 1), :]
    cos_b, sin_b = cos_b[...], sin_b[...]
    sine = sin_a * cos_b + cos_a * sin_b
    back = lanes(sine.shape) % HEAD_DIM >= HEAD_DIM // 2
    return cos_a * cos_b - sin_a * sin_b, jnp.where(back, sine, -sine)


VMEM = pl.BlockSpec(memory_space=pltpu.VMEM)
SMEM = pl.BlockSpec(memory_space=pltpu.SMEM)
ANY = pl.BlockSpec(memory_space=pl.ANY)


def prepare_kernel(
    rank_ref, x_ref, routes_ref, starts_ref, q_ref, k_ref, v_ref, o_ref, gain_one_ref, gain_two_ref,
    router_ref, gate_ref, up_ref, down_ref,
    tall_ref, dense_ref, pack_ref,
):
    rank = rank_ref[0]
    local, shard, hidden = gate_ref.shape
    half = shard // 2
    for i in range(local):
        first = 3 * shard * i
        pack_ref[first : first + shard, :] = gate_ref[i]
        pack_ref[first + shard : first + 2 * shard, :] = up_ref[i]
        first = first + 2 * shard
        pack_ref[first : first + half, :] = down_ref[i, :, :hidden]
        pack_ref[first + half : first + shard, :] = down_ref[i, :, hidden:]
    rows = x_ref.shape[0]
    tall_ref[:rows, :] = x_ref[...]
    routes = routes_ref[...].astype(F32)
    starts = starts_ref[...]
    high = (starts // HEAD_DIM).astype(F32)
    low = (starts % HEAD_DIM).astype(F32)
    none = jnp.zeros_like(high)
    index = [routes[i : i + 1] for i in range(routes.shape[0])] + [high, low, none, none]
    across = x_ref.shape[1] // rows
    index = [
        jnp.concatenate(index[i : i + across], 1) for i in range(0, len(index), across)
    ]
    spare = tall_ref.shape[0] - rows
    index.append(jnp.zeros((spare - len(index), x_ref.shape[1]), F32))
    tall_ref[rows:, :] = jnp.concatenate(index, 0).astype(BF)

    mine = pl.ds(pl.multiple_of(rank * PAIR, PAIR), PAIR)
    dense_ref[:shard, :PAIR] = q_ref[:, mine]
    dense_ref[:shard, 2 * PAIR :] = o_ref[:, mine]
    pair = pl.ds(pl.multiple_of(rank // 2 * PAIR, PAIR), PAIR)
    keys = k_ref[:, pair].astype(F32)
    values = v_ref[:, pair].astype(F32)
    odd = rank % 2 == 1
    keys = jnp.where(odd, pltpu.roll(keys, HEAD_DIM, 1), keys)
    values = jnp.where(odd, values, pltpu.roll(values, HEAD_DIM, 1))
    front = lanes(keys.shape) < HEAD_DIM
    dense_ref[:shard, PAIR : 2 * PAIR] = jnp.where(front, keys, values).astype(BF)
    router = router_ref[...].astype(F32)
    gains = jnp.concatenate(
        [gain_one_ref[...].astype(F32), gain_two_ref[...].astype(F32), jnp.zeros((6, shard), F32)], 0
    )
    groups = [router[i : i + 8] for i in range(0, router.shape[0], 8)]
    empty = jnp.zeros_like(gains)
    dense_ref[shard:, :] = jnp.concatenate([*groups, gains, empty], 1).astype(BF)


def prepare(rank, x, routes_t, starts, attn, gains, router_t, experts):
    rows, width = x.shape
    local, shard, hidden = experts[0].shape
    return pl.pallas_call(
        prepare_kernel,
        in_specs=[SMEM] + [VMEM] * 13,
        out_specs=[VMEM] * 3,
        out_shape=[
            jax.ShapeDtypeStruct((rows + 16, width), BF),
            jax.ShapeDtypeStruct((shard + 8, 3 * PAIR), BF),
            jax.ShapeDtypeStruct((local * 3 * shard, hidden), BF),
        ],
        compiler_params=params(56),
        cost_estimate=busy(3),
        name="prepare",
    )(rank, x, routes_t, starts, *attn, *gains, router_t, *experts)


def load_blocks(blocks, target, sems, rows):
    found, used = [], 0
    for i, parts in enumerate(blocks):
        copies, first = [], 0
        for part in parts:
            count = min(part.shape[0], rows - first)
            copies.append(
                pltpu.make_async_copy(
                    part.at[pl.ds(0, count)], target.at[i, pl.ds(first, count)], sems.at[used]
                )
            )
            first, used = first + count, used + 1
        for copy in copies:
            copy.start()
        found.append(copies)
    return found


def project_kernel(counts, top, order_ref, *refs):
    x_refs, refs = split_refs(refs, counts)
    (
        dense_ref, cos_a_ref, sin_a_ref, cos_b_ref, sin_b_ref,
        q_ref, kv_ref, routes_ref, starts_ref, w_ref, gain_one_ref, gain_two_ref, router_ref,
        held_ref, sems,
    ) = refs
    tables = (cos_a_ref, sin_a_ref, cos_b_ref, sin_b_ref)
    tall, width = held_ref.shape[1:]
    units = len(counts)
    part = q_ref.shape[1] // units
    rows = MICRO * part
    shards = dense_ref.shape[0]
    shard = width // shards
    loads = load_blocks(x_refs, held_ref, sems, tall)
    w_ref[...] = dense_ref[:, :shard, : 2 * PAIR].reshape(width, 2 * PAIR)
    for i in range(0, shards, 2):
        small = [dense_ref[i + j, shard:, :].astype(F32) for j in range(2)]
        spot = pl.ds(i * shard, PAIR)
        front = lanes((8, PAIR)) < HEAD_DIM
        for group in range(5):
            lane = group // 2 * PAIR
            pair = [piece[:, lane : lane + PAIR] for piece in small]
            if group % 2 == 0:
                both = jnp.where(front, pair[0], pltpu.roll(pair[1], HEAD_DIM, 1))
            else:
                both = jnp.where(front, pltpu.roll(pair[0], HEAD_DIM, 1), pair[1])
            if group < 4:
                router_ref[group * 8 : group * 8 + 8, spot] = both
            else:
                gain_one_ref[:, spot] = both[0:1]
                gain_two_ref[:, spot] = both[1:2]
    gain = gain_one_ref[...]
    for unit in range(units):
        for copy in loads[unit]:
            copy.wait()
        x = held_ref[unit, :rows, :].astype(F32)
        scale = lax.rsqrt(jnp.mean(x * x, -1, keepdims=True) + EPSILON)
        lin = mm((x * scale * gain).astype(BF), w_ref[...])
        place = order_ref[unit]
        for m in range(MICRO):
            cosine, sine = block_angles(tables, m * units + place)
            here = lin[m * part : (m + 1) * part]
            spot = pl.ds(pl.multiple_of(place * part, part), part)
            q = turn(here[:, :PAIR], cosine, sine).astype(BF).astype(F32)
            q_ref[m, spot, :] = (q * (1.0 / math.sqrt(HEAD_DIM))).astype(BF)
            kv = here[:, PAIR:]
            kv = jnp.where(lanes(kv.shape) < HEAD_DIM, turn(kv, cosine, sine), kv)
            kv_ref[m, spot, :] = kv.astype(BF)
        index = held_ref[unit, rows:, :].astype(F32)
        across = width // rows

        def number(i, index=index, across=across):
            first = (i % across) * rows
            return index[i // across : i // across + 1, first : first + rows]

        routes_ref[unit] = jnp.concatenate([number(k) for k in range(top)], 0)
        starts = number(top) * HEAD_DIM + number(top + 1)
        starts_ref[unit] = jnp.broadcast_to(starts, starts_ref.shape[1:])


def project(order, x_blocks, top, dense, tables, experts):
    units = len(x_blocks)
    tall, width = x_blocks[0][0].shape
    part = tables[2].shape[0]
    parts = flat(x_blocks)
    index = jax.ShapeDtypeStruct((units, 8, MICRO * part), F32)
    return pl.pallas_call(
        functools.partial(project_kernel, counts_of(x_blocks), top),
        in_specs=[SMEM] + [ANY] * len(parts) + [VMEM] * 5,
        out_specs=[VMEM] * 8,
        out_shape=[
            jax.ShapeDtypeStruct((MICRO, units * part, PAIR), BF),
            jax.ShapeDtypeStruct((MICRO, units * part, PAIR), BF),
            index,
            index,
            jax.ShapeDtypeStruct((width, 2 * PAIR), BF),
            jax.ShapeDtypeStruct((1, width), F32),
            jax.ShapeDtypeStruct((1, width), F32),
            jax.ShapeDtypeStruct((experts, width), F32),
        ],
        scratch_shapes=[
            pltpu.VMEM((units, tall, width), BF),
            pltpu.SemaphoreType.DMA((len(parts),)),
        ],
        compiler_params=params(48),
        cost_estimate=busy(8),
        name="project",
    )(order, *parts, dense, *tables)


def front_heads(pair):
    pair = pair.astype(F32)
    front = lanes(pair.shape) < HEAD_DIM
    return jnp.concatenate(
        [jnp.where(front, pair, 0.0), jnp.where(front, pltpu.roll(pair, HEAD_DIM, 1), 0.0)], 0
    ).astype(BF)


def back_heads(pair):
    pair = pair.astype(F32)
    back = lanes(pair.shape) >= HEAD_DIM
    return jnp.concatenate(
        [jnp.where(back, pltpu.roll(pair, HEAD_DIM, 1), 0.0), jnp.where(back, pair, 0.0)], 0
    ).astype(BF)


def tile_starts(find_ref, start_ref, tile, rows):
    units, _, both = start_ref.shape
    part = both // MICRO
    span = rows // part
    half = units // span
    spot = pl.ds(pl.multiple_of(lax.div(tile, half) * part, part), part)
    pieces = [start_ref[find_ref[lax.rem(tile, half) * span + i], 0:1, spot] for i in range(span)]
    return jnp.concatenate(pieces + pieces, -1)


def attend_kernel(find_ref, q_ref, kv_ref, start_ref, o_ref, lse_ref, s_ref, kvt_ref, p_ref):
    tile = pl.program_id(0)
    rows = q_ref.shape[0]
    tiles = kv_ref.shape[0]

    @pl.when(tile == 0)
    def _():
        for chunk in range(tiles):
            kvt_ref[:, chunk * rows : (chunk + 1) * rows] = kv_ref[chunk].astype(F32).T.astype(BF)

    queries = front_heads(q_ref[...])
    start = tile_starts(find_ref, start_ref, tile, rows).astype(jnp.int32)
    key_row = lax.broadcasted_iota(jnp.int32, (rows, 2 * rows), 0)
    query_row = lanes((rows, 2 * rows)) % rows

    def fold(values, how):
        return how(values.reshape(rows // 8, 8, 2 * rows), axis=0)

    def one_tile(last):
        top = None
        for chunk in range(last + 1):
            seen = key_row >= start - chunk * rows
            if chunk == last:
                seen = seen & (key_row <= query_row)
            found = jnp.where(seen, mm(kv_ref[chunk], queries, NT), HIDDEN)
            s_ref[chunk] = found
            here = fold(found, jnp.max)
            top = here if top is None else jnp.maximum(top, here)
        top = jnp.max(top, axis=0, keepdims=True)
        total = jnp.zeros((8, 2 * rows), F32)
        for chunk in range(last + 1):
            raised = jnp.exp(s_ref[chunk] - top)
            p_ref[chunk * rows : (chunk + 1) * rows, :] = raised.astype(BF)
            total = total + fold(raised, jnp.sum)
        total = jnp.sum(total, axis=0, keepdims=True)
        depth = (last + 1) * rows
        out = mm(kvt_ref[:, :depth], p_ref[:depth, :])[HEAD_DIM:, :] * (1.0 / total)
        out = jnp.concatenate([out[:, :rows], out[:, rows:]], 0)
        o_ref[...] = out.T.astype(BF)
        lse_ref[0] = top + jnp.log(total)

    for last in range(tiles):
        pl.when(tile == last)(functools.partial(one_tile, last))


def attend(find, q, kv, starts, rows=256):
    length = q.shape[0]
    tiles = length // rows
    return pl.pallas_call(
        attend_kernel,
        grid_spec=pltpu.PrefetchScalarGridSpec(
            num_scalar_prefetch=1,
            grid=(tiles,),
            in_specs=[
                pl.BlockSpec((rows, PAIR), lambda t, s: (t, 0)),
                pl.BlockSpec((tiles, rows, PAIR), lambda t, s: (0, 0, 0)),
                pl.BlockSpec(starts.shape, lambda t, s: (0, 0, 0)),
            ],
            out_specs=[
                pl.BlockSpec((rows, PAIR), lambda t, s: (t, 0)),
                pl.BlockSpec((1, 1, 2 * rows), lambda t, s: (t, 0, 0)),
            ],
            scratch_shapes=[
                pltpu.VMEM((tiles, rows, 2 * rows), F32),
                pltpu.VMEM((PAIR, length), BF),
                pltpu.VMEM((length, 2 * rows), BF),
            ],
        ),
        out_shape=[
            jax.ShapeDtypeStruct((length, PAIR), BF),
            jax.ShapeDtypeStruct((tiles, 1, 2 * rows), F32),
        ],
        compiler_params=params(14),
        cost_estimate=busy(20),
        name="attend",
    )(find, q, kv.reshape(tiles, rows, PAIR), starts)


def attend_back_kernel(
    find_ref, q_ref, kv_ref, start_ref, lse_ref, o_ref, do_ref, cos_a_ref, sin_a_ref, cos_b_ref, sin_b_ref,
    dq_ref, dkv_ref, kvt_ref, dkv_acc, ds_ref, dqt_ref,
):
    tile = pl.program_id(0)
    rows = q_ref.shape[0]
    chunks = kv_ref.shape[0]

    @pl.when(tile == 0)
    def _():
        dkv_acc[...] = jnp.zeros_like(dkv_acc)
        for chunk in range(chunks):
            kvt_ref[:, chunk * rows : (chunk + 1) * rows] = kv_ref[chunk].astype(F32).T.astype(BF)

    grad_o = do_ref[...].reshape(rows, PAIR)
    queries = front_heads(q_ref[...])
    grads = back_heads(grad_o)
    product = grad_o.astype(F32) * o_ref[...].astype(F32)
    half = lax.broadcasted_iota(jnp.int32, (8, PAIR), 0)
    picked = (lanes((8, PAIR)) // HEAD_DIM == half).astype(F32)
    sums = mm(picked, product, NT, HIGHEST)
    delta = jnp.concatenate([sums[0:1], sums[1:2]], -1)
    start = tile_starts(find_ref, start_ref, tile, rows).astype(jnp.int32)
    lse = lse_ref[0]
    key_row = lax.broadcasted_iota(jnp.int32, (rows, 2 * rows), 0)
    query_row = lanes((rows, 2 * rows)) % rows

    def one_tile(last):
        for chunk in range(last + 1):
            keys = kv_ref[chunk]
            seen = key_row >= start - chunk * rows
            if chunk == last:
                seen = seen & (key_row <= query_row)
            found = jnp.where(seen, mm(keys, queries, NT), HIDDEN)
            prob = jnp.exp(found - lse)
            grad_s = (prob * (mm(keys, grads, NT) - delta)).astype(BF)
            ds_ref[chunk * rows : (chunk + 1) * rows, :] = grad_s
            dkv_acc[chunk] += mm(grad_s, queries) + mm(prob.astype(BF), grads)
        depth = (last + 1) * rows
        dqt_ref[...] = mm(kvt_ref[:, :depth], ds_ref[:depth, :])[:HEAD_DIM]

    for last in range(chunks):
        pl.when(tile == last)(functools.partial(one_tile, last))

    dq = dqt_ref[...] * (1.0 / math.sqrt(HEAD_DIM))
    dq = jnp.concatenate([dq[:, :rows], dq[:, rows:]], 0).T
    tables = (cos_a_ref, sin_a_ref, cos_b_ref, sin_b_ref)
    part = cos_b_ref.shape[0]

    def turn_back(values, first):
        pieces = []
        for i in range(rows // part):
            cosine, sine = block_angles(tables, first + i)
            pieces.append(turn(values[i * part : (i + 1) * part], cosine, -sine))
        return jnp.concatenate(pieces, 0)

    dq_ref[...] = turn_back(dq, tile * (rows // part)).astype(BF)

    @pl.when(tile == chunks - 1)
    def _():
        for chunk in range(chunks):
            flat = dkv_acc[chunk]
            spot = pl.ds(chunk * rows, rows)
            turned = turn_back(flat, chunk * (rows // part))
            dkv_ref[spot, :] = jnp.where(lanes(flat.shape) < HEAD_DIM, turned, flat).astype(BF)


def attend_back(find, q, kv, starts, lse, o, grad_o, tables, rows=256):
    length = q.shape[0]
    tiles = length // rows
    units, _, part, _ = grad_o.shape
    span = rows // part
    half = tiles // MICRO
    whole = pl.BlockSpec((length, PAIR), lambda t, s: (0, 0))
    return pl.pallas_call(
        attend_back_kernel,
        grid_spec=pltpu.PrefetchScalarGridSpec(
            num_scalar_prefetch=1,
            grid=(tiles,),
            in_specs=[
                pl.BlockSpec((rows, PAIR), lambda t, s: (t, 0)),
                pl.BlockSpec((tiles, rows, PAIR), lambda t, s: (0, 0, 0)),
                pl.BlockSpec(starts.shape, lambda t, s: (0, 0, 0)),
                pl.BlockSpec((1, 1, 2 * rows), lambda t, s: (t, 0, 0)),
                pl.BlockSpec((rows, PAIR), lambda t, s: (t, 0)),
                pl.BlockSpec((span, 1, part, PAIR), lambda t, s: (t % half, t // half, 0, 0)),
            ]
            + [pl.BlockSpec(table.shape, lambda t, s: (0, 0)) for table in tables],
            out_specs=[pl.BlockSpec((rows, PAIR), lambda t, s: (t, 0)), whole],
            scratch_shapes=[
                pltpu.VMEM((PAIR, length), BF),
                pltpu.VMEM((tiles, rows, PAIR), F32),
                pltpu.VMEM((length, 2 * rows), BF),
                pltpu.VMEM((HEAD_DIM, 2 * rows), F32),
            ],
        ),
        out_shape=[
            jax.ShapeDtypeStruct((length, PAIR), BF),
            jax.ShapeDtypeStruct((length, PAIR), BF),
        ],
        compiler_params=params(56),
        cost_estimate=busy(26),
        name="attend_back",
    )(find, q, kv.reshape(tiles, rows, PAIR), starts, lse, o, grad_o, *tables)


def one_hot(rank_rows, local, capacity):
    slots = lax.broadcasted_iota(jnp.int32, (capacity, rank_rows.shape[1]), 0).astype(F32)
    return jnp.concatenate([(rank_rows[e : e + 1] == slots).astype(F32) for e in range(local)], 0)


def gather_lanes(order_ref, blocks, out_ref):
    for i, refs in enumerate(blocks):
        spot = pl.multiple_of(order_ref[i] * PAIR, PAIR)
        first = 0
        for ref in refs:
            part = ref[...].reshape(-1, PAIR)
            last = first + part.shape[0]
            out_ref[first:last, pl.ds(spot, PAIR)] = part
            first = last


def chosen_rows(order_ref, routes, local, experts):
    rows = routes.shape[1]
    routes = routes.astype(jnp.int32) - local * order_ref[0]
    routes = jnp.where(routes < 0, routes + experts, routes)
    ids = lax.broadcasted_iota(jnp.int32, (experts, rows), 0)
    chosen = jnp.zeros((experts, rows), F32)
    for k in range(routes.shape[0]):
        chosen = chosen + (ids == routes[k : k + 1, :]).astype(F32)
    return chosen


def dispatch(rank_ref, units, held_ref, gs_ref, out_ref, loads, store_sems, local, capacity):
    stores = []
    for i, unit in enumerate(units):
        hot = one_hot(rank_ref[unit], local, capacity).astype(BF)
        for copy in loads[i]:
            copy.wait()
        out_ref[i] = mm(hot, held_ref[i]).astype(BF)
        stores.append(pltpu.make_async_copy(out_ref.at[i], gs_ref.at[unit], store_sems.at[i]))
        stores[-1].start()
    return stores


def pick_kernel(local, capacity, experts, units, counts, order_ref, *refs):
    g_refs, refs = split_refs(refs, counts)
    routes_ref, rank_ref, gs_ref, held_ref, out_ref, load_sems, store_sems = refs
    rows = held_ref.shape[1]
    loads = load_blocks(g_refs, held_ref, load_sems, rows)
    before = lax.broadcasted_iota(jnp.int32, (rows, rows), 0) < lanes((rows, rows))
    before = before.astype(F32).astype(BF)
    for unit in range(routes_ref.shape[0]):
        chosen = chosen_rows(order_ref, routes_ref[unit], local, experts)[:8]
        rank_ref[unit] = jnp.where(chosen > 0, mm(chosen.astype(BF), before), -1.0)
    stores = dispatch(
        rank_ref, units, held_ref, gs_ref, out_ref, loads, store_sems, local, capacity
    )
    for copy in stores:
        copy.wait()


def pick_scratch(count, rows, width, slots, loads):
    return [
        pltpu.VMEM((count, rows, width), BF),
        pltpu.VMEM((count, slots, width), BF),
        pltpu.SemaphoreType.DMA((loads,)),
        pltpu.SemaphoreType.DMA((count,)),
    ]


def pick(order, units, blocks, routes, local, capacity, experts):
    width = blocks[0][0].shape[1]
    total, _, rows = routes.shape
    parts = flat(blocks)
    return pl.pallas_call(
        functools.partial(pick_kernel, local, capacity, experts, units, counts_of(blocks)),
        in_specs=[SMEM] + [ANY] * len(parts) + [VMEM],
        out_specs=[VMEM, ANY],
        out_shape=[
            jax.ShapeDtypeStruct((total, 8, rows), F32),
            jax.ShapeDtypeStruct((total, local * capacity, width), BF),
        ],
        scratch_shapes=pick_scratch(len(units), rows, width, local * capacity, len(parts)),
        compiler_params=params(56),
        cost_estimate=busy(1),
        name="pick",
    )(order, *parts, routes)


def lane_copies(order_ref, blocks, target, sems):
    copies = []
    for i, parts in enumerate(blocks):
        spot = pl.ds(pl.multiple_of(order_ref[i] * PAIR, PAIR), PAIR)
        first = 0
        for part in parts:
            count = part.shape[0]
            place = target.at[(pl.ds(first, count),) + (slice(None),) * (len(part.shape) - 2) + (spot,)]
            copies.append(pltpu.make_async_copy(part, place, sems.at[len(copies)]))
            first = first + count
    return copies


def route_kernel(local, capacity, late, o_counts, x_counts, g_counts, order_ref, *refs):
    o_refs, refs = split_refs(refs, o_counts)
    x_refs, refs = split_refs(refs, x_counts)
    g_refs, refs = split_refs(refs, g_counts)
    (
        gain_ref, router_ref, routes_ref, rank_ref, _,
        xs_ref, rows_ref, x1_ref, h2_ref, gates_ref, heads_own_ref, gs_ref, wo_ref,
        heads_ref, held_ref, out_ref, o_sems, x_sems, store_sems,
        g_held_ref, g_out_ref, g_sems, g_store_sems, wo_sems,
    ) = refs
    units, rows, _ = held_ref.shape
    part = rows // MICRO
    experts = router_ref.shape[0]
    o_loads = lane_copies(order_ref, o_refs, heads_ref, o_sems)
    for copy in o_loads:
        copy.start()
    wo_loads = []
    for i, parts in enumerate(g_refs):
        source = parts[-1]
        first = source.shape[0] - PAIR
        spot = pl.ds(pl.multiple_of(order_ref[i] * PAIR, PAIR), PAIR)
        for j in range(units):
            here = pl.ds(j * PAIR, PAIR)
            wo_loads.append(
                pltpu.make_async_copy(
                    source.at[pl.ds(first, PAIR), here],
                    wo_ref.at[here, spot],
                    wo_sems.at[i * units + j],
                )
            )
            wo_loads[-1].start()
    x_loads = load_blocks(x_refs, held_ref, x_sems, rows)
    g_loads = load_blocks([g_refs[unit] for unit in late], g_held_ref, g_sems, rows)
    for copy in o_loads + wo_loads:
        copy.wait()
    for copies in x_loads:
        for copy in copies:
            copy.wait()
    router = router_ref[...].astype(BF)
    stores = dispatch(
        rank_ref, late, g_held_ref, gs_ref, g_out_ref, g_loads, g_store_sems, local, capacity
    )
    for unit in range(units):
        spot = pl.ds(pl.multiple_of(order_ref[unit] * part, part), part)
        heads = jnp.concatenate([heads_ref[m, spot, :] for m in range(MICRO)], 0)
        x1 = held_ref[unit].astype(F32) + mm(heads, wo_ref[...])
        scale = lax.rsqrt(jnp.mean(x1 * x1, -1, keepdims=True) + EPSILON)
        h2 = (x1 * scale * gain_ref[...]).astype(BF)
        held_ref[unit] = h2
        if unit == 0:
            x1_ref[...] = x1
            h2_ref[...] = h2
            heads_own_ref[...] = heads
    for unit in range(units):
        h2 = held_ref[unit]
        hot = one_hot(rank_ref[unit], local, capacity).astype(BF)
        out_ref[unit] = mm(hot, h2).astype(BF)
        stores.append(pltpu.make_async_copy(out_ref.at[unit], xs_ref.at[unit], store_sems.at[unit]))
        stores[-1].start()
        logits = mm(router, h2, NT)
        chosen = chosen_rows(order_ref, routes_ref[unit], local, experts)
        masked = jnp.where(chosen > 0, logits, HIDDEN)
        raised = jnp.exp(masked - jnp.max(masked, 0, keepdims=True))
        raised = jnp.where(chosen > 0, raised, 0.0)
        gates = raised / jnp.sum(raised, 0, keepdims=True)
        rows_ref[unit] = gates[:8]
        if unit == 0:
            gates_ref[...] = gates
    for copy in stores:
        copy.wait()


def route(order, late, o_blocks, x_blocks, g_blocks, gain, router_t, routes, ranks, gs, local, capacity):
    units, _, rows = ranks.shape
    experts, width = router_t.shape
    pieces = [flat(o_blocks), flat(x_blocks), flat(g_blocks)]
    count = sum(len(piece) for piece in pieces)
    late_parts = len(flat([g_blocks[unit] for unit in late]))

    def sems(number):
        return pltpu.SemaphoreType.DMA((number,))

    return pl.pallas_call(
        functools.partial(
            route_kernel,
            local,
            capacity,
            late,
            counts_of(o_blocks),
            counts_of(x_blocks),
            counts_of(g_blocks),
        ),
        in_specs=[SMEM] + [ANY] * count + [VMEM] * 4 + [ANY],
        out_specs=[ANY] + [VMEM] * 5 + [ANY, VMEM],
        out_shape=[
            jax.ShapeDtypeStruct((units, local * capacity, width), BF),
            jax.ShapeDtypeStruct((units, 8, rows), F32),
            jax.ShapeDtypeStruct((rows, width), F32),
            jax.ShapeDtypeStruct((rows, width), BF),
            jax.ShapeDtypeStruct((experts, rows), F32),
            jax.ShapeDtypeStruct((rows, width), BF),
            jax.ShapeDtypeStruct(gs.shape, BF),
            jax.ShapeDtypeStruct((units * PAIR, width), BF),
        ],
        scratch_shapes=[
            pltpu.VMEM((MICRO, units * rows // MICRO, width), BF),
            pltpu.VMEM((units, rows, width), BF),
            pltpu.VMEM((units, local * capacity, width), BF),
            sems(len(pieces[0])),
            sems(len(pieces[1])),
            sems(units),
        ]
        + pick_scratch(len(late), rows, width, local * capacity, late_parts)
        + [sems(units * units)],
        input_output_aliases={count + 5: 6},
        compiler_params=params(56),
        cost_estimate=busy(12),
        name="route",
    )(order, *pieces[0], *pieces[1], *pieces[2], gain, router_t, routes, ranks, gs)


def expert_kernel(
    local, experts,
    order_ref, xs_ref, gs_ref, rank_ref, rows_ref, w_ref,
    ys_ref, dx_ref, dg_ref, dw_ref,
):
    expert = pl.program_id(0)
    units, _, capacity, width = xs_ref.shape
    total = units * capacity
    shards, _, _, block, hidden = w_ref.shape
    half = block // 2
    depth = shards * block
    xs = xs_ref[...].reshape(total, width)
    gs = gs_ref[...].reshape(total, width)
    mine = pl.ds(expert, 1)
    tokens = rank_ref.shape[2]
    slots = lax.broadcasted_iota(jnp.int32, (capacity, tokens), 0).astype(F32)
    gate = jnp.concatenate(
        [
            jnp.sum(jnp.where(rank_ref[u, mine, :] == slots, rows_ref[u, mine, :], 0.0), 1, keepdims=True)
            for u in range(units)
        ],
        0,
    )
    w_gate = w_ref[:, 0, 0].reshape(depth, hidden)
    w_up = w_ref[:, 0, 1].reshape(depth, hidden)
    w_down = jnp.concatenate(
        [w_ref[:, 0, 2, :half].reshape(hidden, hidden), w_ref[:, 0, 2, half:].reshape(hidden, hidden)], 1
    )
    a = mm(xs, w_gate)
    b = mm(xs, w_up)
    sigmoid = jax.nn.sigmoid(a)
    silu = a * sigmoid
    hid = (silu * b).astype(BF)
    y = mm(hid, w_down).astype(BF).astype(F32)
    ys_ref[...] = (gate * y).astype(BF).reshape(ys_ref.shape)
    back = mm(gs, w_down, NT)
    hid_full = hid.astype(F32)
    d_gate = jnp.sum(back * hid_full, -1, keepdims=True)
    d_hid = gate * back
    da = (d_hid * b * sigmoid * (1.0 + a * (1.0 - sigmoid))).astype(BF)
    db = (d_hid * silu).astype(BF)
    dx = mm(da, w_gate, NT) + mm(db, w_up, NT)
    dx_ref[...] = dx.astype(BF).reshape(dx_ref.shape)
    high = d_gate.astype(BF).astype(F32)
    rest = d_gate - high
    shape = (units, capacity, PAIR)
    spot = lanes(shape)
    source = lax.broadcasted_iota(jnp.int32, shape, 0)
    place = jnp.zeros(shape, jnp.int32)
    for unit in range(units):
        ahead = local * (order_ref[0] - order_ref[unit]) + expert + experts
        place = jnp.where(source == unit, lax.rem(ahead, experts), place)
    high = jnp.broadcast_to(high, (total, PAIR)).reshape(shape)
    rest = jnp.broadcast_to(rest, (total, PAIR)).reshape(shape)
    spread = jnp.where(spot == place, high, jnp.where(spot == place + experts, rest, 0.0))
    dg_ref[...] = spread.astype(BF).reshape(dg_ref.shape)
    d_gate_w = mm(xs, da, TN).astype(BF)
    dw_ref[:, 0, 0] = d_gate_w.reshape(shards, block, hidden)
    d_up_w = mm(xs, db, TN).astype(BF)
    dw_ref[:, 0, 1] = d_up_w.reshape(shards, block, hidden)
    scaled = (hid_full * gate).astype(BF)
    d_down_w = mm(scaled, gs, TN).astype(BF)
    dw_ref[:, 0, 2, :half] = d_down_w[:, :hidden].reshape(shards, half, hidden)
    dw_ref[:, 0, 2, half:] = d_down_w[:, hidden:].reshape(shards, half, hidden)


def run_experts(order, xs, gs, ranks, gate_rows, weights, experts):
    units, local, capacity, width = xs.shape
    index = pl.BlockSpec(ranks.shape, lambda e, s: (0, 0, 0))
    shards, _, kinds, block, hidden = weights.shape
    rows = pl.BlockSpec((units, 1, capacity, width), lambda e, s: (0, e, 0, 0))
    narrow = pl.BlockSpec((units, 1, capacity, PAIR), lambda e, s: (0, e, 0, 0))
    wide = pl.BlockSpec((shards, 1, kinds, block, hidden), lambda e, s: (0, e, 0, 0, 0))
    return pl.pallas_call(
        functools.partial(expert_kernel, local, experts),
        grid_spec=pltpu.PrefetchScalarGridSpec(
            num_scalar_prefetch=1,
            grid=(local,),
            in_specs=[rows, rows, index, index, wide],
            out_specs=[rows, rows, narrow, wide],
        ),
        out_shape=[
            jax.ShapeDtypeStruct(xs.shape, BF),
            jax.ShapeDtypeStruct(xs.shape, BF),
            jax.ShapeDtypeStruct((units, local, capacity, PAIR), BF),
            jax.ShapeDtypeStruct(weights.shape, BF),
        ],
        compiler_params=params(56),
        cost_estimate=busy(34),
        name="run_experts",
    )(order, xs, gs, ranks, gate_rows, weights)


def combine_kernel(local, capacity, rank_ref, ys_ref, out_ref):
    hot = one_hot(rank_ref[0], local, capacity).astype(BF)
    slots = local * capacity
    out_ref[0] = mm(hot, ys_ref[0].reshape(slots, ys_ref.shape[-1]), TN).astype(BF)


def combine_narrow_kernel(local, capacity, rank_ref, ys_ref, dg_ref, out_ref):
    hot = one_hot(rank_ref[0], local, capacity).astype(BF)
    slots = local * capacity
    width = ys_ref.shape[-1]
    out_ref[0, :, :width] = mm(hot, ys_ref[0].reshape(slots, width), TN).astype(BF)
    out_ref[0, :, width:] = mm(hot, dg_ref[0].reshape(slots, PAIR), TN).astype(BF)


def combine(core, rank, ys, *dg):
    units, local, capacity, width = ys.shape
    rows = rank.shape[-1]
    count = units // 2
    out_width = width + PAIR * len(dg)

    def slots(last):
        return pl.BlockSpec((1, local, capacity, last), lambda u: (2 * u + core, 0, 0, 0))

    return pl.pallas_call(
        functools.partial(combine_narrow_kernel if dg else combine_kernel, local, capacity),
        grid=(count,),
        in_specs=[pl.BlockSpec((1, 8, rows), lambda u: (2 * u + core, 0, 0)), slots(width)]
        + [slots(PAIR)] * len(dg),
        out_specs=pl.BlockSpec((1, rows, out_width), lambda u: (u, 0, 0)),
        out_shape=jax.ShapeDtypeStruct((count, rows, out_width), BF),
        compiler_params=params(16),
        cost_estimate=busy(1),
        name="combine",
    )(rank, ys, *dg)


def own_kernel(count, *refs):
    grad_refs = refs[:count]
    (
        x1_ref, gates_ref, g_ref, router_ref, gain_ref, wo_ref,
        dx1_ref, do_ref, logit_ref, dgain_ref,
    ) = refs[count:]
    width = x1_ref.shape[1]
    experts = router_ref.shape[0]
    groups = do_ref.shape[0]
    grad = sum(r[...].astype(F32) for r in grad_refs)
    x1 = x1_ref[...]
    flat = grad[:, width:].T
    d_gate = flat[:experts] + flat[experts : 2 * experts]
    gates = gates_ref[...]
    d_logit = gates * (d_gate - jnp.sum(gates * d_gate, 0, keepdims=True))
    logit_ref[...] = d_logit
    high = d_logit.astype(BF)
    low = (d_logit - high.astype(F32)).astype(BF)
    router = router_ref[...]
    dh2 = grad[:, :width] + mm(
        jnp.concatenate([high, low], 0), jnp.concatenate([router, router], 0), TN
    )
    scale = lax.rsqrt(jnp.mean(x1 * x1, -1, keepdims=True) + EPSILON)
    normed = x1 * scale
    dgain_ref[...] = jnp.sum(dh2 * normed, 0, keepdims=True)
    dn = dh2 * gain_ref[...]
    dx1 = g_ref[...].astype(F32) + scale * (dn - normed * jnp.mean(dn * normed, -1, keepdims=True))
    dx1_ref[...] = dx1
    grad_o = mm(dx1.astype(BF), wo_ref[...], NT).astype(BF)
    for i in range(groups):
        do_ref[i] = grad_o[:, i * PAIR : (i + 1) * PAIR]


def own_tokens(grads, x1, gates, g, router_t, gain, w_out):
    rows, width = x1.shape
    groups = w_out.shape[0] // PAIR
    return pl.pallas_call(
        functools.partial(own_kernel, len(grads)),
        out_shape=[
            jax.ShapeDtypeStruct((rows, width), F32),
            jax.ShapeDtypeStruct((groups, rows, PAIR), BF),
            jax.ShapeDtypeStruct(gates.shape, F32),
            jax.ShapeDtypeStruct((1, width), F32),
        ],
        compiler_params=params(56),
        cost_estimate=busy(6),
        name="own_tokens",
    )(*grads, x1, gates, g, router_t, gain, w_out)


def own_weights_kernel(order_ref, dx1_ref, heads_ref, logit_ref, h2_ref, own_ref, other_ref, dr_ref, dwo_ref):
    groups = 2 * own_ref.shape[0]
    dwo_ref[...] = mm(heads_ref[...], dx1_ref[...].astype(BF), TN).astype(BF)
    for i in range(groups):
        spot = pl.multiple_of(order_ref[i] * PAIR, PAIR)
        target = other_ref if i % 2 else own_ref
        target[i // 2] = dwo_ref[:, pl.ds(spot, PAIR)]
    d_logit = logit_ref[...]
    high = d_logit.astype(BF)
    low = (d_logit - high.astype(F32)).astype(BF)
    both = mm(jnp.concatenate([high, low], 0), h2_ref[...])
    experts = d_logit.shape[0]
    dr_ref[...] = both[:experts] + both[experts:]


def own_weights(order, dx1, heads, logit, h2):
    rows, width = dx1.shape
    groups = order.shape[0]
    half = jax.ShapeDtypeStruct((groups // 2, groups * PAIR, PAIR), BF)
    return pl.pallas_call(
        own_weights_kernel,
        in_specs=[pl.BlockSpec(memory_space=pltpu.SMEM)]
        + [pl.BlockSpec(memory_space=pltpu.VMEM)] * 4,
        out_shape=[half, half, jax.ShapeDtypeStruct((logit.shape[0], width), F32)],
        scratch_shapes=[pltpu.VMEM((groups * PAIR, width), BF)],
        compiler_params=params(56),
        cost_estimate=busy(4),
        name="own_weights",
    )(order, dx1, heads, logit, h2)


def project_back_kernel(counts, units, order_ref, *refs):
    x_refs, refs = split_refs(refs, counts)
    gain_ref, dq_ref, dkv_ref, w_ref, dw_in_ref, dgain_in_ref = refs[:6]
    dw_ref, dh_ref, dgain_ref, held_ref, out_ref, load_sems, store_sems = refs[6:]
    rows = held_ref.shape[1]
    part = rows // MICRO
    loads = load_blocks(x_refs, held_ref, load_sems, rows)
    dw = dw_in_ref[...]
    dgain = dgain_in_ref[...]
    stores = []
    for i, unit in enumerate(units):
        spot = pl.ds(pl.multiple_of(order_ref[unit] * part, part), part)
        grads = jnp.concatenate(
            [
                jnp.concatenate([ref[m, spot, :] for m in range(MICRO)], 0)
                for ref in (dq_ref, dkv_ref)
            ],
            1,
        )
        dh = mm(grads, w_ref[...], NT)
        out_ref[i] = dh.astype(BF)
        stores.append(pltpu.make_async_copy(out_ref.at[i], dh_ref.at[i], store_sems.at[i]))
        stores[-1].start()
        for copy in loads[i]:
            copy.wait()
        x = held_ref[i].astype(F32)
        scale = lax.rsqrt(jnp.mean(x * x, -1, keepdims=True) + EPSILON)
        normed = x * scale
        dw = dw + mm(grads, (normed * gain_ref[...]).astype(BF), TN)
        dgain = dgain + jnp.sum(dh * normed, 0, keepdims=True)
    dw_ref[...] = dw
    dgain_ref[...] = dgain
    for copy in stores:
        copy.wait()


def project_back(core, order, x_blocks, rows, gain, dq, dkv, weight, dw, dgain):
    units = list(range(core, len(x_blocks), 2))
    blocks = [x_blocks[unit] for unit in units]
    parts = flat(blocks)
    width = weight.shape[0]
    count = len(units)
    return pl.pallas_call(
        functools.partial(project_back_kernel, counts_of(blocks), units),
        in_specs=[SMEM] + [ANY] * len(parts) + [VMEM] * 6,
        out_specs=[VMEM, ANY, VMEM],
        out_shape=[
            jax.ShapeDtypeStruct((2 * PAIR, width), F32),
            jax.ShapeDtypeStruct((count, rows, width), BF),
            jax.ShapeDtypeStruct((1, width), F32),
        ],
        scratch_shapes=[
            pltpu.VMEM((count, rows, width), BF),
            pltpu.VMEM((count, rows, width), BF),
            pltpu.SemaphoreType.DMA((len(parts),)),
            pltpu.SemaphoreType.DMA((count,)),
        ],
        compiler_params=params(16),
        cost_estimate=busy(4),
        name="project_back",
    )(
        order,
        *parts,
        gain,
        dq.reshape(MICRO, -1, PAIR),
        dkv.reshape(MICRO, -1, PAIR),
        weight,
        dw,
        dgain,
    )


def pack_kernel(local, order_ref, dw_ref, *refs):
    terms = refs[: len(refs) - 4]
    dr_ref, gain_one_ref, gain_two_ref, out_ref = refs[len(refs) - 4 :]
    experts, width = dr_ref.shape
    out_ref[:, : 2 * PAIR] = dw_ref[...].T.astype(BF)
    out_ref[:, 2 * PAIR : 3 * PAIR] = sum(r[...].astype(F32) for r in terms).astype(BF)
    router = pltpu.roll(dr_ref[...], local * order_ref[0], 0)
    rest = jnp.zeros((PAIR - experts - 16, width), F32)
    gains = [jnp.broadcast_to(r[...], (8, width)) for r in (gain_one_ref, gain_two_ref)]
    out_ref[:, 3 * PAIR :] = jnp.concatenate([router, *gains, rest], 0).T.astype(BF)


def pack_dense(order, local, dw, terms, d_router, gain_one, gain_two):
    width = dw.shape[1]
    vmem = pl.BlockSpec(memory_space=pltpu.VMEM)
    return pl.pallas_call(
        functools.partial(pack_kernel, local),
        in_specs=[pl.BlockSpec(memory_space=pltpu.SMEM)] + [vmem] * (len(terms) + 4),
        out_specs=vmem,
        out_shape=jax.ShapeDtypeStruct((width, 4 * PAIR), BF),
        compiler_params=params(14),
        cost_estimate=cost(1, 4 * width * 4 * PAIR),
        name="pack_dense",
    )(order, dw, *terms, d_router, gain_one, gain_two)


def add_up_kernel(pieces_ref, out_ref):
    total = pieces_ref[0].astype(F32)
    for i in range(1, pieces_ref.shape[0]):
        total = total + pieces_ref[i].astype(F32)
    out_ref[...] = total.astype(BF)


def add_up(pieces):
    return pl.pallas_call(
        add_up_kernel,
        out_shape=jax.ShapeDtypeStruct(pieces.shape[1:], BF),
        compiler_params=params(8),
        cost_estimate=cost(1, 2 * pieces.size),
        name="add_up",
    )(pieces)


def unpack_kernel(experts, pack_ref, q_ref, k_ref, v_ref, o_ref, router_ref, gain_one_ref, gain_two_ref):
    units = pack_ref.shape[0]
    total = jnp.zeros(pack_ref.shape[1:2] + (PAIR,), F32)
    for i in range(units):
        piece = pack_ref[i].astype(F32)
        q_ref[:, i * PAIR : (i + 1) * PAIR] = piece[:, :PAIR]
        o_ref[:, i * PAIR : (i + 1) * PAIR] = piece[:, 2 * PAIR : 3 * PAIR]
        total = total + piece[:, 3 * PAIR :]
    front = lanes(total.shape) < HEAD_DIM
    for i in range(0, units, 2):
        first = pack_ref[i, :, PAIR : 2 * PAIR].astype(F32)
        second = pack_ref[i + 1, :, PAIR : 2 * PAIR].astype(F32)
        spot = pl.ds(i * HEAD_DIM, PAIR)
        k_ref[:, spot] = jnp.where(front, first, pltpu.roll(second, HEAD_DIM, 1))
        v_ref[:, spot] = jnp.where(front, pltpu.roll(first, HEAD_DIM, 1), second)
    flat = total.T
    router_ref[...] = flat[:experts]
    gain_one_ref[...] = flat[experts : experts + 1]
    gain_two_ref[...] = flat[experts + 8 : experts + 9]


def unpack_dense(pack, experts):
    units, shard, _ = pack.shape
    return pl.pallas_call(
        functools.partial(unpack_kernel, experts),
        out_shape=[
            jax.ShapeDtypeStruct((shard, units * PAIR), F32),
            jax.ShapeDtypeStruct((shard, units * HEAD_DIM), F32),
            jax.ShapeDtypeStruct((shard, units * HEAD_DIM), F32),
            jax.ShapeDtypeStruct((shard, units * PAIR), F32),
            jax.ShapeDtypeStruct((experts, shard), F32),
            jax.ShapeDtypeStruct((1, shard), F32),
            jax.ShapeDtypeStruct((1, shard), F32),
        ],
        compiler_params=params(8),
        cost_estimate=cost(1, 4 * pack.size),
        name="unpack_dense",
    )(pack)


def open_kernel(local, pack_ref, gate_ref, up_ref, down_ref):
    shard, hidden = gate_ref.shape[1:]
    half = shard // 2
    for i in range(local):
        first = i * 3 * shard
        gate_ref[i] = pack_ref[first : first + shard, :].astype(F32)
        up_ref[i] = pack_ref[first + shard : first + 2 * shard, :].astype(F32)
        first = first + 2 * shard
        down_ref[i, :, :hidden] = pack_ref[first : first + half, :].astype(F32)
        down_ref[i, :, hidden:] = pack_ref[first + half : first + shard, :].astype(F32)


def open_experts(pack, local):
    hidden = pack.shape[1]
    shard = pack.shape[0] // (3 * local)
    return pl.pallas_call(
        functools.partial(open_kernel, local),
        out_shape=[
            jax.ShapeDtypeStruct((local, shard, hidden), F32),
            jax.ShapeDtypeStruct((local, shard, hidden), F32),
            jax.ShapeDtypeStruct((local, shard // 2, 2 * hidden), F32),
        ],
        compiler_params=params(12),
        cost_estimate=cost(1, 6 * pack.size),
        name="open_experts",
    )(pack)


def finish_kernel(x_ref, dx1_ref, gain_ref, *refs):
    out_ref = refs[-1]
    dh = sum(r[...].astype(F32) for r in refs[:-1])
    x = x_ref[...].astype(F32)
    scale = lax.rsqrt(jnp.mean(x * x, -1, keepdims=True) + EPSILON)
    normed = x * scale
    dn = dh * gain_ref[...]
    out_ref[...] = dx1_ref[...] + scale * (dn - normed * jnp.mean(dn * normed, -1, keepdims=True))


def finish(x, dx1, gain, terms):
    return pl.pallas_call(
        finish_kernel,
        out_shape=jax.ShapeDtypeStruct(dx1.shape, F32),
        compiler_params=params(16),
        cost_estimate=cost(1, 8 * dx1.size),
        name="finish",
    )(x, dx1, gain, *terms)


def swap_cores(block):
    units = lax.axis_size("ctx")
    return lax.ppermute(block, "ctx", [(i, i ^ 1) for i in range(units)])


def send_along(block, ahead):
    units = lax.axis_size("ctx")
    return lax.ppermute(block, "ctx", [(i, (i + 2 * ahead) % units) for i in range(units)])


def split_refs(refs, counts):
    found, first = [], 0
    for count in counts:
        found.append(refs[first : first + count])
        first = first + count
    return found, refs[first:]


def counts_of(blocks):
    return [len(parts) for parts in blocks]


def gather_near(block):
    return send_along(block, -1), send_along(block, 1)


def gather_far(near, cut):
    ahead, behind = near
    return send_along(behind[:cut], 1), send_along(ahead[cut:], -1)


def gather_chips(block):
    chips = lax.axis_size("ctx") // 2
    return [block] + [send_along(block, chips - ahead) for ahead in range(1, chips)]


def relative(block, near, far):
    return [(block,), near[:1], far, near[1:]]


def gather_cores(blocks):
    return [piece for parts in blocks for piece in (parts, tuple(swap_cores(part) for part in parts))]


def flat(blocks):
    return [part for parts in blocks for part in parts]


def scatter_cores(own, other):
    came = swap_cores(other)
    return [(a.astype(F32) + b.astype(F32)).astype(BF) for a, b in zip(own, came)]


def scatter_chips(sums):
    return [sums[0]] + [send_along(sums[i], i) for i in range(1, len(sums))]


def scatter_far(far, cut):
    return send_along(far[:cut], 1), send_along(far[cut:], -1)


def pass_on_kernel(ahead_ref, behind_ref, front_ref, back_ref, to_ahead_ref, to_behind_ref):
    cut = front_ref.shape[0]
    front = ahead_ref[:cut, :].astype(F32) + front_ref[...].astype(F32)
    to_ahead_ref[:cut, :] = front.astype(BF)
    to_ahead_ref[cut:, :] = ahead_ref[cut:, :]
    back = behind_ref[cut:, :].astype(F32) + back_ref[...].astype(F32)
    to_behind_ref[:cut, :] = behind_ref[:cut, :]
    to_behind_ref[cut:, :] = back.astype(BF)


def pass_on(sums, passed):
    shape = jax.ShapeDtypeStruct(sums[1].shape, BF)
    ahead, behind = pl.pallas_call(
        pass_on_kernel,
        out_shape=[shape, shape],
        compiler_params=params(10),
        cost_estimate=busy(1),
        name="pass_on",
    )(sums[1], sums[3], *passed)
    return [sums[0], ahead, behind]


def scatter_near(sums):
    own, ahead, behind = sums
    return [own, send_along(ahead, 1), send_along(behind, -1)]


def scatter_ctx(own, other):
    return scatter_chips(scatter_cores(own, other))


def per_device(
    tokens,
    routes,
    doc_starts,
    attn_gain,
    attn_q,
    attn_k,
    attn_v,
    attn_out,
    ffn_gain,
    router,
    w_gate,
    w_up,
    w_down,
    cotangent,
):
    part = tokens.shape[2]
    width = tokens.shape[3]
    top = routes.shape[3]
    experts = router.shape[1]
    local, shard, hidden = w_gate.shape
    units = lax.axis_size("ctx")
    shards = lax.axis_size("fsdp")
    rank = lax.axis_index("ctx").astype(jnp.int32)
    rows = MICRO * part
    length = units * rows
    capacity = MICRO * (5 * part * top // (4 * experts))
    places = jnp.arange(units, dtype=jnp.int32)
    order = (2 * (rank // 2 + places // 2) + ((rank ^ places) & 1)) % units
    find = (2 * (places // 2 - rank // 2) + ((rank ^ places) & 1)) % units

    x_own = tokens[0].reshape(rows, width)
    g_own = cotangent[0].reshape(rows, width)
    x_tall, dense, expert_pack = prepare(
        rank.reshape(1),
        x_own,
        routes[0].reshape(rows, top).T,
        doc_starts[0].reshape(1, rows),
        (attn_q, attn_k, attn_v, attn_out),
        (attn_gain.reshape(1, shard), ffn_gain.reshape(1, shard)),
        router.T,
        (w_gate, w_up, w_down),
    )
    weights = lax.all_gather(expert_pack, "fsdp", axis=0, tiled=True)
    weights = weights.reshape(shards, local, 3, shard, hidden)
    x_near = gather_chips(x_tall)
    dense = lax.all_gather(dense, "fsdp", axis=0, tiled=True)
    dense, x_near = together(dense, x_near)
    dense = dense.reshape(shards, -1, 3 * PAIR)
    x_blocks = gather_cores([(block,) for block in x_near])
    wo_part = dense[:, :shard, 2 * PAIR :].reshape(units, PAIR, PAIR)
    wo_part = wo_part.transpose(1, 0, 2).reshape(PAIR, width)
    g_wo = jnp.concatenate([g_own, wo_part], 0)
    g_wo, x_blocks = together(g_wo, x_blocks)
    g_near = gather_near(g_wo)

    tables = angle_tables(0, length // part, part) + angle_tables(0, part, 1)
    q, kv, route_rows, starts, w_qkv, gain_one, gain_two, router_t = project(
        order, x_blocks, top, dense, tables, experts
    )
    q = q.reshape(length, PAIR)
    kv = kv.reshape(length, PAIR)
    o, lse = attend(find, q, kv, starts)
    o = o.reshape(MICRO, length // MICRO, PAIR)
    o, g_near, g_wo = together(o, g_near, g_wo)
    o_chips = gather_chips(o)
    g_far = gather_far(g_near, (rows + PAIR) // 2)
    near_blocks = gather_cores([(g_wo,), g_near[:1], g_near[1:]])
    early, late = [0, 1, 2, 3, 6, 7], [4, 5]
    ranks, gs = pick(order, early, near_blocks, route_rows, local, capacity, experts)
    g_far, ranks = together(g_far, ranks)
    g_blocks = near_blocks[:4] + gather_cores([g_far]) + near_blocks[4:]
    o_chips[2], g_blocks[5] = together(o_chips[2], g_blocks[5])
    o_blocks = gather_cores([(block,) for block in o_chips])
    o = o.reshape(length, PAIR)
    router_t = jnp.roll(router_t, -local * rank, 0)
    xs, gate_rows, x1, h2, gates, heads, gs, w_out = route(
        order, late, o_blocks, x_blocks, g_blocks, gain_two, router_t, route_rows, ranks, gs,
        local, capacity,
    )
    xs = xs.reshape(units, local, capacity, width)
    gs = gs.reshape(units, local, capacity, width)
    router_t = router_t.astype(BF)
    ys, dx, dg, dw = run_experts(order, xs, gs, ranks, gate_rows, weights, experts)
    dw = dw.reshape(shards * local * 3 * shard, hidden)
    dw = lax.psum_scatter(dw, "fsdp", scatter_dimension=0, tiled=True)
    grad_own, grad_other = combine(0, ranks, dx, dg), combine(1, ranks, dx, dg)
    grad_own, ys = together(grad_own, ys)
    grad_sums = scatter_cores(grad_own, grad_other)
    mix_sums = scatter_cores(combine(0, ranks, ys), combine(1, ranks, ys))
    grad_sums = pass_on(grad_sums, scatter_far(grad_sums[2], part))
    grads, mix_sums = together(scatter_near(grad_sums), mix_sums)
    mix_passed = scatter_far(mix_sums[2], part)
    dx1, grad_o, d_logit, d_gain_two = own_tokens(
        grads, x1, gates, g_own, router_t, gain_two, w_out
    )
    grad_o = lax.all_to_all(grad_o, "ctx", split_axis=0, concat_axis=0, tiled=True)
    grad_o = grad_o.reshape(units, MICRO, part, PAIR)
    dx1_late, d_logit, mix_passed = together(dx1, d_logit, mix_passed)
    dwo_own, dwo_other, d_router = own_weights(order, dx1_late, heads, d_logit, h2)
    dwo_sums = scatter_cores(dwo_own, dwo_other)
    mix_sums = pass_on(mix_sums, mix_passed)
    grad_o, dwo_sums, mix_sums = together(grad_o, dwo_sums, mix_sums)
    mixes = scatter_near(mix_sums)
    dwo_terms = scatter_chips(dwo_sums)
    dq, dkv = attend_back(find, q, kv, starts, lse, o, grad_o, tables)
    dq, dkv, mixes, dwo_terms = together(dq, dkv, mixes, dwo_terms)
    dw_qkv = jnp.zeros((2 * PAIR, width), F32)
    d_gain_one = jnp.zeros((1, width), F32)
    dw_qkv, dh_other, d_gain_one = project_back(
        1, order, x_blocks, rows, gain_one, dq, dkv, w_qkv, dw_qkv, d_gain_one
    )
    dw_qkv, dh_own, d_gain_one = project_back(
        0, order, x_blocks, rows, gain_one, dq, dkv, w_qkv, dw_qkv, d_gain_one
    )
    dh_sums = scatter_cores(dh_own, dh_other)
    dh_sums, d_gain_one = together(dh_sums, d_gain_one)
    dh_terms = scatter_near(pass_on(dh_sums, scatter_far(dh_sums[2], part)))
    pack = pack_dense(order, local, dw_qkv, dwo_terms, d_router, d_gain_one, d_gain_two)
    pack = pack.reshape(shards, shard, -1)
    pack = lax.all_to_all(pack, "fsdp", split_axis=0, concat_axis=0, tiled=True)
    d_gate, d_up, d_down = open_experts(dw, local)
    mixed = (x1 + sum(term.astype(F32) for term in mixes)).astype(BF)
    pack, mixed, d_gate, d_up, d_down = together(pack, mixed, d_gate, d_up, d_down)
    pack = lax.all_gather(add_up(pack), "ctx", axis=0, tiled=False)
    pack, dh_terms = together(pack, dh_terms)
    d_tokens = finish(x_own, dx1, gain_one, dh_terms)
    d_q, d_k, d_v, d_out, d_router, d_gain_one, d_gain_two = unpack_dense(pack, experts)
    return (
        mixed.reshape(1, MICRO, part, width),
        d_tokens.reshape(1, MICRO, part, width),
        d_gain_one.reshape(shard),
        d_q,
        d_k,
        d_v,
        d_out,
        d_gain_two.reshape(shard),
        d_router.T,
        d_gate,
        d_up,
        d_down,
    )


def solution(mesh):
    return jax.shard_map(
        per_device,
        mesh=mesh,
        in_specs=(
            P("fsdp", None, "ctx", None),
            P("fsdp", None, "ctx", None),
            P("fsdp", None, "ctx"),
            P("fsdp"),
            P("fsdp", None),
            P("fsdp", None),
            P("fsdp", None),
            P("fsdp", None),
            P("fsdp"),
            P("fsdp", None),
            P("ctx", "fsdp", None),
            P("ctx", "fsdp", None),
            P("ctx", "fsdp", None),
            P("fsdp", None, "ctx", None),
        ),
        out_specs=(
            P("fsdp", None, "ctx", None),
            P("fsdp", None, "ctx", None),
            P("fsdp"),
            P("fsdp", None),
            P("fsdp", None),
            P("fsdp", None),
            P("fsdp", None),
            P("fsdp"),
            P("fsdp", None),
            P("ctx", "fsdp", None),
            P("ctx", "fsdp", None),
            P("ctx", "fsdp", None),
        ),
        check_vma=False,
    )
```
